128 devices in a mesh: row: 2 (over core), seq: 64 (over z, y, x).
Axes of the slice: x: 4, y: 4, z: 4, core: 2. Of those that a mesh axis runs over, the one named last changes fastest.
Arguments:
- tokens: bfloat16 [4, 4096, 2048], P('row', 'seq'), may hold values from -6 to 6
- lengths: int32 [4, 4], P('row'), may hold values from 0 to 4096, as said below
- norm_one: bfloat16 [2048], P(('row', 'seq')), may hold values from 0.5 to 1.5
- gelu_weight: bfloat16 [2048, 2816], P(('row', 'seq')), may hold values from -0.125 to 0.125
- input_weight: bfloat16 [2048, 2816], P(('row', 'seq')), may hold values from -0.125 to 0.125
- conv_weight: bfloat16 [2816, 4], P(('row', 'seq')), may hold values from -3 to 3
- conv_bias: bfloat16 [2816], P(('row', 'seq')), may hold values from -3 to 3
- gate_input: bfloat16 [2816, 176], P(('row', 'seq')), may hold values from -0.4375 to 0.4375
- bias_input: bfloat16 [2816], P(('row', 'seq')), may hold values from -4 to 4
- gate_recur: bfloat16 [2816, 176], P(('row', 'seq')), may hold values from -0.4375 to 0.4375
- bias_recur: bfloat16 [2816], P(('row', 'seq')), may hold values from -4 to 4
- decay_param: bfloat16 [2816], P(('row', 'seq')), may hold values from -12 to -3
- out_weight: bfloat16 [2816, 2048], P(('row', 'seq')), may hold values from -0.109375 to 0.109375
- norm_two: bfloat16 [2048], P(('row', 'seq')), may hold values from 0.5 to 1.5
- gate_weight: bfloat16 [2048, 6144], P(('row', 'seq')), may hold values from -0.125 to 0.125
- up_weight: bfloat16 [2048, 6144], P(('row', 'seq')), may hold values from -0.125 to 0.125
- down_weight: bfloat16 [6144, 2048], P(('row', 'seq')), may hold values from -0.078125 to 0.078125
- cotangent: bfloat16 [4, 4096, 2048], P('row', 'seq'), may hold values from -6 to 6
Outputs:
- output: bfloat16 [4, 4096, 2048], P('row', 'seq')
- grad_tokens: float32 [4, 4096, 2048], P('row', 'seq')
- grad_norm_one: float32 [2048], P(('row', 'seq'))
- grad_gelu_weight: float32 [2048, 2816], P(('row', 'seq'))
- grad_input_weight: float32 [2048, 2816], P(('row', 'seq'))
- grad_conv_weight: float32 [2816, 4], P(('row', 'seq'))
- grad_conv_bias: float32 [2816], P(('row', 'seq'))
- grad_gate_input: float32 [2816, 176], P(('row', 'seq'))
- grad_bias_input: float32 [2816], P(('row', 'seq'))
- grad_gate_recur: float32 [2816, 176], P(('row', 'seq'))
- grad_bias_recur: float32 [2816], P(('row', 'seq'))
- grad_decay_param: float32 [2816], P(('row', 'seq'))
- grad_out_weight: float32 [2816, 2048], P(('row', 'seq'))
- grad_norm_two: float32 [2048], P(('row', 'seq'))
- grad_gate_weight: float32 [2048, 6144], P(('row', 'seq'))
- grad_up_weight: float32 [2048, 6144], P(('row', 'seq'))
- grad_down_weight: float32 [6144, 2048], P(('row', 'seq'))
The draws below stay inside these ranges and needn't reach their ends.
Inputs may be any that keep to these rules, and one draw needn't show every extreme that they name: Each row lists its sequences' lengths in order, each of 1024 tokens or more, then zeros; they sum to at most 4096, the remaining slots of the row being padding. Among the 2 rows of each index of row, one holds a single sequence of 4096 tokens.
All inputs are finite; a program needn't handle non-finite values.
Results may differ from the reference program's by a relative error of at most 0.012.
The reference program's roundings to bfloat16 on the way count: a program that leaves them out, or rounds other values in their place, can miss the bound.
Values may be sent and summed in bfloat16 or wider, within the bound.
No kernel may reach another device: no remote copies, remote signals or barrier semaphores. Data moves between devices by JAX's collectives and lax.ppermute only.
A program may use at most 512 MiB of HBM per device.

```python
import jax
import jax.numpy as jnp
from jax import lax

D = 2048
R = 2816
FF = 6144
H = 16
HS = 176
CONV = 4
MINLEN = 1024
ROWS_DEV = 2
SLOTS = 4096
ROWS = 4
MAXSEG = 4


def draw_lengths(key, part):
    key = jax.random.fold_in(key, 5)
    pick_key, size_key = jax.random.split(key)
    groups = ROWS // ROWS_DEV
    chosen = jax.random.randint(pick_key, (groups,), 0, ROWS_DEV)
    row_number = jnp.arange(ROWS, dtype=jnp.int32)
    spanning = row_number % ROWS_DEV == chosen[row_number // ROWS_DEV]
    levels = jax.random.randint(size_key, (ROWS, MAXSEG), 0, 32)
    raw_len = MINLEN + (SLOTS - MINLEN) * (levels * levels) // 1024
    ends_at = jnp.cumsum(raw_len, axis=1)
    packed = jnp.where(ends_at <= SLOTS, raw_len, 0)
    columns = jnp.arange(MAXSEG, dtype=jnp.int32)
    full_row = jnp.where(columns == 0, SLOTS, 0)
    return jnp.where(spanning[:, None], full_row[None, :], packed).astype(jnp.int32)


def draw_decay_param(key, part):
    key = jax.random.fold_in(key, 9)
    shares = jax.random.uniform(key, (R,), jnp.float32)
    low_rate = 0.5 / SLOTS
    high_rate = 0.08
    rates = jnp.exp(jnp.log(low_rate) + shares * (jnp.log(high_rate) - jnp.log(low_rate)))
    return jnp.log(jnp.expm1(0.25 * rates)).astype(jnp.bfloat16)


def block_levels(key, shape, pieces, smallest, high):
    factor_of = 1.0
    for axis_at, blocks in pieces:
        heights = jax.random.uniform(jax.random.fold_in(jax.random.fold_in(key, 6), axis_at), (blocks,), jnp.float32, smallest / len(pieces), high / len(pieces))
        factor_of = factor_of * jnp.repeat(jnp.exp(heights), shape[axis_at] // blocks).reshape((-1,) + (1,) * (len(shape) - 1 - axis_at))
    return factor_of


def noise(own_key, extent, width, limit, pieces=(), held_as=jnp.bfloat16):
    factor_of = block_levels(own_key, extent, pieces, -0.22, 0.18) if pieces else 1.0
    entries = jax.random.normal(own_key, extent, jnp.float32) * width * factor_of
    return jnp.minimum(jnp.maximum(entries, -limit), limit).astype(held_as)


def setup_inputs(seed: int = 0) -> dict:
    seeds = jax.random.split(jax.random.key(seed), 19)
    return {
        "tokens": noise(seeds[0], (ROWS, SLOTS, D), 1.0, 6.0, ((0, 2), (1, 64))),
        "lengths": draw_lengths(jax.random.fold_in(seeds[18], 71), 0),
        "norm_one": jnp.clip(1.0 + 0.1 * jax.random.normal(seeds[2], (D,), jnp.float32), 0.5, 1.5).astype(jnp.bfloat16),
        "gelu_weight": noise(seeds[3], (D, R), D ** -0.5, 0.125, ((0, 128),)),
        "input_weight": noise(seeds[4], (D, R), D ** -0.5, 0.125, ((0, 128),)),
        "conv_weight": noise(seeds[5], (R, CONV), CONV ** -0.5, 3.0, ((0, 128),)),
        "conv_bias": noise(seeds[6], (R,), 0.5, 3.0, ((0, 128),)),
        "gate_input": noise(seeds[7], (R, HS), HS ** -0.5, 0.4375, ((0, 128),)),
        "bias_input": noise(seeds[8], (R,), 1.0, 4.0, ((0, 128),)),
        "gate_recur": noise(seeds[9], (R, HS), HS ** -0.5, 0.4375, ((0, 128),)),
        "bias_recur": noise(seeds[10], (R,), 1.0, 4.0, ((0, 128),)),
        "decay_param": draw_decay_param(jax.random.fold_in(seeds[18], 71), 0),
        "out_weight": noise(seeds[12], (R, D), R ** -0.5, 0.109375, ((0, 128),)),
        "norm_two": jnp.clip(1.0 + 0.1 * jax.random.normal(seeds[13], (D,), jnp.float32), 0.5, 1.5).astype(jnp.bfloat16),
        "gate_weight": noise(seeds[14], (D, FF), D ** -0.5, 0.125, ((0, 128),)),
        "up_weight": noise(seeds[15], (D, FF), D ** -0.5, 0.125, ((0, 128),)),
        "down_weight": noise(seeds[16], (FF, D), FF ** -0.5, 0.078125, ((0, 128),)),
        "cotangent": noise(seeds[17], (ROWS, SLOTS, D), 1.0, 6.0, ((0, 2), (1, 64))),
    }


@jax.custom_vjp
def low(v):
    return lax.optimization_barrier(v.astype(jnp.bfloat16)).astype(jnp.float32)

@jax.custom_vjp
def low_back(v):
    return v

def low_keep(v):
    return (low(v), None)

def low_pass(kept, grad):
    return (grad,)

def back_keep(v):
    return (v, None)

def back_low(kept, grad):
    return (low(grad),)
low.defvjp(low_keep, low_pass)
low_back.defvjp(back_keep, back_low)
epsilon = 1e-06
beta_floor = 0.001

def exact_dot(left, right):
    return jnp.dot(left, right, precision=lax.Precision.HIGHEST)

def chain_combine(earlier, later):
    return (earlier[0] * later[0], later[0] * earlier[1] + later[1])

def rms_scale(values, gain):
    return values * lax.rsqrt(lax.optimization_barrier(jnp.mean(values * values, axis=-1, keepdims=True)) + epsilon) * gain

def gated_inputs(reset_flag, raw_input, raw_recur, values, bias_input, bias_recur, decay_param):
    gate_in = jax.nn.sigmoid(raw_input + bias_input)
    gate_rec = jax.nn.sigmoid(raw_recur + bias_recur)
    log_decay = -8.0 * gate_rec * jax.nn.softplus(decay_param)
    factor = jnp.exp(log_decay) * (1.0 - reset_flag)
    root = jnp.sqrt(jnp.maximum(-jnp.expm1(2.0 * log_decay), beta_floor))
    return (factor, root * gate_in * values)

def segment_tables(lengths):
    slot_index = jnp.arange(SLOTS, dtype=jnp.int32)
    seg_starts = (jnp.cumsum(lengths, axis=1) - lengths).astype(jnp.int32)
    seg_live = lengths > 0
    before = seg_live[:, None, :] & (seg_starts[:, None, :] <= slot_index[None, :, None])
    begins = seg_live[:, None, :] & (seg_starts[:, None, :] == slot_index[None, :, None])
    segment = lax.optimization_barrier(jnp.sum(before.astype(jnp.int32), axis=2)).astype(jnp.int32)
    reset_flag = lax.optimization_barrier(jnp.sum(begins.astype(jnp.int32), axis=2)).astype(jnp.float32)
    row_total = lax.optimization_barrier(jnp.sum(lengths, axis=1)).astype(jnp.int32)
    valid_mask = (slot_index[None, :] < row_total[:, None]).astype(jnp.float32)
    return (segment, reset_flag, valid_mask)

def row_forward(row_tokens, segment, reset_flag, valid_mask, params):
    norm_one, gelu_weight, input_weight, conv_weight, conv_bias, gate_input, bias_input, gate_recur, bias_recur, decay_param, out_weight, norm_two, gate_weight, up_weight, down_weight = params
    normed = low(rms_scale(row_tokens, norm_one))
    gelu_pre = low_back(exact_dot(normed, gelu_weight))
    conv_in = low(low_back(exact_dot(normed, input_weight)))
    conv_out = conv_bias + conv_weight[:, 0] * conv_in
    for offset in range(1, CONV):
        shifted = jnp.concatenate([jnp.zeros((offset, R), jnp.float32), conv_in[:SLOTS - offset]], axis=0)
        earlier_seg = jnp.concatenate([jnp.full((offset,), -1, jnp.int32), segment[:SLOTS - offset]])
        same_seg = (earlier_seg == segment).astype(jnp.float32)
        conv_out = conv_out + conv_weight[:, offset] * shifted * same_seg[:, None]
    conv_vals = low(low_back(conv_out))
    blocks = conv_vals.reshape(SLOTS, H, HS)
    raw_input = low_back(jnp.einsum('thk,hkj->thj', blocks, gate_input.reshape(H, HS, HS), precision=lax.Precision.HIGHEST).reshape(SLOTS, R))
    raw_recur = low_back(jnp.einsum('thk,hkj->thj', blocks, gate_recur.reshape(H, HS, HS), precision=lax.Precision.HIGHEST).reshape(SLOTS, R))
    factor, drive_in = gated_inputs(reset_flag[:, None], raw_input, raw_recur, conv_vals, bias_input, bias_recur, decay_param)
    cumulative, rec_state = lax.associative_scan(chain_combine, (factor, drive_in), axis=0)
    mixed = low(jax.nn.gelu(gelu_pre) * rec_state)
    middle = row_tokens + low_back(exact_dot(mixed, out_weight))
    normed_two = low(rms_scale(middle, norm_two))
    gate_pre = low_back(exact_dot(normed_two, gate_weight))
    up_pre = low_back(exact_dot(normed_two, up_weight))
    inner_act = low(jax.nn.gelu(gate_pre) * up_pre)
    return (middle + low_back(exact_dot(inner_act, down_weight))) * valid_mask[:, None]

def reference(tokens, lengths, norm_one, gelu_weight, input_weight, conv_weight, conv_bias, gate_input, bias_input, gate_recur, bias_recur, decay_param, out_weight, norm_two, gate_weight, up_weight, down_weight, cotangent):
    segment, reset_flag, valid_mask = segment_tables(lengths)
    weights = tuple((element.astype(jnp.float32) for element in (norm_one, gelu_weight, input_weight, conv_weight, conv_bias, gate_input, bias_input, gate_recur, bias_recur, decay_param, out_weight, norm_two, gate_weight, up_weight, down_weight)))

    def forward_all(rows_in, params):

        def one_row(element):
            return row_forward(element[0], element[1], element[2], element[3], params)
        return lax.map(jax.checkpoint(one_row), (rows_in, segment, reset_flag, valid_mask))
    result, pull_back = jax.vjp(forward_all, tokens.astype(jnp.float32), weights)
    grad_tokens, grad_list = pull_back(cotangent.astype(jnp.float32))
    return (result.astype(jnp.bfloat16), grad_tokens, grad_list[0], grad_list[1], grad_list[2], grad_list[3], grad_list[4], grad_list[5], grad_list[6], grad_list[7], grad_list[8], grad_list[9], grad_list[10], grad_list[11], grad_list[12], grad_list[13], grad_list[14])
```

```python
from functools import partial

import jax
import jax.numpy as jnp
from jax import lax
from jax.experimental import pallas as pl
from jax.experimental.pallas import tpu as pltpu
from jax.sharding import Mesh
from jax.sharding import PartitionSpec as P

epsilon = 1e-06
beta_floor = 0.001
bf16 = jnp.bfloat16
f32 = jnp.float32
everywhere = ("row", "z", "y", "x")
team = ("row", "z")
plane = ("y", "x")
vmem_limit = 56 * 1024 * 1024


def hop(block, axis, distance):
    count = lax.axis_size(axis)
    return lax.ppermute(block, axis, [(i, (i + distance) % count) for i in range(count)])


def place(buffer, piece, at, dim):
    return lax.dynamic_update_slice_in_dim(buffer, jnp.expand_dims(piece, dim), at, dim)


def gather_axis(piece, axis, dim):
    mine = lax.axis_index(axis)
    shape = piece.shape[:dim] + (4,) + piece.shape[dim:]
    above, below, across = hop(piece, axis, -1), hop(piece, axis, 1), hop(piece, axis, 2)
    whole = place(jnp.zeros(shape, piece.dtype), piece, mine, dim)
    whole = place(whole, above, (mine + 1) % 4, dim)
    whole = place(whole, below, (mine + 3) % 4, dim)
    return place(whole, across, (mine + 2) % 4, dim)


def reduce_axis(whole, axis, dim):
    mine = lax.axis_index(axis)

    def piece(offset):
        return lax.dynamic_index_in_dim(whole, (mine + offset) % 4, dim, keepdims=False)

    total = piece(0).astype(f32)
    for offset in (2, 1, 3):
        total = total + hop(piece(offset).astype(bf16), axis, offset).astype(f32)
    return total


def gather_team(block):
    half = block.shape[0] // 2
    below, above = hop(block, "z", 1), hop(block, "z", -1)
    across = jnp.concatenate([hop(below[:half], "z", 1), hop(above[half:], "z", -1)], axis=0)
    parts = []
    for part in (block, above, across, below):
        parts += [part, hop(part, "row", 1)]
    return parts


def reduce_team(partial_sum):
    blocks = partial_sum.reshape(4, 2, -1, partial_sum.shape[-1])
    sums = [None] * 4
    for offset in (2, 1, 3, 0):
        sums[offset] = blocks[offset, 0].astype(f32) + hop(blocks[offset, 1].astype(bf16), "row", 1).astype(f32)
    half = sums[0].shape[0] // 2
    from_below = hop(sums[2][:half].astype(bf16), "z", 1)
    from_above = hop(sums[2][half:].astype(bf16), "z", -1)
    up = jnp.concatenate([sums[1][:half] + from_below.astype(f32), sums[1][half:]], axis=0)
    down = jnp.concatenate([sums[3][:half], sums[3][half:] + from_above.astype(f32)], axis=0)
    return (
        sums[0]
        + hop(up.astype(bf16), "z", 1).astype(f32)
        + hop(down.astype(bf16), "z", -1).astype(f32)
    )


def project_in(left, weight):
    return jnp.dot(left, weight, preferred_element_type=f32)


def project_back(grad, weight):
    return lax.dot_general(grad, weight, (((1,), (1,)), ((), ())), preferred_element_type=f32)


def outer_sum(left, grad):
    return lax.dot_general(left, grad, (((0,), (0,)), ((), ())), preferred_element_type=f32)


def kernel_call(kernel, outs, scratch=()):
    return pl.pallas_call(
        kernel,
        out_shape=[jax.ShapeDtypeStruct(shape, dtype) for shape, dtype in outs],
        scratch_shapes=list(scratch),
        compiler_params=pltpu.CompilerParams(vmem_limit_bytes=vmem_limit),
    )


def chunk_rows(chunk, size):
    return pl.ds(pl.multiple_of(chunk * size, size), size)


def panels(ref, rows):
    return jnp.concatenate([ref[at, rows, :] for at in range(ref.shape[0])], axis=1)


def set_panels(ref, rows, value):
    for at in range(ref.shape[0]):
        ref[at, rows, :] = value[:, at * 128 : (at + 1) * 128]


def gates_kernel(
    cin, halo, masks, params, w_in, w_rec,
    conv, factor, g_in, g_rec, kept_out, state, decay, ends, ext, raw_in, raw_rec, drive,
):
    tokens, width = cin.shape
    count = halo.shape[0]
    size = tokens // count
    tiles = width // 128

    def convolve(chunk, carry):
        rows = chunk_rows(chunk, size)
        ext[0:8, :] = halo[chunk].astype(f32)
        ext[8 : 8 + size, :] = cin[rows, :].astype(f32)
        total = params[4:5, :] + params[0:1, :] * ext[8 : 8 + size, :]
        for k in (1, 2, 3):
            total = total + params[k : k + 1, :] * ext[8 - k : 8 - k + size, :] * masks[rows, k : k + 1]
        conv[rows, :] = total.astype(bf16)
        return carry

    lax.fori_loop(0, count, convolve, 0)
    raw_in[...] = jnp.dot(conv[...], w_in[...], preferred_element_type=f32)
    raw_rec[...] = jnp.dot(conv[...], w_rec[...], preferred_element_type=f32)

    def gate(chunk, carry):
        rows = chunk_rows(chunk, size)
        gate_in = jax.nn.sigmoid(raw_in[rows, :] + params[5:6, :])
        gate_rec = jax.nn.sigmoid(raw_rec[rows, :] + params[6:7, :])
        log_decay = gate_rec * params[7:8, :]
        base = jnp.exp(log_decay)
        kept = -jnp.tanh(log_decay) * (base * base + 1.0)
        scale = jnp.sqrt(jnp.maximum(kept, beta_floor))
        set_panels(factor, rows, base * masks[rows, 0:1])
        g_in[rows, :] = gate_in
        g_rec[rows, :] = gate_rec
        kept_out[rows, :] = kept
        set_panels(drive, rows, scale * gate_in * conv[rows, :].astype(f32))
        return carry

    lax.fori_loop(0, count, gate, 0)

    def scan(slot, carry):
        at = pl.ds(slot, count, stride=size)
        after = []
        for tile, (held, gone) in enumerate(carry):
            step = factor[tile, at, :]
            held = step * held + drive[tile, at, :]
            gone = step * gone
            state[tile, at, :] = held
            decay[tile, at, :] = gone
            after.append((held, gone))
        return tuple(after)

    first = pl.ds(0, count, stride=size)
    start = []
    for tile in range(tiles):
        zero = drive[tile, first, :] * 0.0
        start.append((zero, zero + 1.0))
    last = lax.fori_loop(0, size, scan, tuple(start))
    for tile, (held, gone) in enumerate(last):
        ends[0, :, tile * 128 : (tile + 1) * 128] = gone
        ends[1, :, tile * 128 : (tile + 1) * 128] = held


def carry_kernel(backward, spot, pieces, entering):
    z_at, mine = spot[0], spot[1]
    places = pieces.shape[0]
    order = range(places - 1, -1, -1) if backward else range(places)
    decay, state = pieces[order[0], 0], pieces[order[0], 1]
    here = jnp.where(mine == order[0], 1.0, 0.0)
    own_decay, own_state = jnp.zeros_like(decay) + here, jnp.zeros_like(state)
    for place_at in order[1:]:
        here = jnp.where(mine == place_at, 1.0, 0.0)
        own_decay = own_decay + decay * here
        own_state = own_state + state * here
        step = pieces[place_at, 0]
        state = step * state + pieces[place_at, 1]
        decay = step * decay
    held = jnp.zeros((4, decay.shape[1]), f32)
    for step in range(4):
        z = 3 - step if backward else step
        offset = lax.rem(z - z_at + 4, 4)
        own = jnp.zeros_like(held)
        following = jnp.zeros_like(held)
        for candidate in range(4):
            pick = jnp.where(offset == candidate, 1.0, 0.0)
            part = slice(candidate * 4, candidate * 4 + 4)
            own = own + pick * (own_decay[part] * held + own_state[part])
            following = following + pick * (decay[part] * held + state[part])
        for row in range(4):
            entering[offset * 4 + row] = own[row : row + 1]
        held = following


def gelu_parts(value):
    slope = 0.7978845608028654
    square = value * value
    inner = jnp.tanh(slope * (value + 0.044715 * value * square))
    half = 0.5 * (1.0 + inner)
    act = value * half
    grad = half + 0.5 * value * (1.0 - inner * inner) * slope * (1.0 + 3 * 0.044715 * square)
    return act, grad


def mix_kernel(pre, state, decay, entering, out_rows, rec_state, mixed, partial_sum):
    count = entering.shape[0]
    tokens, width = rec_state.shape
    size = tokens // count

    def mix(chunk, carry):
        rows = chunk_rows(chunk, size)
        full = panels(state, rows) + panels(decay, rows) * entering[chunk]
        rec_state[rows, :] = full
        mixed[rows, :] = (gelu_parts(pre[rows, :])[0] * full).astype(bf16)
        return carry

    lax.fori_loop(0, count, mix, 0)

    def project(block, carry):
        rows = chunk_rows(block, 128)
        partial_sum[rows, :] = jnp.dot(
            mixed[rows, :], out_rows[...], preferred_element_type=f32
        ).astype(bf16)
        return carry

    lax.fori_loop(0, tokens // 128, project, 0)


def unmix_kernel(
    grad_mixed, pre, rec_state, factor, grad_gelu, adjoint, reach, ends, grad_state
):
    tokens, width = rec_state.shape
    count = ends.shape[1]
    size = tokens // count
    tiles = width // 128

    def unmix(chunk, carry):
        rows = chunk_rows(chunk, size)
        act, slope = gelu_parts(pre[rows, :])
        grad = grad_mixed[rows, :]
        grad_gelu[rows, :] = (grad * rec_state[rows, :] * slope).astype(bf16)
        set_panels(grad_state, rows, grad * act)
        return carry

    lax.fori_loop(0, count, unmix, 0)

    def scan(step, carry):
        at = pl.ds(size - 1 - step, count, stride=size)
        after = []
        for tile, (held, gone, ahead) in enumerate(carry):
            held = ahead * held + grad_state[tile, at, :]
            gone = ahead * gone
            adjoint[tile, at, :] = held
            reach[tile, at, :] = gone
            after.append((held, gone, factor[tile, at, :]))
        return tuple(after)

    first = pl.ds(0, count, stride=size)
    start = []
    for tile in range(tiles):
        zero = factor[tile, first, :] * 0.0
        start.append((zero, zero + 1.0, zero + 1.0))
    last = lax.fori_loop(0, size, scan, tuple(start))
    for tile, (held, gone, ahead) in enumerate(last):
        ends[0, :, tile * 128 : (tile + 1) * 128] = ahead * gone
        ends[1, :, tile * 128 : (tile + 1) * 128] = ahead * held


def ungate_kernel(
    adjoint, reach, arriving, rec_state, entering, factor, g_in, g_rec, kept, conv, cin, halo, masks,
    params, w_in, w_rec, grad_in, grad_rec, grad_conv, sums, ext, direct,
):
    tokens, width = cin.shape
    count = halo.shape[0]
    size = tokens // count
    zero = params[0:8, :] * 0.0

    def fold(value):
        total = value[0:8]
        for at in range(8, size, 8):
            total = total + value[at : at + 8]
        return total

    def ungate(chunk, carry):
        sum_in, sum_rec, sum_decay = carry
        rows = chunk_rows(chunk, size)
        ext[7:8, :] = entering[chunk]
        ext[8 : 8 + size, :] = rec_state[rows, :]
        full = panels(adjoint, rows) + panels(reach, rows) * arriving[chunk]
        square = kept[rows, :]
        scale = jnp.sqrt(jnp.maximum(square, beta_floor))
        gate_in = g_in[rows, :]
        gate_rec = g_rec[rows, :]
        values = conv[rows, :].astype(f32)
        scaled = full * scale
        drive = full * gate_in * values
        slope = jnp.where(square > beta_floor, (1.0 - square) / scale, 0.0)
        grad_log = full * panels(factor, rows) * ext[7 : 7 + size, :] - slope * drive
        raw_in = scale * drive * (1.0 - gate_in)
        pulled = grad_log * gate_rec
        raw_rec = pulled * params[7:8, :] * (1.0 - gate_rec)
        grad_in[rows, :] = raw_in.astype(bf16)
        grad_rec[rows, :] = raw_rec.astype(bf16)
        direct[rows, :] = scaled * gate_in
        return (sum_in + fold(raw_in), sum_rec + fold(raw_rec), sum_decay + fold(pulled))

    sum_in, sum_rec, sum_decay = lax.fori_loop(0, count, ungate, (zero, zero, zero))
    back = (((1,), (1,)), ((), ()))
    direct[...] += lax.dot_general(grad_in[...], w_in[...], back, preferred_element_type=f32)
    direct[...] += lax.dot_general(grad_rec[...], w_rec[...], back, preferred_element_type=f32)

    def taps(chunk, carry):
        sum_bias, sum_taps = carry
        rows = chunk_rows(chunk, size)
        grad = direct[rows, :].astype(bf16)
        grad_conv[rows, :] = grad
        grad = grad.astype(f32)
        ext[0:8, :] = halo[chunk].astype(f32)
        ext[8 : 8 + size, :] = cin[rows, :].astype(f32)
        new_taps = [sum_taps[0] + fold(grad * ext[8 : 8 + size, :])]
        for k in (1, 2, 3):
            moved = ext[8 - k : 8 - k + size, :] * masks[rows, k : k + 1]
            new_taps.append(sum_taps[k] + fold(grad * moved))
        return (sum_bias + fold(grad), tuple(new_taps))

    sum_bias, sum_taps = lax.fori_loop(0, count, taps, (zero, (zero,) * 4))
    rows_out = sum_taps + (sum_bias, sum_in, sum_rec, sum_decay * params[8:9, :])
    for index, total in enumerate(rows_out):
        sums[index : index + 1, :] = jnp.sum(total, axis=0, keepdims=True)


def unconvolve_kernel(grad_conv, halo, masks, params, out, ext):
    tokens, width = grad_conv.shape
    count = halo.shape[0]
    size = tokens // count

    def spread(chunk, carry):
        rows = chunk_rows(chunk, size)
        ext[0:size, :] = grad_conv[rows, :].astype(f32)
        ext[size : size + 8, :] = halo[chunk].astype(f32)
        total = params[0:1, :] * ext[0:size, :]
        for k in (1, 2, 3):
            total = total + params[k : k + 1, :] * ext[k : k + size, :] * masks[rows, 3 + k : 4 + k]
        out[rows, :] = total.astype(bf16)
        return carry

    lax.fori_loop(0, count, spread, 0)


def body(
    tokens,
    lengths,
    norm_one,
    gelu_weight,
    input_weight,
    conv_weight,
    conv_bias,
    gate_input,
    bias_input,
    gate_recur,
    bias_recur,
    decay_param,
    out_weight,
    norm_two,
    gate_weight,
    up_weight,
    down_weight,
    cotangent,
):
    row_count, size, model = tokens.shape
    local = row_count * size
    block, hidden = gelu_weight.shape
    inner = gate_weight.shape[1]
    head = gate_input.shape[1]
    channels, units = hidden // 8, inner // 8
    strip = gate_input.shape[0]
    width = -(-channels // 128) * 128
    spare = width - channels
    z_at, y_at, x_at = (lax.axis_index(name) for name in ("z", "y", "x"))
    plane_at = y_at * 4 + x_at
    chunks = 16
    total_tokens = chunks * size
    flat = tokens.reshape(local, model)

    token_parts = gather_team(flat)
    team_tokens = jnp.concatenate(token_parts, axis=0)

    gains = jnp.stack([norm_one, norm_two], axis=1)
    gains = jnp.broadcast_to(
        jnp.pad(gains, ((0, 0), (0, spare - 2)))[:, None, :], (block, 8, spare)
    )
    first = jnp.concatenate(
        [
            gelu_weight.reshape(block, 8, channels),
            gains,
            input_weight.reshape(block, 8, channels),
            jnp.zeros_like(gains),
        ],
        axis=2,
    ).transpose(1, 0, 2)
    first = lax.all_to_all(first, team, 0, 0, tiled=True)
    first_width = first.shape[2]
    first = gather_axis(first, "x", 1)
    first = gather_axis(first.reshape(8, 4 * block, first_width), "y", 1)
    first = first.reshape(model, first_width)
    small = jnp.stack([conv_bias, bias_input, bias_recur, decay_param], axis=1)
    second = jnp.concatenate([out_weight, gate_input, gate_recur, conv_weight, small], axis=1)
    second = gather_axis(gather_axis(second, "y", 0), "x", 1).reshape(channels, -1)
    second = jnp.pad(second, ((0, spare), (0, 0)))
    third = jnp.concatenate(
        [gate_weight.reshape(block, 8, units), up_weight.reshape(block, 8, units)], axis=2
    ).transpose(1, 0, 2)
    third = lax.all_to_all(third, team, 0, 0, tiled=True)
    third = lax.all_gather(third, plane, axis=0, tiled=False)
    third = third.reshape(16, 8, block, 2 * units).transpose(1, 0, 2, 3).reshape(model, 2 * units)
    down = lax.all_gather(down_weight, plane, axis=0, tiled=True)

    gain_one = first[:, channels].astype(f32)[None, :]
    gain_two = first[:, channels + 1].astype(f32)[None, :]
    out_rows = second[:, :model]
    own_head = (jnp.arange(width)[:, None] // head) == (jnp.arange(width)[None, :] // head)

    def spread_heads(part):
        return jnp.where(own_head, jnp.concatenate([part, part, part], axis=1)[:, :width], 0)

    w_in = spread_heads(second[:, model : model + head])
    w_rec = spread_heads(second[:, model + head : model + 2 * head])
    rows_small = second[:, model + 2 * head :].astype(f32).T
    decay_row = rows_small[7:8]
    params = jnp.concatenate(
        [
            rows_small[:7],
            -8.0 * jax.nn.softplus(decay_row),
            -8.0 * jax.nn.sigmoid(decay_row),
            jnp.zeros((7, width), f32),
        ],
        axis=0,
    )

    lens = jnp.stack([lengths, hop(lengths, "row", 1)], axis=0)
    starts = jnp.cumsum(lens, axis=2) - lens
    chunk_z = (z_at + jnp.arange(4)) % 4
    first_slot = chunk_z * (16 * size) + plane_at * size

    def position(slot):
        live = (lens > 0)[None, :, :, None, :] & (starts[None, :, :, None, :] <= slot[..., None])
        origin = jnp.max(jnp.where(live, starts[None, :, :, None, :], 0), axis=-1)
        return slot - origin

    slots = first_slot[:, None, None, None] + jnp.arange(size)[None, None, None, :]
    slots = jnp.broadcast_to(slots, (4, 2, row_count, size))
    here = position(slots)
    columns = [here != 0] + [here >= k for k in (1, 2, 3)]
    for k in (1, 2, 3):
        ahead = slots + k
        columns.append((position(ahead) >= k) & (ahead < 64 * size))
    columns.append(jnp.zeros_like(columns[0]))
    masks = jnp.stack(columns, axis=-1).astype(f32).reshape(total_tokens, 8)
    row_total = jnp.sum(lengths, axis=1)
    own_slots = (z_at * 16 + plane_at) * size + jnp.arange(size)
    valid = (own_slots[None, :] < row_total[:, None]).astype(f32).reshape(local, 1)

    token_float = team_tokens.astype(f32)
    scale_one = lax.rsqrt(jnp.mean(token_float * token_float, axis=-1, keepdims=True) + epsilon)
    normed = (token_float * scale_one * gain_one).astype(bf16)
    conv_in = project_in(normed, first[:, width:]).astype(bf16)
    by_chunk = (chunks, size, width)
    halo = hop(conv_in.reshape(by_chunk)[:, size - 8 :], plane, 1)
    halo = jnp.where(plane_at == 0, jnp.roll(halo, 4, axis=0), halo)
    gelu_pre = project_in(normed, first[:, :width])
    wide = ((total_tokens, width), f32)
    narrow = ((total_tokens, width), bf16)
    paneled = ((width // 128, total_tokens, 128), f32)
    ends_shape = ((2, chunks, width), f32)
    extended = pltpu.VMEM((size + 8, width), f32)
    whole = pltpu.VMEM(*wide)
    folded = pltpu.VMEM(*paneled)
    conv_vals, factor, g_in, g_rec, kept, local_state, decay, ends = kernel_call(
        gates_kernel,
        [narrow, paneled, wide, wide, wide, paneled, paneled, ends_shape],
        [extended, whole, whole, folded],
    )(conv_in, halo, masks, params, w_in, w_rec)

    def carried(ends, backward):
        pieces = lax.all_to_all(jnp.broadcast_to(ends, (16,) + ends.shape), plane, 0, 0, tiled=True)
        spot = jnp.stack([z_at, plane_at]).astype(jnp.int32)
        return pl.pallas_call(
            partial(carry_kernel, backward),
            out_shape=jax.ShapeDtypeStruct((chunks, 1, width), f32),
            in_specs=[pl.BlockSpec(memory_space=pltpu.SMEM), pl.BlockSpec(memory_space=pltpu.VMEM)],
            out_specs=pl.BlockSpec(memory_space=pltpu.VMEM),
        )(spot, pieces)

    entering = carried(ends, False)
    rec_state, mixed, partial_middle = kernel_call(
        mix_kernel, [wide, narrow, ((total_tokens, model), bf16)]
    )(gelu_pre, local_state, decay, entering, out_rows)
    own_tokens = flat.astype(f32)
    middle = own_tokens + reduce_team(partial_middle)

    scale_two = lax.rsqrt(jnp.mean(middle * middle, axis=-1, keepdims=True) + epsilon)
    normed_two = (middle * scale_two * gain_two).astype(bf16)
    upstream = cotangent.reshape(local, model).astype(f32) * valid
    grad_down = jnp.concatenate(gather_team(upstream.astype(bf16)), axis=0)
    team_two = jnp.concatenate(gather_team(normed_two), axis=0)
    pre = project_in(team_two, third)
    gate_pre, up_pre = pre[:, :units], pre[:, units:]
    gate_act, gate_slope = gelu_parts(gate_pre)
    inner_act = (gate_act * up_pre).astype(bf16)
    grad_inner = project_back(grad_down, down)
    grad_pre = jnp.concatenate(
        [(grad_inner * up_pre * gate_slope).astype(bf16), (grad_inner * gate_act).astype(bf16)],
        axis=1,
    )
    grad_two = reduce_team(project_back(grad_pre, third))
    result = (middle + reduce_team(project_in(inner_act, down))) * valid
    output = result.reshape(row_count, size, model).astype(bf16)

    def to_owners(grad):
        width = grad.shape[1]
        grad = grad.astype(bf16).reshape(8, 16, block, width).transpose(1, 0, 2, 3)
        grad = grad.reshape(16 * 8 * block, width)
        grad = lax.psum_scatter(grad, plane, scatter_dimension=0, tiled=True)
        return grad.reshape(8, block, width)

    def back_to_rows(grad):
        return lax.all_to_all(grad, team, 0, 0, tiled=True).astype(f32).transpose(1, 0, 2)

    grad_third = to_owners(outer_sum(team_two, grad_pre))
    grad_down_weight = lax.psum_scatter(
        outer_sum(inner_act, grad_down).astype(bf16), plane, scatter_dimension=0, tiled=True
    ).astype(f32)
    grad_third = back_to_rows(grad_third)
    grad_gate_weight = grad_third[:, :, :units].reshape(block, inner)
    grad_up_weight = grad_third[:, :, units:].reshape(block, inner)

    def norm_back(values, scale, gain, grad):
        pulled = gain * grad
        mean = jnp.mean(pulled * values, axis=-1, keepdims=True)
        return scale * pulled - values * (scale * scale * scale * mean)

    def gain_grad(gain, pairs):
        total = sum(jnp.sum(weight.astype(f32) * grad, axis=1) for weight, grad in pairs)
        return total / gain.astype(f32)

    grad_norm_two = gain_grad(
        norm_two, [(gate_weight, grad_gate_weight), (up_weight, grad_up_weight)]
    )
    grad_middle = upstream + norm_back(middle, scale_two, gain_two, grad_two)
    grad_branch = jnp.concatenate(gather_team(grad_middle.astype(bf16)), axis=0)

    grad_mixed = project_back(grad_branch, out_rows)
    grad_gelu, adjoint, reach, ends = kernel_call(
        unmix_kernel, [narrow, paneled, paneled, ends_shape], [folded]
    )(grad_mixed, gelu_pre, rec_state, factor)
    arriving = carried(ends, True)
    grad_in, grad_rec, grad_conv, sums = kernel_call(
        ungate_kernel, [narrow, narrow, narrow, ((8, width), f32)], [extended, whole]
    )(
        adjoint, reach, arriving, rec_state, entering, factor, g_in, g_rec, kept, conv_vals, conv_in,
        halo, masks, params, w_in, w_rec,
    )
    ahead = hop(grad_conv.reshape(by_chunk)[:, :8], plane, -1)
    ahead = jnp.where(plane_at == 15, jnp.roll(ahead, -4, axis=0), ahead)
    (grad_conv_in,) = kernel_call(unconvolve_kernel, [narrow], [extended])(
        grad_conv, ahead, masks, params
    )

    def own_heads(grad):
        grad = jnp.where(own_head, grad, 0)[:channels]
        return grad[:, :head] + grad[:, head:channels]

    grad_second = jnp.concatenate(
        [
            outer_sum(mixed, grad_branch)[:channels],
            own_heads(outer_sum(conv_vals, grad_in)),
            own_heads(outer_sum(conv_vals, grad_rec)),
            sums.T[:channels],
        ],
        axis=1,
    )
    grad_second = grad_second.astype(bf16).reshape(4, 4, strip, -1)
    grad_second = reduce_axis(reduce_axis(grad_second, "x", 1), "y", 0)
    grad_out_weight = grad_second[:, :model]
    grad_gate_input = grad_second[:, model : model + head]
    grad_gate_recur = grad_second[:, model + head : model + 2 * head]
    grad_small = grad_second[:, model + 2 * head :]

    grad_pair = jnp.concatenate([grad_gelu, grad_conv_in], axis=1)
    grad_normed = reduce_team(project_back(grad_pair, first))
    grad_first = outer_sum(normed, grad_pair).astype(bf16).reshape(8, 4, 4 * block, 2 * width)
    grad_first = reduce_axis(grad_first, "y", 1).reshape(8, 4, block, 2 * width)
    grad_first = reduce_axis(grad_first, "x", 1)
    grad_first = back_to_rows(grad_first.astype(bf16))
    grad_gelu_weight = grad_first[:, :, :channels].reshape(block, hidden)
    grad_input_weight = grad_first[:, :, width : width + channels].reshape(block, hidden)
    grad_norm_one = gain_grad(
        norm_one, [(gelu_weight, grad_gelu_weight), (input_weight, grad_input_weight)]
    )
    own_scale = lax.rsqrt(jnp.mean(own_tokens * own_tokens, axis=-1, keepdims=True) + epsilon)
    grad_tokens = grad_middle + norm_back(own_tokens, own_scale, gain_one, grad_normed)
    return (
        output,
        grad_tokens.reshape(row_count, size, model),
        grad_norm_one,
        grad_gelu_weight,
        grad_input_weight,
        grad_small[:, :4],
        grad_small[:, 4],
        grad_gate_input,
        grad_small[:, 5],
        grad_gate_recur,
        grad_small[:, 6],
        grad_small[:, 7],
        grad_out_weight,
        grad_norm_two,
        grad_gate_weight,
        grad_up_weight,
        grad_down_weight,
    )


def solution(mesh):
    grid = Mesh(mesh.devices.reshape(2, 4, 4, 4), everywhere)
    slots = P("row", ("z", "y", "x"), None)
    line = P(everywhere)
    sheet = P(everywhere, None)
    return jax.shard_map(
        body,
        mesh=grid,
        in_specs=(
            slots, P("row", None), line, sheet, sheet, sheet, line, sheet, line, sheet, line, line,
            sheet, line, sheet, sheet, sheet, slots,
        ),
        out_specs=(
            slots, slots, line, sheet, sheet, sheet, line, sheet, line, sheet, line, line, sheet,
            line, sheet, sheet, sheet,
        ),
        check_vma=False,
    )
```

```python
from functools import partial

import jax
import jax.numpy as jnp
from jax import lax
from jax.experimental import pallas as pl
from jax.experimental.pallas import tpu as pltpu
from jax.sharding import Mesh
from jax.sharding import PartitionSpec as P

epsilon = 1e-06
beta_floor = 0.001
bf16 = jnp.bfloat16
f32 = jnp.float32
everywhere = ("row", "z", "y", "x")
team = ("row", "z")
plane = ("y", "x")
vmem_limit = 32 * 1024 * 1024


def hop(block, axis, distance):
    count = lax.axis_size(axis)
    return lax.ppermute(block, axis, [(i, (i + distance) % count) for i in range(count)])


def gather_plane(piece):
    return lax.all_to_all(jnp.broadcast_to(piece, (16,) + piece.shape), plane, 0, 0, tiled=True)


def total_of(pieces):
    return jnp.sum(pieces.astype(f32), axis=0)


def after(value, *others):
    return lax.optimization_barrier((value,) + others)[0]


def joined(*parts):
    return jnp.concatenate(parts, axis=0)


def gather_team(block):
    z_at = lax.axis_index("z")
    half = block.shape[0] // 2
    below, above = hop(block, "z", 1), hop(block, "z", -1)
    across = joined(hop(below[:half], "z", 1), hop(above[half:], "z", -1))
    own = jnp.zeros((4,) + block.shape, block.dtype)
    for offset, part in ((0, block), (1, above), (3, below), (2, across)):
        own = lax.dynamic_update_index_in_dim(own, part, (z_at + offset) % 4, 0)
    own = own.reshape(4 * block.shape[0], -1)
    return own, hop(own, "row", 1), (above, below)


def reduce_team(other, own):
    z_at = lax.axis_index("z")
    other = hop(other, "row", 1).reshape(4, -1, other.shape[-1])
    own = own.reshape(other.shape)

    def block(offset):
        at = (z_at + offset) % 4
        parts = [lax.dynamic_index_in_dim(whole, at, 0, keepdims=False) for whole in (own, other)]
        return parts[0].astype(f32) + parts[1].astype(f32)

    sums = {offset: block(offset) for offset in (2, 1, 3, 0)}
    half = own.shape[1] // 2
    from_below = hop(sums[2][:half].astype(bf16), "z", 1)
    from_above = hop(sums[2][half:].astype(bf16), "z", -1)
    up = joined(sums[1][:half] + from_below.astype(f32), sums[1][half:]).astype(bf16)
    down = joined(sums[3][:half], sums[3][half:] + from_above.astype(f32)).astype(bf16)
    total = sums[0] + hop(up, "z", 1).astype(f32) + hop(down, "z", -1).astype(f32)
    return total, up


def project_in(left, weight):
    return jnp.dot(left, weight, preferred_element_type=f32)


def project_back(grad, weight):
    return lax.dot_general(grad, weight, (((1,), (1,)), ((), ())), preferred_element_type=f32)


def outer_sum(left, grad):
    return lax.dot_general(left, grad, (((0,), (0,)), ((), ())), preferred_element_type=f32)


def fold_down(rows, width):
    over = rows.shape[-1] - width
    group = rows.shape[-2] * over // width
    tail = [rows[..., at : at + group, width:] for at in range(0, rows.shape[-2], group)]
    return jnp.concatenate([rows[..., :width], jnp.concatenate(tail, axis=-1)], axis=-2)


def unfold_down(rows, model):
    width = rows.shape[-1]
    over = model - width
    count = rows.shape[-2] * width // model
    tail = rows[..., count:, :]
    tail = [tail[..., at : at + over] for at in range(0, width, over)]
    return jnp.concatenate([rows[..., :count, :], jnp.concatenate(tail, axis=-2)], axis=-1)


def cost(micros):
    return pl.CostEstimate(flops=0, bytes_accessed=int(micros * 3.0e6), transcendentals=0)


def kernel_call(kernel, micros, outs, scratch=()):
    return pl.pallas_call(
        kernel,
        cost_estimate=cost(micros),
        out_shape=[jax.ShapeDtypeStruct(shape, dtype) for shape, dtype in outs],
        scratch_shapes=list(scratch),
        compiler_params=pltpu.CompilerParams(vmem_limit_bytes=vmem_limit),
    )


def chunk_rows(chunk, size):
    return pl.ds(pl.multiple_of(chunk * size, size), size)


def panels(ref, rows):
    return jnp.concatenate([ref[at, rows, :] for at in range(ref.shape[0])], axis=1)


def set_panels(ref, rows, value):
    for at in range(ref.shape[0]):
        ref[at, rows, :] = value[:, at * 128 : (at + 1) * 128]


def gates_kernel(
    cin, halo, masks, params, w_in, w_rec,
    conv, factor, g_in, g_rec, kept_out, state, decay, ends, ext, raw_in, raw_rec, drive,
):
    tokens, width = cin.shape
    count = halo.shape[0]
    size = tokens // count
    tiles = width // 128

    def convolve(chunk, carry):
        rows = chunk_rows(chunk, size)
        ext[0:8, :] = halo[chunk].astype(f32)
        ext[8 : 8 + size, :] = cin[rows, :].astype(f32)
        total = params[4:5, :] + params[0:1, :] * ext[8 : 8 + size, :]
        for k in (1, 2, 3):
            total = total + params[k : k + 1, :] * ext[8 - k : 8 - k + size, :] * masks[rows, k : k + 1]
        conv[rows, :] = total.astype(bf16)
        return carry

    lax.fori_loop(0, count, convolve, 0)
    raw_in[...] = jnp.dot(conv[...], w_in[...], preferred_element_type=f32)
    raw_rec[...] = jnp.dot(conv[...], w_rec[...], preferred_element_type=f32)

    def gate(chunk, carry):
        rows = chunk_rows(chunk, size)
        gate_in = jax.nn.sigmoid(raw_in[rows, :] + params[5:6, :])
        gate_rec = jax.nn.sigmoid(raw_rec[rows, :] + params[6:7, :])
        log_decay = gate_rec * params[7:8, :]
        base = jnp.exp(log_decay)
        kept = -jnp.tanh(log_decay) * (base * base + 1.0)
        scale = jnp.sqrt(jnp.maximum(kept, beta_floor))
        set_panels(factor, rows, base * masks[rows, 0:1])
        g_in[rows, :] = gate_in
        g_rec[rows, :] = gate_rec
        kept_out[rows, :] = kept
        set_panels(drive, rows, scale * gate_in * conv[rows, :].astype(f32))
        return carry

    lax.fori_loop(0, count, gate, 0)

    def scan(slot, carry):
        at = pl.ds(slot, count, stride=size)
        after = []
        for tile, (held, gone) in enumerate(carry):
            step = factor[tile, at, :]
            held = step * held + drive[tile, at, :]
            gone = step * gone
            state[tile, at, :] = held
            decay[tile, at, :] = gone
            after.append((held, gone))
        return tuple(after)

    first = pl.ds(0, count, stride=size)
    start = []
    for tile in range(tiles):
        zero = drive[tile, first, :] * 0.0
        start.append((zero, zero + 1.0))
    last = lax.fori_loop(0, size, scan, tuple(start))
    for tile, (held, gone) in enumerate(last):
        ends[0, :, tile * 128 : (tile + 1) * 128] = gone
        ends[1, :, tile * 128 : (tile + 1) * 128] = held


def carry_kernel(backward, spot, pieces, entering):
    mine = spot[0]
    places = pieces.shape[0]
    order = range(places - 1, -1, -1) if backward else range(places)
    decay, state = pieces[order[0], 0], pieces[order[0], 1]
    here = jnp.where(mine == order[0], 1.0, 0.0)
    own_decay, own_state = jnp.zeros_like(decay) + here, jnp.zeros_like(state)
    for place_at in order[1:]:
        here = jnp.where(mine == place_at, 1.0, 0.0)
        own_decay = own_decay + decay * here
        own_state = own_state + state * here
        step = pieces[place_at, 0]
        state = step * state + pieces[place_at, 1]
        decay = step * decay
    for row in range(2):
        held = jnp.zeros((2, decay.shape[1]), f32)
        for z in range(3, -1, -1) if backward else range(4):
            start = row * 8 + z * 2
            part = slice(start, start + 2)
            inside = own_decay[part] * held + own_state[part]
            held = decay[part] * held + state[part]
            for line in range(2):
                entering[start + line] = inside[line : line + 1]


def gelu_parts(value):
    slope = 0.7978845608028654
    square = value * value
    inner = jnp.tanh(slope * (value + 0.044715 * value * square))
    half = 0.5 * (1.0 + inner)
    act = value * half
    grad = half + 0.5 * value * (1.0 - inner * inner) * slope * (1.0 + 3 * 0.044715 * square)
    return act, grad


def mix_kernel(pre, state, decay, entering, out_rows, rec_state, mixed, partial_sum):
    count = entering.shape[0]
    tokens, width = rec_state.shape
    size = tokens // count

    def mix(chunk, carry):
        rows = chunk_rows(chunk, size)
        full = panels(state, rows) + panels(decay, rows) * entering[chunk]
        rec_state[rows, :] = full
        mixed[rows, :] = (gelu_parts(pre[rows, :])[0] * full).astype(bf16)
        return carry

    lax.fori_loop(0, count, mix, 0)
    partial_sum[...] = jnp.dot(
        mixed[...], out_rows[...], preferred_element_type=f32
    ).astype(bf16)


def unmix_kernel(
    mixed_own, mixed_other, pre_own, pre_other, rec_own, rec_other, factor,
    grad_gelu, adjoint, reach, ends, grad_state,
):
    half, width = rec_own.shape
    count = ends.shape[1]
    size = 2 * half // count
    tiles = width // 128

    def unmix(start, grad_mixed, pre, rec_state, chunk, carry):
        rows = chunk_rows(chunk, size)
        out = chunk_rows(chunk + start, size)
        act, slope = gelu_parts(pre[rows, :])
        grad = grad_mixed[rows, :]
        grad_gelu[out, :] = (grad * rec_state[rows, :] * slope).astype(bf16)
        set_panels(grad_state, out, grad * act)
        return carry

    lax.fori_loop(0, count // 2, partial(unmix, 0, mixed_own, pre_own, rec_own), 0)
    lax.fori_loop(0, count // 2, partial(unmix, count // 2, mixed_other, pre_other, rec_other), 0)

    def scan(step, carry):
        at = pl.ds(size - 1 - step, count, stride=size)
        after = []
        for tile, (held, gone, ahead) in enumerate(carry):
            held = ahead * held + grad_state[tile, at, :]
            gone = ahead * gone
            adjoint[tile, at, :] = held
            reach[tile, at, :] = gone
            after.append((held, gone, factor[tile, at, :]))
        return tuple(after)

    first = pl.ds(0, count, stride=size)
    start = []
    for tile in range(tiles):
        zero = factor[tile, first, :] * 0.0
        start.append((zero, zero + 1.0, zero + 1.0))
    last = lax.fori_loop(0, size, scan, tuple(start))
    for tile, (held, gone, ahead) in enumerate(last):
        ends[0, :, tile * 128 : (tile + 1) * 128] = ahead * gone
        ends[1, :, tile * 128 : (tile + 1) * 128] = ahead * held


def ungate_kernel(
    adjoint, reach, arriving, rec_own, rec_other, entering, factor, g_in, g_rec, kept, conv, cin,
    halo, masks, params, w_in, w_rec, grad_in, grad_rec, grad_conv, sums, ext, direct,
):
    tokens, width = cin.shape
    count = halo.shape[0]
    size = tokens // count
    zero = params[0:8, :] * 0.0

    def fold(value):
        total = value[0:8]
        for at in range(8, size, 8):
            total = total + value[at : at + 8]
        return total

    def ungate(start, rec_state, chunk, carry):
        sum_in, sum_rec, sum_decay = carry
        ext[8 : 8 + size, :] = rec_state[chunk_rows(chunk, size), :]
        chunk = chunk + start
        rows = chunk_rows(chunk, size)
        ext[7:8, :] = entering[chunk]
        full = panels(adjoint, rows) + panels(reach, rows) * arriving[chunk]
        square = kept[rows, :]
        scale = jnp.sqrt(jnp.maximum(square, beta_floor))
        gate_in = g_in[rows, :]
        gate_rec = g_rec[rows, :]
        values = conv[rows, :].astype(f32)
        scaled = full * scale
        drive = full * gate_in * values
        slope = jnp.where(square > beta_floor, (1.0 - square) / scale, 0.0)
        grad_log = full * panels(factor, rows) * ext[7 : 7 + size, :] - slope * drive
        raw_in = scale * drive * (1.0 - gate_in)
        pulled = grad_log * gate_rec
        raw_rec = pulled * params[7:8, :] * (1.0 - gate_rec)
        grad_in[rows, :] = raw_in.astype(bf16)
        grad_rec[rows, :] = raw_rec.astype(bf16)
        direct[rows, :] = scaled * gate_in
        return (sum_in + fold(raw_in), sum_rec + fold(raw_rec), sum_decay + fold(pulled))

    half = count // 2
    totals = lax.fori_loop(0, half, partial(ungate, 0, rec_own), (zero, zero, zero))
    sum_in, sum_rec, sum_decay = lax.fori_loop(0, half, partial(ungate, half, rec_other), totals)
    back = (((1,), (1,)), ((), ()))
    direct[...] += lax.dot_general(grad_in[...], w_in[...], back, preferred_element_type=f32)
    direct[...] += lax.dot_general(grad_rec[...], w_rec[...], back, preferred_element_type=f32)

    def taps(chunk, carry):
        sum_bias, sum_taps = carry
        rows = chunk_rows(chunk, size)
        grad = direct[rows, :].astype(bf16)
        grad_conv[rows, :] = grad
        grad = grad.astype(f32)
        ext[0:8, :] = halo[chunk].astype(f32)
        ext[8 : 8 + size, :] = cin[rows, :].astype(f32)
        new_taps = [sum_taps[0] + fold(grad * ext[8 : 8 + size, :])]
        for k in (1, 2, 3):
            moved = ext[8 - k : 8 - k + size, :] * masks[rows, k : k + 1]
            new_taps.append(sum_taps[k] + fold(grad * moved))
        return (sum_bias + fold(grad), tuple(new_taps))

    sum_bias, sum_taps = lax.fori_loop(0, count, taps, (zero, (zero,) * 4))
    rows_out = sum_taps + (sum_bias, sum_in, sum_rec, sum_decay * params[8:9, :])
    for index, total in enumerate(rows_out):
        sums[index : index + 1, :] = jnp.sum(total, axis=0, keepdims=True)


def unconvolve_kernel(grad_conv, halo, masks, params, out, ext):
    tokens, width = grad_conv.shape
    count = halo.shape[0]
    size = tokens // count

    def spread(chunk, carry):
        rows = chunk_rows(chunk, size)
        ext[0:size, :] = grad_conv[rows, :].astype(f32)
        ext[size : size + 8, :] = halo[chunk].astype(f32)
        total = params[0:1, :] * ext[0:size, :]
        for k in (1, 2, 3):
            total = total + params[k : k + 1, :] * ext[k : k + size, :] * masks[rows, 3 + k : 4 + k]
        out[rows, :] = total.astype(bf16)
        return carry

    lax.fori_loop(0, count, spread, 0)


def body(
    tokens,
    lengths,
    norm_one,
    gelu_weight,
    input_weight,
    conv_weight,
    conv_bias,
    gate_input,
    bias_input,
    gate_recur,
    bias_recur,
    decay_param,
    out_weight,
    norm_two,
    gate_weight,
    up_weight,
    down_weight,
    cotangent,
):
    row_count, size, model = tokens.shape
    local = row_count * size
    block, hidden = gelu_weight.shape
    inner = gate_weight.shape[1]
    head = gate_input.shape[1]
    channels, units = hidden // 8, inner // 8
    strip = gate_input.shape[0]
    width = -(-channels // 128) * 128
    spare = width - channels
    row_at, z_at, y_at, x_at = (lax.axis_index(name) for name in everywhere)
    plane_at = y_at * 4 + x_at
    chunks = 16
    total_tokens = chunks * size
    flat = tokens.reshape(local, model)

    row_total = jnp.sum(lengths, axis=1)
    own_slots = (z_at * 16 + plane_at) * size + jnp.arange(size)
    valid = (own_slots[None, :] < row_total[:, None]).astype(f32).reshape(local, 1)
    upstream = cotangent.reshape(local, model).astype(f32) * valid

    def team_rows(block):
        whole = lax.all_gather(block, team, axis=0, tiled=False).reshape(2, 4 * local, model)
        return [
            lax.dynamic_index_in_dim(whole, row_at ^ other, 0, keepdims=False) for other in (0, 1)
        ]

    tokens_own, tokens_other = team_rows(flat)

    gains = jnp.stack([norm_one, norm_two], axis=1)
    gains = jnp.broadcast_to(
        jnp.pad(gains, ((0, 0), (0, spare - 2)))[:, None, :], (block, 8, spare)
    )
    lead = jnp.concatenate([input_weight.reshape(block, 8, channels), gains], axis=2)
    lead = lead.transpose(1, 0, 2)[:, None]
    lead = jnp.broadcast_to(lead, (8, 16, block, width)).reshape(model, width)
    input_full = lax.all_to_all(lead, everywhere, 0, 0, tiled=True)
    third = jnp.concatenate(
        [
            gate_weight.reshape(block, 8, units),
            up_weight.reshape(block, 8, units),
            gelu_weight.reshape(block, 8, channels),
            jnp.zeros_like(gains),
        ],
        axis=2,
    ).transpose(1, 0, 2)
    third = lax.all_to_all(after(third, input_full), team, 0, 0, tiled=True).reshape(8 * block, -1)
    first, third = third[:, 2 * units :], third[:, : 2 * units]
    small = jnp.stack([conv_bias, bias_input, bias_recur, decay_param], axis=1)
    rest = jnp.concatenate([gate_input, gate_recur, conv_weight, small], axis=1)
    rest = jnp.pad(rest, ((0, 32 - strip), (0, width - rest.shape[1])))
    rest = gather_plane(after(rest, first))[:, :strip].reshape(channels, width)
    rest = jnp.pad(rest, ((0, spare), (0, 0)))

    def in_order(rows, count):
        rows = rows.reshape(16, count, block, rows.shape[-1])
        return rows.transpose(1, 0, 2, 3).reshape(count * 16 * block, rows.shape[-1])

    cuts = -(-model // width)
    out_pack = jnp.pad(out_weight, ((0, 32 - strip), (0, cuts * width - model)))
    out_pack = out_pack.reshape(32, cuts, width).transpose(1, 0, 2).reshape(cuts * 32, width)
    second = jnp.concatenate([first, out_pack], axis=0)
    second = lax.all_gather(second, plane, axis=0, tiled=False)
    gelu_full = in_order(second[:, : 8 * block], 8)
    out_rows = second[:, 8 * block :].reshape(16, cuts, 32, width)[:, :, :strip]
    out_rows = out_rows.transpose(0, 2, 1, 3).reshape(channels, cuts * width)[:, :model]
    out_rows = jnp.pad(out_rows, ((0, spare), (0, 0)))

    third = jnp.concatenate([third, fold_down(down_weight, 2 * units)], axis=0)
    third = lax.all_gather(third, plane, axis=0, tiled=False)
    down = unfold_down(third[:, 8 * block :], model).reshape(units, model)
    third = in_order(third[:, : 8 * block], 8)

    gain_one = input_full[:, channels].astype(f32)[None, :]
    gain_two = input_full[:, channels + 1].astype(f32)[None, :]
    own_head = (jnp.arange(width)[:, None] // head) == (jnp.arange(width)[None, :] // head)

    def spread_heads(part):
        return jnp.where(own_head, jnp.concatenate([part, part, part], axis=1)[:, :width], 0)

    w_in = spread_heads(rest[:, :head])
    w_rec = spread_heads(rest[:, head : 2 * head])
    rows_small = rest[:, 2 * head : 2 * head + 8].astype(f32).T
    decay_row = rows_small[7:8]
    params = jnp.concatenate(
        [
            rows_small[:7],
            -8.0 * jax.nn.softplus(decay_row),
            -8.0 * jax.nn.sigmoid(decay_row),
            jnp.zeros((7, width), f32),
        ],
        axis=0,
    )

    lens = jnp.stack([lengths, hop(lengths, "row", 1)], axis=0)
    starts = jnp.cumsum(lens, axis=2) - lens
    first_slot = jnp.arange(4) * (16 * size) + plane_at * size

    def position(slot):
        live = (lens > 0)[:, None, :, None, :] & (starts[:, None, :, None, :] <= slot[..., None])
        origin = jnp.max(jnp.where(live, starts[:, None, :, None, :], 0), axis=-1)
        return slot - origin

    slots = first_slot[None, :, None, None] + jnp.arange(size)[None, None, None, :]
    slots = jnp.broadcast_to(slots, (2, 4, row_count, size))
    here = position(slots)
    columns = [here != 0] + [here >= k for k in (1, 2, 3)]
    for k in (1, 2, 3):
        ahead = slots + k
        columns.append((position(ahead) >= k) & (ahead < 64 * size))
    columns.append(jnp.zeros_like(columns[0]))
    masks = jnp.stack(columns, axis=-1).astype(f32).reshape(total_tokens, 8)

    def rms_unit(values):
        return lax.rsqrt(jnp.mean(values * values, axis=-1, keepdims=True) + epsilon)

    def norm_half(values):
        values = values.astype(f32)
        return (values * rms_unit(values) * gain_one).astype(bf16)

    normed_own, normed_other = norm_half(tokens_own), norm_half(tokens_other)

    def turned(rim, shift):
        by_z = rim.reshape((2, 4, row_count) + rim.shape[1:])
        return jnp.roll(by_z, shift, axis=1).reshape(rim.shape)

    conv_in = jnp.concatenate(
        [project_in(half, input_full).astype(bf16) for half in (normed_own, normed_other)], axis=0
    )
    by_chunk = (chunks, size, width)
    halo = hop(conv_in.reshape(by_chunk)[:, size - 8 :], plane, 1)
    halo = jnp.where(plane_at == 0, turned(halo, 1), halo)
    wide = ((total_tokens, width), f32)
    narrow = ((total_tokens, width), bf16)
    paneled = ((width // 128, total_tokens, 128), f32)
    ends_shape = ((2, chunks, width), f32)
    extended = pltpu.VMEM((size + 8, width), f32)
    whole = pltpu.VMEM(*wide)
    folded = pltpu.VMEM(*paneled)
    conv_vals, factor, g_in, g_rec, kept, local_state, decay, ends = kernel_call(
        gates_kernel,
        60,
        [narrow, paneled, wide, wide, wide, paneled, paneled, ends_shape],
        [extended, whole, whole, folded],
    )(conv_in, halo, masks, params, w_in, w_rec)

    down_own, down_other = team_rows(after(upstream.astype(bf16), ends))

    def carried(ends, backward):
        pieces = lax.all_to_all(jnp.broadcast_to(ends, (16,) + ends.shape), plane, 0, 0, tiled=True)
        spot = plane_at.astype(jnp.int32).reshape(1)
        return pl.pallas_call(
            partial(carry_kernel, backward),
            cost_estimate=cost(1),
            out_shape=jax.ShapeDtypeStruct((chunks, 1, width), f32),
            in_specs=[pl.BlockSpec(memory_space=pltpu.SMEM), pl.BlockSpec(memory_space=pltpu.VMEM)],
            out_specs=pl.BlockSpec(memory_space=pltpu.VMEM),
        )(spot, pieces)

    entering = carried(ends, False)
    gelu_own, gelu_other = project_in(normed_own, gelu_full), project_in(normed_other, gelu_full)
    half = total_tokens // 2

    def mix(which, gelu_pre):
        rows = pl.BlockSpec((half, width), lambda i: (0, 0))
        folds = pl.BlockSpec((width // 128, half, 128), lambda i: (0, which, 0))
        return pl.pallas_call(
            mix_kernel,
            cost_estimate=cost(5),
            out_shape=[
                jax.ShapeDtypeStruct((half, width), f32),
                jax.ShapeDtypeStruct((half, width), bf16),
                jax.ShapeDtypeStruct((half, model), bf16),
            ],
            grid=(1,),
            in_specs=[
                rows,
                folds,
                folds,
                pl.BlockSpec((chunks // 2, 1, width), lambda i: (which, 0, 0)),
                pl.BlockSpec((width, model), lambda i: (0, 0)),
            ],
            out_specs=[
                pl.BlockSpec((half, width), lambda i: (0, 0)),
                pl.BlockSpec((half, width), lambda i: (0, 0)),
                pl.BlockSpec((half, model), lambda i: (0, 0)),
            ],
            compiler_params=pltpu.CompilerParams(vmem_limit_bytes=vmem_limit),
        )(gelu_pre, local_state, decay, entering, out_rows)

    other_state, other_mixed, other_middle = mix(1, gelu_other)
    own_state, own_mixed, own_middle = mix(0, gelu_own)
    mixed = jnp.concatenate([own_mixed, other_mixed], axis=0)
    own_tokens = flat.astype(f32)
    middle = own_tokens + reduce_team(other_middle, own_middle)[0]

    scale_two = rms_unit(middle)
    normed_two = (middle * scale_two * gain_two).astype(bf16)
    two_own, two_other, _ = gather_team(normed_two)

    def feed(values, grad_inner):
        pre = project_in(values, third)
        act, slope = gelu_parts(pre[:, :units])
        up = pre[:, units:]
        grad = [(grad_inner * up * slope).astype(bf16), (grad_inner * act).astype(bf16)]
        return (act * up).astype(bf16), jnp.concatenate(grad, axis=1)

    inner_own, pre_own = feed(two_own, project_back(down_own, down))
    inner_other, pre_other = feed(two_other, project_back(down_other, down))
    terms_other = project_back(pre_other, third).astype(bf16)
    terms_own = project_back(pre_own, third).astype(bf16)
    grad_two, _ = reduce_team(terms_other, terms_own)
    grad_down, inner_act = joined(down_own, down_other), joined(inner_own, inner_other)
    team_two, grad_pre = joined(two_own, two_other), joined(pre_own, pre_other)

    def by_owner(grad):
        grad = grad.astype(bf16).reshape(-1, 16, block, grad.shape[1]).transpose(1, 0, 2, 3)
        return grad.reshape(16, -1, grad.shape[-1])

    def back_to_rows(grad):
        grad = grad.astype(bf16).reshape(8, block, -1)
        return lax.all_to_all(grad, team, 0, 0, tiled=True).astype(f32).transpose(1, 0, 2)

    def norm_back(values, scale, gain, grad):
        pulled = gain * grad
        mean = jnp.mean(pulled * values, axis=-1, keepdims=True)
        return scale * pulled - values * (scale * scale * scale * mean)

    def gain_grad(gain, pairs):
        total = sum(jnp.sum(weight.astype(f32) * grad, axis=1) for weight, grad in pairs)
        return total / gain.astype(f32)

    grad_middle = upstream + norm_back(middle, scale_two, gain_two, grad_two)
    branch_own, branch_other, first_branch = gather_team(grad_middle.astype(bf16))
    grad_third = jnp.concatenate(
        [
            by_owner(after(outer_sum(team_two, grad_pre).astype(bf16), *first_branch)),
            fold_down(
                after(outer_sum(inner_act, grad_down).astype(bf16), *first_branch).reshape(
                    16, -1, model
                ),
                2 * units,
            ),
        ],
        axis=1,
    )
    share = grad_third.shape[1]
    grad_third = lax.psum_scatter(
        grad_third.reshape(16 * share, 2 * units), plane, scatter_dimension=0, tiled=True
    )
    grad_down_weight = unfold_down(grad_third[8 * block :], model).astype(f32)

    grad_gelu, adjoint, reach, ends = kernel_call(
        unmix_kernel, 100, [narrow, paneled, paneled, ends_shape], [folded]
    )(
        project_back(branch_own, out_rows), project_back(branch_other, out_rows),
        gelu_own, gelu_other, own_state, other_state, factor,
    )
    normed = joined(normed_own, normed_other)
    grad_branch = joined(branch_own, branch_other)
    grad_out_weight = outer_sum(mixed, grad_branch)[:channels].astype(bf16)
    grad_gelu_full = outer_sum(normed, grad_gelu).astype(bf16)
    grad_out_rows = after(grad_out_weight, branch_other).reshape(16, strip, model)
    grad_out_rows = lax.all_to_all(grad_out_rows, plane, 0, 0, tiled=True)
    arriving = carried(after(ends, grad_out_rows), True)
    arriving = after(arriving, grad_gelu_full)
    grad_gelu_rows = after(by_owner(grad_gelu_full), arriving)
    grad_gelu_rows = lax.all_to_all(grad_gelu_rows, plane, 0, 0, tiled=True)
    grad_in, grad_rec, grad_conv, sums = kernel_call(
        ungate_kernel, 100, [narrow, narrow, narrow, ((8, width), f32)], [extended, whole]
    )(
        adjoint, reach, arriving, own_state, other_state, entering, factor, g_in, g_rec, kept,
        conv_vals, conv_in, halo, masks, params, w_in, w_rec,
    )
    first_half = lax.select(row_at == 0, inner_own, inner_other)
    inner_rows = joined(first_half, lax.select(row_at == 0, inner_other, inner_own))
    result = project_in(after(inner_rows, grad_conv), down).astype(bf16)
    result = lax.psum_scatter(result, team, scatter_dimension=0, tiled=True)
    result = (middle + result.astype(f32)) * valid
    output = result.reshape(row_count, size, model).astype(bf16)
    ahead = hop(grad_conv.reshape(by_chunk)[:, :8], plane, -1)
    ahead = jnp.where(plane_at == 15, turned(ahead, -1), ahead)
    (grad_conv_in,) = kernel_call(unconvolve_kernel, 1, [narrow], [extended])(
        grad_conv, ahead, masks, params
    )

    def own_heads(grad):
        grad = jnp.where(own_head, grad, 0)[:channels]
        return grad[:, :head] + grad[:, head:channels]

    grad_conv_in = after(grad_conv_in, grad_gelu_rows)
    grad_pair = jnp.concatenate([grad_conv_in, grad_gelu], axis=1)
    pair_weight = jnp.concatenate([input_full, gelu_full], axis=1)
    terms_other = project_back(grad_pair[half:], pair_weight).astype(bf16)
    grad_normed, upward = reduce_team(terms_other, project_back(grad_pair[:half], pair_weight).astype(bf16))
    grad_rest = jnp.concatenate(
        [
            own_heads(outer_sum(conv_vals, grad_in)),
            own_heads(outer_sum(conv_vals, grad_rec)),
            sums.T[:channels],
        ],
        axis=1,
    ).astype(bf16)
    grad_rest = grad_rest.reshape(16, strip, -1)
    grad_rest = jnp.pad(
        grad_rest, ((0, 0), (0, 32 - strip), (0, width - grad_rest.shape[2]))
    )
    grad_input_full = outer_sum(normed, grad_conv_in).astype(bf16)
    grad_lead = jnp.concatenate([by_owner(grad_input_full), grad_rest], axis=1)
    grad_lead = lax.all_to_all(grad_lead, plane, 0, 0, tiled=True)
    grad_lead = total_of(after(grad_lead, upward))
    cut = 8 * block
    grad_rest = grad_lead[cut : cut + strip]
    grad_out_weight = total_of(after(grad_out_rows, upward))
    grad_gelu_rows = total_of(after(grad_gelu_rows, upward)).astype(bf16)
    grad_gate_input = grad_rest[:, :head]
    grad_gate_recur = grad_rest[:, head : 2 * head]
    grad_small = grad_rest[:, 2 * head : 2 * head + 8]
    team_third = jnp.concatenate(
        [after(grad_third[:cut], upward), grad_lead[:cut].astype(bf16), grad_gelu_rows], axis=1
    )
    team_third = back_to_rows(team_third)
    grad_input_weight = team_third[:, :, 2 * units : 2 * units + channels].reshape(block, hidden)
    grad_gelu_weight = team_third[:, :, 2 * units + width :][:, :, :channels].reshape(block, hidden)
    grad_gate_weight = team_third[:, :, :units].reshape(block, inner)
    grad_up_weight = team_third[:, :, units : 2 * units].reshape(block, inner)

    grad_norm_two = gain_grad(
        norm_two, [(gate_weight, grad_gate_weight), (up_weight, grad_up_weight)]
    )
    grad_norm_one = gain_grad(
        norm_one, [(gelu_weight, grad_gelu_weight), (input_weight, grad_input_weight)]
    )
    own_scale = rms_unit(own_tokens)
    grad_tokens = grad_middle + norm_back(own_tokens, own_scale, gain_one, grad_normed)
    return (
        output,
        grad_tokens.reshape(row_count, size, model),
        grad_norm_one,
        grad_gelu_weight,
        grad_input_weight,
        grad_small[:, :4],
        grad_small[:, 4],
        grad_gate_input,
        grad_small[:, 5],
        grad_gate_recur,
        grad_small[:, 6],
        grad_small[:, 7],
        grad_out_weight,
        grad_norm_two,
        grad_gate_weight,
        grad_up_weight,
        grad_down_weight,
    )


def solution(mesh):
    grid = Mesh(mesh.devices.reshape(2, 4, 4, 4), everywhere)
    slots = P("row", ("z", "y", "x"), None)
    line = P(everywhere)
    sheet = P(everywhere, None)
    return jax.shard_map(
        body,
        mesh=grid,
        in_specs=(
            slots, P("row", None), line, sheet, sheet, sheet, line, sheet, line, sheet, line, line,
            sheet, line, sheet, sheet, sheet, slots,
        ),
        out_specs=(
            slots, slots, line, sheet, sheet, sheet, line, sheet, line, sheet, line, line, sheet,
            line, sheet, sheet, sheet,
        ),
        check_vma=False,
    )
```

```python
from functools import partial

import jax
import jax.numpy as jnp
from jax import lax
from jax.experimental import pallas as pl
from jax.experimental.pallas import tpu as pltpu
from jax.sharding import Mesh
from jax.sharding import PartitionSpec as P

epsilon = 1e-06
beta_floor = 0.001
bf16 = jnp.bfloat16
f32 = jnp.float32
everywhere = ("row", "z", "y", "x")
team = ("row", "z")
plane = ("y", "x")
vmem_limit = 32 * 1024 * 1024


def hop(block, axis, distance):
    count = lax.axis_size(axis)
    return lax.ppermute(block, axis, [(i, (i + distance) % count) for i in range(count)])


def gather_plane(piece):
    return lax.all_to_all(jnp.broadcast_to(piece, (16,) + piece.shape), plane, 0, 0, tiled=True)


def outer_kernel(packed, left_own, left_other, right_own, right_other, out):
    total = outer_sum(left_own[...], right_own[...]) + outer_sum(left_other[...], right_other[...])
    count, rows, columns = out.shape
    total = total.astype(bf16).reshape(count, rows, total.shape[1])
    out[:, :, : total.shape[2]] = total
    if total.shape[2] < columns:
        out[:, :, total.shape[2] :] = jnp.zeros((count, rows, columns - total.shape[2]), bf16)


def add_outer(packed, left, right):
    half, model = left[0].shape
    if len(right) == 1:
        right, starts = right * 2, (0, 1)
    else:
        starts = (0, 0)
    columns = right[0].shape[1]
    block = model // 128
    return pl.pallas_call(
        outer_kernel,
        cost_estimate=cost(model * columns / 350000),
        grid=(8,),
        in_specs=[pl.BlockSpec(memory_space=pl.ANY)]
        + [pl.BlockSpec((half, 16 * block), lambda s: (0, s))] * 2
        + [pl.BlockSpec((half, columns), partial(lambda at, s: (at, 0), at)) for at in starts],
        out_specs=pl.BlockSpec((16, block, packed.shape[2]), lambda s: (0, s, 0)),
        out_shape=jax.ShapeDtypeStruct(packed.shape, packed.dtype),
        input_output_aliases={0: 0},
        compiler_params=pltpu.CompilerParams(vmem_limit_bytes=vmem_limit),
    )(packed, *left, *right)


def strips_kernel(strip, left_own, left_other, right_own, right_other, out, total):
    total[...] = outer_sum(left_own[...], right_own[...]) + outer_sum(
        left_other[...], right_other[...]
    )
    for place in range(out.shape[0]):
        start = place * strip
        out[place] = total[start : start + out.shape[1], :].astype(bf16)


def outer_strips(left, right, strip, shape):
    places, rows, columns = shape
    half, width = left[0].shape
    model = right[0].shape[1]
    return pl.pallas_call(
        partial(strips_kernel, strip),
        cost_estimate=cost(4),
        grid=(model // columns,),
        in_specs=[pl.BlockSpec((half, width), lambda s: (0, 0))] * 2
        + [pl.BlockSpec((half, columns), lambda s: (0, s))] * 2,
        out_specs=pl.BlockSpec((places, 32, columns), lambda s: (0, s, 0)),
        out_shape=jax.ShapeDtypeStruct(shape, bf16),
        scratch_shapes=[pltpu.VMEM((width, columns), f32)],
        compiler_params=pltpu.CompilerParams(vmem_limit_bytes=vmem_limit),
    )(*left, *right)


def folded_kernel(left_own, left_other, right_own, right_other, out):
    _, rows, columns = out.shape
    total = outer_sum(left_own[...], right_own[...]) + outer_sum(left_other[...], right_other[...])
    total = total.astype(bf16).reshape(out.shape[0], -1, total.shape[1])
    tall = total.shape[1]
    out[:, :tall, :] = total[:, :, :columns]
    over = total.shape[2] - columns
    for at in range(columns // over):
        part = total[:, at * (rows - tall) : (at + 1) * (rows - tall), columns:]
        out[:, tall:, at * over : (at + 1) * over] = part


def outer_folded(left, right, shape):
    places, rows, columns = shape
    tokens, units = left[0].shape
    model = right[0].shape[1]
    high = units * model // (places * columns)
    return pl.pallas_call(
        folded_kernel,
        cost_estimate=cost(5),
        grid=(2,),
        in_specs=[pl.BlockSpec((tokens, units // 2), lambda s: (0, s))] * 2
        + [pl.BlockSpec((tokens, model), lambda s: (0, 0))] * 2,
        out_specs=pl.BlockSpec((places // 2, high, columns), lambda s: (s, rows // high - 1, 0)),
        out_shape=jax.ShapeDtypeStruct(shape, bf16),
        compiler_params=pltpu.CompilerParams(vmem_limit_bytes=vmem_limit),
    )(*left, *right)


def total_of(pieces):
    return jnp.sum(pieces.astype(f32), axis=0)


def after(value, *others):
    return lax.optimization_barrier((value,) + others)[0]


def joined(*parts):
    return jnp.concatenate(parts, axis=0)


def gather_team(block, *stage):
    z_at = lax.axis_index("z")
    half = block.shape[0] // 2
    below, above = hop(block, "z", 1), hop(block, "z", -1)
    if stage:
        below, above = after(below, *stage), after(above, *stage)
    across = joined(hop(below[:half], "z", 1), hop(above[half:], "z", -1))
    own = jnp.zeros((4,) + block.shape, block.dtype)
    for offset, part in ((0, block), (1, above), (3, below), (2, across)):
        own = lax.dynamic_update_index_in_dim(own, part, (z_at + offset) % 4, 0)
    own = own.reshape(4 * block.shape[0], -1)
    return own, hop(own, "row", 1)


def reduce_team(other, own):
    z_at = lax.axis_index("z")
    other = hop(other, "row", 1).reshape(4, -1, other.shape[-1])
    own = own.reshape(other.shape)

    def block(offset):
        at = (z_at + offset) % 4
        parts = [lax.dynamic_index_in_dim(whole, at, 0, keepdims=False) for whole in (own, other)]
        return parts[0].astype(f32) + parts[1].astype(f32)

    sums = {offset: block(offset) for offset in (2, 1, 3, 0)}
    half = own.shape[1] // 2
    from_below = hop(sums[2][:half].astype(bf16), "z", 1)
    from_above = hop(sums[2][half:].astype(bf16), "z", -1)
    up = joined(sums[1][:half] + from_below.astype(f32), sums[1][half:]).astype(bf16)
    down = joined(sums[3][:half], sums[3][half:] + from_above.astype(f32)).astype(bf16)
    up, down = hop(up, "z", 1), hop(down, "z", -1)
    return sums[0] + up.astype(f32) + down.astype(f32), up


def project_in(left, weight):
    return jnp.dot(left, weight, preferred_element_type=f32)


def project_back(grad, weight):
    return lax.dot_general(grad, weight, (((1,), (1,)), ((), ())), preferred_element_type=f32)


def outer_sum(left, grad):
    return lax.dot_general(left, grad, (((0,), (0,)), ((), ())), preferred_element_type=f32)


def fold_down(rows, width):
    over = rows.shape[-1] - width
    group = rows.shape[-2] * over // width
    tail = [rows[..., at : at + group, width:] for at in range(0, rows.shape[-2], group)]
    return jnp.concatenate([rows[..., :width], jnp.concatenate(tail, axis=-1)], axis=-2)


def unfold_down(rows, model):
    width = rows.shape[-1]
    over = model - width
    count = rows.shape[-2] * width // model
    tail = rows[..., count:, :]
    tail = [tail[..., at : at + over] for at in range(0, width, over)]
    return jnp.concatenate([rows[..., :count, :], jnp.concatenate(tail, axis=-2)], axis=-1)


def cost(micros):
    return pl.CostEstimate(flops=0, bytes_accessed=int(micros * 3.0e6), transcendentals=0)


def kernel_call(kernel, micros, outs, scratch=()):
    return pl.pallas_call(
        kernel,
        cost_estimate=cost(micros),
        out_shape=[jax.ShapeDtypeStruct(shape, dtype) for shape, dtype in outs],
        scratch_shapes=list(scratch),
        compiler_params=pltpu.CompilerParams(vmem_limit_bytes=vmem_limit),
    )


def chunk_rows(chunk, size):
    return pl.ds(pl.multiple_of(chunk * size, size), size)


def panels(ref, rows):
    return jnp.concatenate([ref[at, rows, :] for at in range(ref.shape[0])], axis=1)


def set_panels(ref, rows, value):
    for at in range(ref.shape[0]):
        ref[at, rows, :] = value[:, at * 128 : (at + 1) * 128]


def gate_parts(raw_in, raw_rec, params):
    gate_in = jax.nn.sigmoid(raw_in + params[5:6, :])
    gate_rec = jax.nn.sigmoid(raw_rec + params[6:7, :])
    log_decay = gate_rec * params[7:8, :]
    base = jnp.exp(log_decay)
    return gate_in, gate_rec, base, -jnp.tanh(log_decay) * (base * base + 1.0)


def gates_kernel(
    cin, halo, masks, params, w_in, w_rec,
    conv, factor, state, decay, ends, ext, raw_in, raw_rec, drive,
):
    tokens, width = cin.shape
    count = halo.shape[0]
    size = tokens // count
    tiles = width // 128

    def convolve(chunk, carry):
        rows = chunk_rows(chunk, size)
        ext[0:8, :] = halo[chunk].astype(f32)
        ext[8 : 8 + size, :] = cin[rows, :].astype(f32)
        total = params[4:5, :] + params[0:1, :] * ext[8 : 8 + size, :]
        for k in (1, 2, 3):
            total = total + params[k : k + 1, :] * ext[8 - k : 8 - k + size, :] * masks[rows, k : k + 1]
        conv[rows, :] = total.astype(bf16)
        return carry

    lax.fori_loop(0, count, convolve, 0)
    raw_in[...] = jnp.dot(conv[...], w_in[...], preferred_element_type=f32)
    raw_rec[...] = jnp.dot(conv[...], w_rec[...], preferred_element_type=f32)

    def gate(chunk, carry):
        rows = chunk_rows(chunk, size)
        gate_in, _, base, kept = gate_parts(raw_in[rows, :], raw_rec[rows, :], params)
        scale = jnp.sqrt(jnp.maximum(kept, beta_floor))
        set_panels(factor, rows, base * masks[rows, 0:1])
        set_panels(drive, rows, scale * gate_in * conv[rows, :].astype(f32))
        return carry

    lax.fori_loop(0, count, gate, 0)

    def scan(slot, carry):
        at = pl.ds(slot, count, stride=size)
        after = []
        for tile, (held, gone) in enumerate(carry):
            step = factor[tile, at, :]
            held = step * held + drive[tile, at, :]
            gone = step * gone
            state[tile, at, :] = held
            decay[tile, at, :] = gone
            after.append((held, gone))
        return tuple(after)

    first = pl.ds(0, count, stride=size)
    start = []
    for tile in range(tiles):
        zero = drive[tile, first, :] * 0.0
        start.append((zero, zero + 1.0))
    last = lax.fori_loop(0, size, scan, tuple(start))
    for tile, (held, gone) in enumerate(last):
        ends[0, :, tile * 128 : (tile + 1) * 128] = gone
        ends[1, :, tile * 128 : (tile + 1) * 128] = held


def carry_kernel(backward, spot, pieces, entering):
    mine = spot[0]
    places = pieces.shape[0]
    order = range(places - 1, -1, -1) if backward else range(places)
    decay, state = pieces[order[0], 0], pieces[order[0], 1]
    here = jnp.where(mine == order[0], 1.0, 0.0)
    own_decay, own_state = jnp.zeros_like(decay) + here, jnp.zeros_like(state)
    for place_at in order[1:]:
        here = jnp.where(mine == place_at, 1.0, 0.0)
        own_decay = own_decay + decay * here
        own_state = own_state + state * here
        step = pieces[place_at, 0]
        state = step * state + pieces[place_at, 1]
        decay = step * decay
    for row in range(2):
        held = jnp.zeros((2, decay.shape[1]), f32)
        for z in range(3, -1, -1) if backward else range(4):
            start = row * 8 + z * 2
            part = slice(start, start + 2)
            inside = own_decay[part] * held + own_state[part]
            held = decay[part] * held + state[part]
            for line in range(2):
                entering[start + line] = inside[line : line + 1]


def gelu_parts(value):
    slope = 0.7978845608028654
    square = value * value
    inner = jnp.tanh(slope * (value + 0.044715 * value * square))
    half = 0.5 * (1.0 + inner)
    act = value * half
    grad = half + 0.5 * value * (1.0 - inner * inner) * slope * (1.0 + 3 * 0.044715 * square)
    return act, grad


def mix_kernel(pre, state, decay, entering, out_rows, rec_state, mixed, partial_sum):
    count = entering.shape[0]
    tokens, width = rec_state.shape
    size = tokens // count

    def mix(chunk, carry):
        rows = chunk_rows(chunk, size)
        full = panels(state, rows) + panels(decay, rows) * entering[chunk]
        rec_state[rows, :] = full
        mixed[rows, :] = (gelu_parts(pre[rows, :])[0] * full).astype(bf16)
        return carry

    lax.fori_loop(0, count, mix, 0)
    partial_sum[...] = jnp.dot(
        mixed[...], out_rows[...], preferred_element_type=f32
    ).astype(bf16)


def unmix_kernel(
    mixed_own, mixed_other, pre_own, pre_other, rec_own, rec_other, factor,
    grad_gelu, adjoint, reach, ends, grad_state,
):
    half, width = rec_own.shape
    count = ends.shape[1]
    size = 2 * half // count
    tiles = width // 128

    def unmix(start, grad_mixed, pre, rec_state, chunk, carry):
        rows = chunk_rows(chunk, size)
        out = chunk_rows(chunk + start, size)
        act, slope = gelu_parts(pre[rows, :])
        grad = grad_mixed[rows, :]
        grad_gelu[out, :] = (grad * rec_state[rows, :] * slope).astype(bf16)
        set_panels(grad_state, out, grad * act)
        return carry

    lax.fori_loop(0, count // 2, partial(unmix, 0, mixed_own, pre_own, rec_own), 0)
    lax.fori_loop(0, count // 2, partial(unmix, count // 2, mixed_other, pre_other, rec_other), 0)

    def scan(step, carry):
        at = pl.ds(size - 1 - step, count, stride=size)
        after = []
        for tile, (held, gone, ahead) in enumerate(carry):
            held = ahead * held + grad_state[tile, at, :]
            gone = ahead * gone
            adjoint[tile, at, :] = held
            reach[tile, at, :] = gone
            after.append((held, gone, factor[tile, at, :]))
        return tuple(after)

    first = pl.ds(0, count, stride=size)
    start = []
    for tile in range(tiles):
        zero = factor[tile, first, :] * 0.0
        start.append((zero, zero + 1.0, zero + 1.0))
    last = lax.fori_loop(0, size, scan, tuple(start))
    for tile, (held, gone, ahead) in enumerate(last):
        ends[0, :, tile * 128 : (tile + 1) * 128] = ahead * gone
        ends[1, :, tile * 128 : (tile + 1) * 128] = ahead * held


def ungate_kernel(
    adjoint, reach, arriving, rec_own, rec_other, entering, conv, cin, halo, masks, params, w_in,
    w_rec, grad_in, grad_rec, grad_conv, sums, ext, direct, raw_rec,
):
    tokens, width = cin.shape
    count = halo.shape[0]
    size = tokens // count
    zero = params[0:8, :] * 0.0

    def fold(value):
        total = value[0:8]
        for at in range(8, size, 8):
            total = total + value[at : at + 8]
        return total

    def ungate(start, rec_state, chunk, carry):
        sum_in, sum_rec, sum_decay = carry
        ext[8 : 8 + size, :] = rec_state[chunk_rows(chunk, size), :]
        chunk = chunk + start
        rows = chunk_rows(chunk, size)
        ext[7:8, :] = entering[chunk]
        full = panels(adjoint, rows) + panels(reach, rows) * arriving[chunk]
        gate_in, gate_rec, base, square = gate_parts(direct[rows, :], raw_rec[rows, :], params)
        scale = jnp.sqrt(jnp.maximum(square, beta_floor))
        values = conv[rows, :].astype(f32)
        scaled = full * scale
        drive = full * gate_in * values
        slope = jnp.where(square > beta_floor, (1.0 - square) / scale, 0.0)
        grad_log = full * base * masks[rows, 0:1] * ext[7 : 7 + size, :] - slope * drive
        raw_in = scale * drive * (1.0 - gate_in)
        pulled = grad_log * gate_rec
        rec = pulled * params[7:8, :] * (1.0 - gate_rec)
        grad_in[rows, :] = raw_in.astype(bf16)
        grad_rec[rows, :] = rec.astype(bf16)
        direct[rows, :] = scaled * gate_in
        return (sum_in + fold(raw_in), sum_rec + fold(rec), sum_decay + fold(pulled))

    direct[...] = jnp.dot(conv[...], w_in[...], preferred_element_type=f32)
    raw_rec[...] = jnp.dot(conv[...], w_rec[...], preferred_element_type=f32)
    half = count // 2
    totals = lax.fori_loop(0, half, partial(ungate, 0, rec_own), (zero, zero, zero))
    sum_in, sum_rec, sum_decay = lax.fori_loop(0, half, partial(ungate, half, rec_other), totals)
    back = (((1,), (1,)), ((), ()))
    direct[...] += lax.dot_general(grad_in[...], w_in[...], back, preferred_element_type=f32)
    direct[...] += lax.dot_general(grad_rec[...], w_rec[...], back, preferred_element_type=f32)

    def taps(chunk, carry):
        sum_bias, sum_taps = carry
        rows = chunk_rows(chunk, size)
        grad = direct[rows, :].astype(bf16)
        grad_conv[rows, :] = grad
        grad = grad.astype(f32)
        ext[0:8, :] = halo[chunk].astype(f32)
        ext[8 : 8 + size, :] = cin[rows, :].astype(f32)
        new_taps = [sum_taps[0] + fold(grad * ext[8 : 8 + size, :])]
        for k in (1, 2, 3):
            moved = ext[8 - k : 8 - k + size, :] * masks[rows, k : k + 1]
            new_taps.append(sum_taps[k] + fold(grad * moved))
        return (sum_bias + fold(grad), tuple(new_taps))

    sum_bias, sum_taps = lax.fori_loop(0, count, taps, (zero, (zero,) * 4))
    rows_out = sum_taps + (sum_bias, sum_in, sum_rec, sum_decay * params[8:9, :])
    for index, total in enumerate(rows_out):
        sums[index : index + 1, :] = jnp.sum(total, axis=0, keepdims=True)


def unconvolve_kernel(grad_conv, halo, masks, params, out, ext):
    tokens, width = grad_conv.shape
    count = halo.shape[0]
    size = tokens // count

    def spread(chunk, carry):
        rows = chunk_rows(chunk, size)
        ext[0:size, :] = grad_conv[rows, :].astype(f32)
        ext[size : size + 8, :] = halo[chunk].astype(f32)
        total = params[0:1, :] * ext[0:size, :]
        for k in (1, 2, 3):
            total = total + params[k : k + 1, :] * ext[k : k + size, :] * masks[rows, 3 + k : 4 + k]
        out[rows, :] = total.astype(bf16)
        return carry

    lax.fori_loop(0, count, spread, 0)


def body(
    tokens,
    lengths,
    norm_one,
    gelu_weight,
    input_weight,
    conv_weight,
    conv_bias,
    gate_input,
    bias_input,
    gate_recur,
    bias_recur,
    decay_param,
    out_weight,
    norm_two,
    gate_weight,
    up_weight,
    down_weight,
    cotangent,
):
    row_count, size, model = tokens.shape
    local = row_count * size
    block, hidden = gelu_weight.shape
    inner = gate_weight.shape[1]
    head = gate_input.shape[1]
    channels, units = hidden // 8, inner // 8
    strip = gate_input.shape[0]
    width = -(-channels // 128) * 128
    spare = width - channels
    row_at, z_at, y_at, x_at = (lax.axis_index(name) for name in everywhere)
    plane_at = y_at * 4 + x_at
    chunks = 16
    total_tokens = chunks * size
    flat = tokens.reshape(local, model)

    row_total = jnp.sum(lengths, axis=1)
    own_slots = (z_at * 16 + plane_at) * size + jnp.arange(size)
    valid = (own_slots[None, :] < row_total[:, None]).astype(f32).reshape(local, 1)
    upstream = cotangent.reshape(local, model).astype(f32) * valid

    def halves(whole):
        whole = whole.reshape(2, 4 * local, -1)
        return [
            lax.dynamic_index_in_dim(whole, row_at ^ other, 0, keepdims=False) for other in (0, 1)
        ]

    tokens_own, tokens_other = halves(lax.all_gather(flat, team, axis=0, tiled=True))

    gains = jnp.stack([norm_one, norm_two], axis=1)
    gains = jnp.broadcast_to(
        jnp.pad(gains, ((0, 0), (0, spare - 2)))[:, None, :], (block, 8, spare)
    )
    third = jnp.concatenate(
        [
            gelu_weight.reshape(block, 8, channels),
            jnp.zeros_like(gains),
            gate_weight.reshape(block, 8, units),
            up_weight.reshape(block, 8, units),
        ],
        axis=2,
    ).transpose(1, 0, 2)
    lead = jnp.concatenate([input_weight.reshape(block, 8, channels), gains], axis=2)
    lead = lead.transpose(1, 0, 2)[:, None]
    lead = jnp.broadcast_to(lead, (8, 16, block, width)).reshape(model, width)
    input_full = lax.all_to_all(lead, everywhere, 0, 0, tiled=True)
    third = lax.all_to_all(after(third, input_full), team, 0, 0, tiled=True).reshape(8 * block, -1)
    first, third = third[:, :width], third[:, width:]
    small = jnp.stack([conv_bias, bias_input, bias_recur, decay_param], axis=1)
    rest = jnp.concatenate([gate_input, gate_recur, conv_weight, small], axis=1)
    rest = jnp.pad(rest, ((0, 32 - strip), (0, width - rest.shape[1])))
    rest = gather_plane(after(rest, first))

    def in_order(rows, count):
        rows = rows.reshape(16, count, block, rows.shape[-1])
        return rows.transpose(1, 0, 2, 3).reshape(count * 16 * block, rows.shape[-1])

    cuts = -(-model // width)
    out_pack = jnp.pad(out_weight, ((0, 32 - strip), (0, cuts * width - model)))
    out_pack = out_pack.reshape(32, cuts, width).transpose(1, 0, 2).reshape(cuts * 32, width)
    second = jnp.concatenate([first, out_pack], axis=0)
    second = lax.all_gather(second, plane, axis=0, tiled=False)
    gelu_full = in_order(second[:, : 8 * block], 8)
    out_rows = second[:, 8 * block :].reshape(16, cuts, 32, width)[:, :, :strip]
    out_rows = out_rows.transpose(0, 2, 1, 3).reshape(channels, cuts * width)[:, :model]
    out_rows = jnp.pad(out_rows, ((0, spare), (0, 0)))

    third = jnp.concatenate([third, fold_down(down_weight, 2 * units)], axis=0)
    third = lax.all_gather(third, plane, axis=0, tiled=False)
    down = unfold_down(third[:, 8 * block :], model).reshape(units, model)
    third = in_order(third[:, : 8 * block], 8)

    gain_one = input_full[:, channels].astype(f32)[None, :]
    gain_two = input_full[:, channels + 1].astype(f32)[None, :]
    def rms_unit(values):
        return lax.rsqrt(jnp.mean(values * values, axis=-1, keepdims=True) + epsilon)

    def norm_half(values):
        values = values.astype(f32)
        return (values * rms_unit(values) * gain_one).astype(bf16)

    own_head = (jnp.arange(width)[:, None] // head) == (jnp.arange(width)[None, :] // head)

    def spread_heads(part):
        return jnp.where(own_head, jnp.concatenate([part, part, part], axis=1)[:, :width], 0)

    own_tokens = flat.astype(f32)
    normed_own, normed_other = norm_half(tokens_own), norm_half(tokens_other)
    conv_in = joined(
        project_in(normed_own, input_full).astype(bf16),
        project_in(normed_other, input_full).astype(bf16),
    )
    by_chunk = (chunks, size, width)
    halo = hop(conv_in.reshape(by_chunk)[:, size - 8 :], plane, 1)
    rest = after(rest, halo)[:, :strip].reshape(channels, width)
    rest = jnp.pad(rest, ((0, spare), (0, 0)))
    w_in = spread_heads(rest[:, :head])
    w_rec = spread_heads(rest[:, head : 2 * head])
    rows_small = rest[:, 2 * head : 2 * head + 8].astype(f32).T
    decay_row = rows_small[7:8]
    params = jnp.concatenate(
        [
            rows_small[:7],
            -8.0 * jax.nn.softplus(decay_row),
            -8.0 * jax.nn.sigmoid(decay_row),
            jnp.zeros((7, width), f32),
        ],
        axis=0,
    )

    lens = jnp.stack([lengths, hop(lengths, "row", 1)], axis=0)
    starts = jnp.cumsum(lens, axis=2) - lens
    first_slot = jnp.arange(4) * (16 * size) + plane_at * size

    def position(slot):
        live = (lens > 0)[:, None, :, None, :] & (starts[:, None, :, None, :] <= slot[..., None])
        origin = jnp.max(jnp.where(live, starts[:, None, :, None, :], 0), axis=-1)
        return slot - origin

    slots = first_slot[None, :, None, None] + jnp.arange(size)[None, None, None, :]
    slots = jnp.broadcast_to(slots, (2, 4, row_count, size))
    here = position(slots)
    columns = [here != 0] + [here >= k for k in (1, 2, 3)]
    for k in (1, 2, 3):
        ahead = slots + k
        columns.append((position(ahead) >= k) & (ahead < 64 * size))
    columns.append(jnp.zeros_like(columns[0]))
    masks = jnp.stack(columns, axis=-1).astype(f32).reshape(total_tokens, 8)

    def turned(rim, shift):
        by_z = rim.reshape((2, 4, row_count) + rim.shape[1:])
        return jnp.roll(by_z, shift, axis=1).reshape(rim.shape)

    halo = jnp.where(plane_at == 0, turned(halo, 1), halo)
    wide = ((total_tokens, width), f32)
    narrow = ((total_tokens, width), bf16)
    paneled = ((width // 128, total_tokens, 128), f32)
    ends_shape = ((2, chunks, width), f32)
    extended = pltpu.VMEM((size + 8, width), f32)
    whole = pltpu.VMEM(*wide)
    folded = pltpu.VMEM(*paneled)
    conv_vals, factor, local_state, decay, ends = kernel_call(
        gates_kernel,
        60,
        [narrow, paneled, paneled, paneled, ends_shape],
        [extended, whole, whole, folded],
    )(conv_in, halo, masks, params, w_in, w_rec)


    def carried(pieces, backward):
        spot = plane_at.astype(jnp.int32).reshape(1)
        return pl.pallas_call(
            partial(carry_kernel, backward),
            cost_estimate=cost(1),
            out_shape=jax.ShapeDtypeStruct((chunks, 1, width), f32),
            in_specs=[pl.BlockSpec(memory_space=pltpu.SMEM), pl.BlockSpec(memory_space=pltpu.VMEM)],
            out_specs=pl.BlockSpec(memory_space=pltpu.VMEM),
        )(spot, pieces)

    pieces = gather_plane(ends)
    down_own, down_other = gather_team(after(upstream.astype(bf16), conv_in), pieces)
    entering = after(carried(pieces, False), down_own)
    gelu_own, gelu_other = project_in(normed_own, gelu_full), project_in(normed_other, gelu_full)
    half = total_tokens // 2

    def mix(which, gelu_pre):
        rows = pl.BlockSpec((half, width), lambda i: (0, 0))
        folds = pl.BlockSpec((width // 128, half, 128), lambda i: (0, which, 0))
        return pl.pallas_call(
            mix_kernel,
            cost_estimate=cost(5),
            out_shape=[
                jax.ShapeDtypeStruct((half, width), f32),
                jax.ShapeDtypeStruct((half, width), bf16),
                jax.ShapeDtypeStruct((half, model), bf16),
            ],
            grid=(1,),
            in_specs=[
                rows,
                folds,
                folds,
                pl.BlockSpec((chunks // 2, 1, width), lambda i: (which, 0, 0)),
                pl.BlockSpec((width, model), lambda i: (0, 0)),
            ],
            out_specs=[
                pl.BlockSpec((half, width), lambda i: (0, 0)),
                pl.BlockSpec((half, width), lambda i: (0, 0)),
                pl.BlockSpec((half, model), lambda i: (0, 0)),
            ],
            compiler_params=pltpu.CompilerParams(vmem_limit_bytes=vmem_limit),
        )(gelu_pre, local_state, decay, entering, out_rows)

    other_state, other_mixed, other_middle = mix(1, gelu_other)
    own_state, own_mixed, own_middle = mix(0, gelu_own)
    middle = own_tokens + reduce_team(other_middle, own_middle)[0]

    scale_two = rms_unit(middle)
    normed_two = (middle * scale_two * gain_two).astype(bf16)
    two_own, two_other = gather_team(normed_two)

    def feed(values, grad_inner):
        pre = project_in(values, third)
        act, slope = gelu_parts(pre[:, :units])
        up = pre[:, units:]
        grad = [(grad_inner * up * slope).astype(bf16), (grad_inner * act).astype(bf16)]
        return (act * up).astype(bf16), jnp.concatenate(grad, axis=1)

    inner_own, pre_own = feed(two_own, project_back(down_own, down))
    inner_other, pre_other = feed(two_other, project_back(down_other, down))
    terms_other = project_back(pre_other, third).astype(bf16)
    terms_own = project_back(pre_own, third).astype(bf16)
    grad_two, _ = reduce_team(terms_other, terms_own)
    def back_to_rows(grad):
        grad = grad.astype(bf16).reshape(8, block, -1)
        return lax.all_to_all(grad, team, 0, 0, tiled=True).astype(f32).transpose(1, 0, 2)

    def norm_back(values, scale, gain, grad):
        pulled = gain * grad
        mean = jnp.mean(pulled * values, axis=-1, keepdims=True)
        return scale * pulled - values * (scale * scale * scale * mean)

    def gain_grad(gain, pairs):
        total = sum(jnp.sum(weight.astype(f32) * grad, axis=1) for weight, grad in pairs)
        return total / gain.astype(f32)

    grad_middle = upstream + norm_back(middle, scale_two, gain_two, grad_two)
    branch_own, branch_other = gather_team(grad_middle.astype(bf16))
    share = 8 * block + units * model // (32 * units)
    grad_third = outer_folded(
        (inner_own, inner_other), (down_own, down_other), (16, share, 2 * units)
    )
    grad_third = add_outer(grad_third, (two_own, two_other), (pre_own, pre_other))
    grad_third = after(grad_third, grad_two)
    grad_third = lax.psum_scatter(
        grad_third.reshape(16 * share, 2 * units), plane, scatter_dimension=0, tiled=True
    )
    grad_down_weight = unfold_down(grad_third[8 * block :], model).astype(f32)

    grad_gelu, adjoint, reach, ends = kernel_call(
        unmix_kernel, 100, [narrow, paneled, paneled, ends_shape], [folded]
    )(
        project_back(branch_own, out_rows), project_back(branch_other, out_rows),
        gelu_own, gelu_other, own_state, other_state, factor,
    )
    normed = (normed_own, normed_other)
    cuts = 4
    grad_out_rows = outer_strips(
        (own_mixed, other_mixed),
        (branch_own, branch_other),
        strip,
        (16, 32 * cuts, model // cuts),
    )
    grad_gelu_rows = jnp.zeros((16, 8 * block, width), bf16)
    grad_gelu_rows = add_outer(grad_gelu_rows, normed, (grad_gelu,))
    arriving = after(carried(gather_plane(ends), True), grad_gelu_rows, grad_out_rows)
    grad_gelu_rows = lax.all_to_all(after(grad_gelu_rows, arriving), plane, 0, 0, tiled=True)
    grad_in, grad_rec, grad_conv, sums = kernel_call(
        ungate_kernel, 100, [narrow, narrow, narrow, ((8, width), f32)], [extended, whole, whole]
    )(
        adjoint, reach, arriving, own_state, other_state, entering, conv_vals, conv_in, halo, masks,
        params, w_in, w_rec,
    )
    ahead = hop(grad_conv.reshape(by_chunk)[:, :8], plane, -1)
    grad_out_rows = after(grad_out_rows, ahead, grad_gelu_rows)
    grad_out_rows = lax.all_to_all(grad_out_rows, plane, 0, 0, tiled=True)
    ahead = jnp.where(plane_at == 15, turned(ahead, -1), ahead)
    (grad_conv_in,) = kernel_call(unconvolve_kernel, 1, [narrow], [extended])(
        grad_conv, ahead, masks, params
    )

    def own_heads(grad):
        grad = jnp.where(own_head, grad, 0)[:channels]
        return grad[:, :head] + grad[:, head:channels]

    late_own, late_other = after(inner_own, grad_conv_in), after(inner_other, grad_conv_in)
    first_half = lax.select(row_at == 0, late_own, late_other)
    inner_rows = joined(first_half, lax.select(row_at == 0, late_other, late_own))
    result = project_in(inner_rows, down).astype(bf16)
    result = lax.psum_scatter(result, team, scatter_dimension=0, tiled=True)
    result = (middle + result.astype(f32)) * valid
    output = result.reshape(row_count, size, model).astype(bf16)
    grad_rest = jnp.concatenate(
        [
            own_heads(outer_sum(conv_vals, grad_in)),
            own_heads(outer_sum(conv_vals, grad_rec)),
            sums.T[:channels],
        ],
        axis=1,
    ).astype(bf16)
    grad_rest = grad_rest.reshape(16, strip, -1)
    grad_rest = jnp.pad(
        grad_rest, ((0, 0), (0, 32 - strip), (0, width - grad_rest.shape[2]))
    )
    grad_lead = jnp.pad(grad_rest, ((0, 0), (8 * block, 0), (0, 0)))
    grad_conv_in = after(grad_conv_in, grad_out_rows, grad_lead)
    grad_pair = jnp.concatenate([grad_conv_in, grad_gelu], axis=1)
    pair_weight = jnp.concatenate([input_full, gelu_full], axis=1)
    terms_other = project_back(grad_pair[half:], pair_weight).astype(bf16)
    grad_normed, upward = reduce_team(terms_other, project_back(grad_pair[:half], pair_weight).astype(bf16))
    grad_lead = add_outer(grad_lead, normed, (grad_conv_in,))
    grad_lead = lax.all_to_all(after(grad_lead, grad_out_rows), plane, 0, 0, tiled=True)
    cut = 8 * block
    grad_lead = total_of(after(grad_lead, upward))
    grad_rest = grad_lead[cut : cut + strip]
    grad_gelu_rows = total_of(after(grad_gelu_rows, upward)).astype(bf16)
    grad_out_weight = total_of(after(grad_out_rows, upward))
    grad_out_weight = grad_out_weight.reshape(cuts, 32, -1).transpose(1, 0, 2)
    grad_out_weight = grad_out_weight.reshape(32, model)[:strip]
    grad_gate_input = grad_rest[:, :head]
    grad_gate_recur = grad_rest[:, head : 2 * head]
    grad_small = grad_rest[:, 2 * head : 2 * head + 8]
    team_third = jnp.concatenate(
        [after(grad_third[:cut], upward), grad_lead[:cut].astype(bf16), grad_gelu_rows], axis=1
    )
    team_third = back_to_rows(team_third)
    grad_input_weight = team_third[:, :, 2 * units : 2 * units + channels].reshape(block, hidden)
    grad_gelu_weight = team_third[:, :, 2 * units + width :][:, :, :channels].reshape(block, hidden)
    grad_gate_weight = team_third[:, :, :units].reshape(block, inner)
    grad_up_weight = team_third[:, :, units : 2 * units].reshape(block, inner)

    grad_norm_two = gain_grad(
        norm_two, [(gate_weight, grad_gate_weight), (up_weight, grad_up_weight)]
    )
    grad_norm_one = gain_grad(
        norm_one, [(gelu_weight, grad_gelu_weight), (input_weight, grad_input_weight)]
    )
    own_scale = rms_unit(own_tokens)
    grad_tokens = grad_middle + norm_back(own_tokens, own_scale, gain_one, grad_normed)
    return (
        output,
        grad_tokens.reshape(row_count, size, model),
        grad_norm_one,
        grad_gelu_weight,
        grad_input_weight,
        grad_small[:, :4],
        grad_small[:, 4],
        grad_gate_input,
        grad_small[:, 5],
        grad_gate_recur,
        grad_small[:, 6],
        grad_small[:, 7],
        grad_out_weight,
        grad_norm_two,
        grad_gate_weight,
        grad_up_weight,
        grad_down_weight,
    )


def solution(mesh):
    grid = Mesh(mesh.devices.reshape(2, 4, 4, 4), everywhere)
    slots = P("row", ("z", "y", "x"), None)
    line = P(everywhere)
    sheet = P(everywhere, None)
    return jax.shard_map(
        body,
        mesh=grid,
        in_specs=(
            slots, P("row", None), line, sheet, sheet, sheet, line, sheet, line, sheet, line, line,
            sheet, line, sheet, sheet, sheet, slots,
        ),
        out_specs=(
            slots, slots, line, sheet, sheet, sheet, line, sheet, line, sheet, line, line, sheet,
            line, sheet, sheet, sheet,
        ),
        check_vma=False,
    )
```

```python
from functools import partial

import jax
import jax.numpy as jnp
from jax import lax
from jax.experimental import pallas as pl
from jax.experimental.pallas import tpu as pltpu
from jax.sharding import Mesh
from jax.sharding import PartitionSpec as P

epsilon = 1e-06
beta_floor = 0.001
bf16 = jnp.bfloat16
f32 = jnp.float32
everywhere = ("row", "z", "y", "x")
team = ("row", "z")
plane = ("y", "x")
vmem_limit = 32 * 1024 * 1024


def hop(block, axis, distance):
    count = lax.axis_size(axis)
    return lax.ppermute(block, axis, [(i, (i + distance) % count) for i in range(count)])


def gather_plane(piece):
    return lax.all_to_all(jnp.broadcast_to(piece, (16,) + piece.shape), plane, 0, 0, tiled=True)


def outer_kernel(packed, left_own, left_other, right_own, right_other, out):
    total = outer_sum(left_own[...], right_own[...]) + outer_sum(left_other[...], right_other[...])
    count, rows, columns = out.shape
    total = total.astype(bf16).reshape(count, rows, total.shape[1])
    out[:, :, : total.shape[2]] = total
    if total.shape[2] < columns:
        out[:, :, total.shape[2] :] = jnp.zeros((count, rows, columns - total.shape[2]), bf16)


def add_outer(packed, left, right):
    half, model = left[0].shape
    if len(right) == 1:
        right, starts = right * 2, (0, 1)
    else:
        starts = (0, 0)
    columns = right[0].shape[1]
    block = model // 128
    return pl.pallas_call(
        outer_kernel,
        cost_estimate=cost(model * columns / 350000),
        grid=(8,),
        in_specs=[pl.BlockSpec(memory_space=pl.ANY)]
        + [pl.BlockSpec((half, 16 * block), lambda s: (0, s))] * 2
        + [pl.BlockSpec((half, columns), partial(lambda at, s: (at, 0), at)) for at in starts],
        out_specs=pl.BlockSpec((16, block, packed.shape[2]), lambda s: (0, s, 0)),
        out_shape=jax.ShapeDtypeStruct(packed.shape, packed.dtype),
        input_output_aliases={0: 0},
        compiler_params=pltpu.CompilerParams(vmem_limit_bytes=vmem_limit),
    )(packed, *left, *right)


def strips_kernel(strip, packed, left_own, left_other, right_own, right_other, out, total):
    step = pl.program_id(0)

    @pl.when(step % 2 == 0)
    def compute():
        total[...] = outer_sum(left_own[...], right_own[...]) + outer_sum(
            left_other[...], right_other[...]
        )

    for part in range(2):

        @pl.when(step % 2 == part)
        def store(part=part):
            for place in range(out.shape[0]):
                start = place * strip + part * 16
                out[place] = total[start : start + 16, :].astype(bf16)


def add_strips(packed, left, right, strip, first):
    half, width = left[0].shape
    columns = right[0].shape[1] // 4
    row = first // 16

    def spot(step):
        lower, strip_at = step % 2, step // 2
        last = strip_at == 3
        return (0, jnp.where(last, row + 2, row + lower), jnp.where(last, lower, strip_at))

    return pl.pallas_call(
        partial(strips_kernel, strip),
        cost_estimate=cost(4),
        grid=(8,),
        in_specs=[pl.BlockSpec(memory_space=pl.ANY)]
        + [pl.BlockSpec((half, width), lambda s: (0, 0))] * 2
        + [pl.BlockSpec((half, columns), lambda s: (0, s // 2))] * 2,
        out_specs=pl.BlockSpec((packed.shape[0], 16, columns), spot),
        out_shape=jax.ShapeDtypeStruct(packed.shape, packed.dtype),
        input_output_aliases={0: 0},
        scratch_shapes=[pltpu.VMEM((width, columns), f32)],
        compiler_params=pltpu.CompilerParams(vmem_limit_bytes=vmem_limit),
    )(packed, *left, *right)


def folded_kernel(left_own, left_other, right_own, right_other, out):
    _, rows, columns = out.shape
    total = outer_sum(left_own[...], right_own[...]) + outer_sum(left_other[...], right_other[...])
    total = total.astype(bf16).reshape(out.shape[0], -1, total.shape[1])
    tall = total.shape[1]
    out[:, :tall, :] = total[:, :, :columns]
    over = total.shape[2] - columns
    for at in range(columns // over):
        part = total[:, at * (rows - tall) : (at + 1) * (rows - tall), columns:]
        out[:, tall:, at * over : (at + 1) * over] = part


def outer_folded(left, right, shape, first):
    places, rows, columns = shape
    tokens, units = left[0].shape
    model = right[0].shape[1]
    high = units * model // (places * columns)
    return pl.pallas_call(
        folded_kernel,
        cost_estimate=cost(5),
        grid=(2,),
        in_specs=[pl.BlockSpec((tokens, units // 2), lambda s: (0, s))] * 2
        + [pl.BlockSpec((tokens, model), lambda s: (0, 0))] * 2,
        out_specs=pl.BlockSpec((places // 2, high, columns), lambda s: (s, first // high, 0)),
        out_shape=jax.ShapeDtypeStruct(shape, bf16),
        compiler_params=pltpu.CompilerParams(vmem_limit_bytes=vmem_limit),
    )(*left, *right)


def total_of(pieces):
    return jnp.sum(pieces.astype(f32), axis=0)


def after(value, *others):
    return lax.optimization_barrier((value,) + others)[0]


def joined(*parts):
    return jnp.concatenate(parts, axis=0)


def gather_team(block, *stage):
    z_at = lax.axis_index("z")
    half = block.shape[0] // 2
    below, above = hop(block, "z", 1), hop(block, "z", -1)
    if stage:
        below, above = after(below, *stage), after(above, *stage)
    across = joined(hop(below[:half], "z", 1), hop(above[half:], "z", -1))
    own = jnp.zeros((4,) + block.shape, block.dtype)
    for offset, part in ((0, block), (1, above), (3, below), (2, across)):
        own = lax.dynamic_update_index_in_dim(own, part, (z_at + offset) % 4, 0)
    own = own.reshape(4 * block.shape[0], -1)
    return own, hop(own, "row", 1)


def reduce_team(other, own):
    z_at = lax.axis_index("z")
    other = hop(other, "row", 1).reshape(4, -1, other.shape[-1])
    own = own.reshape(other.shape)

    def block(offset):
        at = (z_at + offset) % 4
        parts = [lax.dynamic_index_in_dim(whole, at, 0, keepdims=False) for whole in (own, other)]
        return parts[0].astype(f32) + parts[1].astype(f32)

    sums = {offset: block(offset) for offset in (2, 1, 3, 0)}
    half = own.shape[1] // 2
    from_below = hop(sums[2][:half].astype(bf16), "z", 1)
    from_above = hop(sums[2][half:].astype(bf16), "z", -1)
    up = joined(sums[1][:half] + from_below.astype(f32), sums[1][half:]).astype(bf16)
    down = joined(sums[3][:half], sums[3][half:] + from_above.astype(f32)).astype(bf16)
    up, down = hop(up, "z", 1), hop(down, "z", -1)
    return sums[0] + up.astype(f32) + down.astype(f32), up


def project_in(left, weight):
    return jnp.dot(left, weight, preferred_element_type=f32)


def project_back(grad, weight):
    return lax.dot_general(grad, weight, (((1,), (1,)), ((), ())), preferred_element_type=f32)


def outer_sum(left, grad):
    return lax.dot_general(left, grad, (((0,), (0,)), ((), ())), preferred_element_type=f32)


def fold_down(rows, width):
    over = rows.shape[-1] - width
    group = rows.shape[-2] * over // width
    tail = [rows[..., at : at + group, width:] for at in range(0, rows.shape[-2], group)]
    return jnp.concatenate([rows[..., :width], jnp.concatenate(tail, axis=-1)], axis=-2)


def unfold_down(rows, model):
    width = rows.shape[-1]
    over = model - width
    count = rows.shape[-2] * width // model
    tail = rows[..., count:, :]
    tail = [tail[..., at : at + over] for at in range(0, width, over)]
    return jnp.concatenate([rows[..., :count, :], jnp.concatenate(tail, axis=-2)], axis=-1)


def cost(micros):
    return pl.CostEstimate(flops=0, bytes_accessed=int(micros * 3.0e6), transcendentals=0)


def kernel_call(kernel, micros, outs, scratch=()):
    return pl.pallas_call(
        kernel,
        cost_estimate=cost(micros),
        out_shape=[jax.ShapeDtypeStruct(shape, dtype) for shape, dtype in outs],
        scratch_shapes=list(scratch),
        compiler_params=pltpu.CompilerParams(vmem_limit_bytes=vmem_limit),
    )


def chunk_rows(chunk, size):
    return pl.ds(pl.multiple_of(chunk * size, size), size)


def panels(ref, rows):
    return jnp.concatenate([ref[at, rows, :] for at in range(ref.shape[0])], axis=1)


def set_panels(ref, rows, value):
    for at in range(ref.shape[0]):
        ref[at, rows, :] = value[:, at * 128 : (at + 1) * 128]


def gate_parts(raw_in, raw_rec, params):
    gate_in = jax.nn.sigmoid(raw_in + params[5:6, :])
    gate_rec = jax.nn.sigmoid(raw_rec + params[6:7, :])
    log_decay = gate_rec * params[7:8, :]
    base = jnp.exp(log_decay)
    return gate_in, gate_rec, base, -jnp.tanh(log_decay) * (base * base + 1.0)


def gates_kernel(
    cin, halo, masks, params, w_in, w_rec,
    conv, factor, state, decay, ends, ext, raw_in, raw_rec, drive,
):
    tokens, width = cin.shape
    count = halo.shape[0]
    size = tokens // count
    tiles = width // 128

    def convolve(chunk, carry):
        rows = chunk_rows(chunk, size)
        ext[0:8, :] = halo[chunk].astype(f32)
        ext[8 : 8 + size, :] = cin[rows, :].astype(f32)
        total = params[4:5, :] + params[0:1, :] * ext[8 : 8 + size, :]
        for k in (1, 2, 3):
            total = total + params[k : k + 1, :] * ext[8 - k : 8 - k + size, :] * masks[rows, k : k + 1]
        conv[rows, :] = total.astype(bf16)
        return carry

    lax.fori_loop(0, count, convolve, 0)
    raw_in[...] = jnp.dot(conv[...], w_in[...], preferred_element_type=f32)
    raw_rec[...] = jnp.dot(conv[...], w_rec[...], preferred_element_type=f32)

    def gate(chunk, carry):
        rows = chunk_rows(chunk, size)
        gate_in, _, base, kept = gate_parts(raw_in[rows, :], raw_rec[rows, :], params)
        scale = jnp.sqrt(jnp.maximum(kept, beta_floor))
        set_panels(factor, rows, base * masks[rows, 0:1])
        set_panels(drive, rows, scale * gate_in * conv[rows, :].astype(f32))
        return carry

    lax.fori_loop(0, count, gate, 0)

    def scan(slot, carry):
        at = pl.ds(slot, count, stride=size)
        after = []
        for tile, (held, gone) in enumerate(carry):
            step = factor[tile, at, :]
            held = step * held + drive[tile, at, :]
            gone = step * gone
            state[tile, at, :] = held
            decay[tile, at, :] = gone
            after.append((held, gone))
        return tuple(after)

    first = pl.ds(0, count, stride=size)
    start = []
    for tile in range(tiles):
        zero = drive[tile, first, :] * 0.0
        start.append((zero, zero + 1.0))
    last = lax.fori_loop(0, size, scan, tuple(start))
    for tile, (held, gone) in enumerate(last):
        ends[0, :, tile * 128 : (tile + 1) * 128] = gone
        ends[1, :, tile * 128 : (tile + 1) * 128] = held


def carry_kernel(backward, spot, pieces, entering):
    mine = spot[0]
    places = pieces.shape[0]
    order = range(places - 1, -1, -1) if backward else range(places)
    decay, state = pieces[order[0], 0], pieces[order[0], 1]
    here = jnp.where(mine == order[0], 1.0, 0.0)
    own_decay, own_state = jnp.zeros_like(decay) + here, jnp.zeros_like(state)
    for place_at in order[1:]:
        here = jnp.where(mine == place_at, 1.0, 0.0)
        own_decay = own_decay + decay * here
        own_state = own_state + state * here
        step = pieces[place_at, 0]
        state = step * state + pieces[place_at, 1]
        decay = step * decay
    for row in range(2):
        held = jnp.zeros((2, decay.shape[1]), f32)
        for z in range(3, -1, -1) if backward else range(4):
            start = row * 8 + z * 2
            part = slice(start, start + 2)
            inside = own_decay[part] * held + own_state[part]
            held = decay[part] * held + state[part]
            for line in range(2):
                entering[start + line] = inside[line : line + 1]


def gelu_parts(value):
    slope = 0.7978845608028654
    square = value * value
    inner = jnp.tanh(slope * (value + 0.044715 * value * square))
    half = 0.5 * (1.0 + inner)
    act = value * half
    grad = half + 0.5 * value * (1.0 - inner * inner) * slope * (1.0 + 3 * 0.044715 * square)
    return act, grad


def mix_kernel(pre, state, decay, entering, out_rows, rec_state, mixed, partial_sum):
    count = entering.shape[0]
    tokens, width = rec_state.shape
    size = tokens // count

    def mix(chunk, carry):
        rows = chunk_rows(chunk, size)
        full = panels(state, rows) + panels(decay, rows) * entering[chunk]
        rec_state[rows, :] = full
        mixed[rows, :] = (gelu_parts(pre[rows, :])[0] * full).astype(bf16)
        return carry

    lax.fori_loop(0, count, mix, 0)
    partial_sum[...] = jnp.dot(
        mixed[...], out_rows[...], preferred_element_type=f32
    ).astype(bf16)


def unmix_kernel(
    mixed_own, mixed_other, pre_own, pre_other, rec_own, rec_other, factor,
    grad_gelu, adjoint, reach, ends, grad_state,
):
    half, width = rec_own.shape
    count = ends.shape[1]
    size = 2 * half // count
    tiles = width // 128

    def unmix(start, grad_mixed, pre, rec_state, chunk, carry):
        rows = chunk_rows(chunk, size)
        out = chunk_rows(chunk + start, size)
        act, slope = gelu_parts(pre[rows, :])
        grad = grad_mixed[rows, :]
        grad_gelu[out, :] = (grad * rec_state[rows, :] * slope).astype(bf16)
        set_panels(grad_state, out, grad * act)
        return carry

    lax.fori_loop(0, count // 2, partial(unmix, 0, mixed_own, pre_own, rec_own), 0)
    lax.fori_loop(0, count // 2, partial(unmix, count // 2, mixed_other, pre_other, rec_other), 0)

    def scan(step, carry):
        at = pl.ds(size - 1 - step, count, stride=size)
        after = []
        for tile, (held, gone, ahead) in enumerate(carry):
            held = ahead * held + grad_state[tile, at, :]
            gone = ahead * gone
            adjoint[tile, at, :] = held
            reach[tile, at, :] = gone
            after.append((held, gone, factor[tile, at, :]))
        return tuple(after)

    first = pl.ds(0, count, stride=size)
    start = []
    for tile in range(tiles):
        zero = factor[tile, first, :] * 0.0
        start.append((zero, zero + 1.0, zero + 1.0))
    last = lax.fori_loop(0, size, scan, tuple(start))
    for tile, (held, gone, ahead) in enumerate(last):
        ends[0, :, tile * 128 : (tile + 1) * 128] = ahead * gone
        ends[1, :, tile * 128 : (tile + 1) * 128] = ahead * held


def ungate_kernel(
    adjoint, reach, arriving, rec_own, rec_other, entering, conv, cin, halo, masks, params, w_in,
    w_rec, grad_in, grad_rec, grad_conv, sums, ext, direct, raw_rec,
):
    tokens, width = cin.shape
    count = halo.shape[0]
    size = tokens // count
    zero = params[0:8, :] * 0.0

    def fold(value):
        total = value[0:8]
        for at in range(8, size, 8):
            total = total + value[at : at + 8]
        return total

    def ungate(start, rec_state, chunk, carry):
        sum_in, sum_rec, sum_decay = carry
        ext[8 : 8 + size, :] = rec_state[chunk_rows(chunk, size), :]
        chunk = chunk + start
        rows = chunk_rows(chunk, size)
        ext[7:8, :] = entering[chunk]
        full = panels(adjoint, rows) + panels(reach, rows) * arriving[chunk]
        gate_in, gate_rec, base, square = gate_parts(direct[rows, :], raw_rec[rows, :], params)
        scale = jnp.sqrt(jnp.maximum(square, beta_floor))
        values = conv[rows, :].astype(f32)
        scaled = full * scale
        drive = full * gate_in * values
        slope = jnp.where(square > beta_floor, (1.0 - square) / scale, 0.0)
        grad_log = full * base * masks[rows, 0:1] * ext[7 : 7 + size, :] - slope * drive
        raw_in = scale * drive * (1.0 - gate_in)
        pulled = grad_log * gate_rec
        rec = pulled * params[7:8, :] * (1.0 - gate_rec)
        grad_in[rows, :] = raw_in.astype(bf16)
        grad_rec[rows, :] = rec.astype(bf16)
        direct[rows, :] = scaled * gate_in
        return (sum_in + fold(raw_in), sum_rec + fold(rec), sum_decay + fold(pulled))

    direct[...] = jnp.dot(conv[...], w_in[...], preferred_element_type=f32)
    raw_rec[...] = jnp.dot(conv[...], w_rec[...], preferred_element_type=f32)
    half = count // 2
    totals = lax.fori_loop(0, half, partial(ungate, 0, rec_own), (zero, zero, zero))
    sum_in, sum_rec, sum_decay = lax.fori_loop(0, half, partial(ungate, half, rec_other), totals)
    back = (((1,), (1,)), ((), ()))
    direct[...] += lax.dot_general(grad_in[...], w_in[...], back, preferred_element_type=f32)
    direct[...] += lax.dot_general(grad_rec[...], w_rec[...], back, preferred_element_type=f32)

    def taps(chunk, carry):
        sum_bias, sum_taps = carry
        rows = chunk_rows(chunk, size)
        grad = direct[rows, :].astype(bf16)
        grad_conv[rows, :] = grad
        grad = grad.astype(f32)
        ext[0:8, :] = halo[chunk].astype(f32)
        ext[8 : 8 + size, :] = cin[rows, :].astype(f32)
        new_taps = [sum_taps[0] + fold(grad * ext[8 : 8 + size, :])]
        for k in (1, 2, 3):
            moved = ext[8 - k : 8 - k + size, :] * masks[rows, k : k + 1]
            new_taps.append(sum_taps[k] + fold(grad * moved))
        return (sum_bias + fold(grad), tuple(new_taps))

    sum_bias, sum_taps = lax.fori_loop(0, count, taps, (zero, (zero,) * 4))
    rows_out = sum_taps + (sum_bias, sum_in, sum_rec, sum_decay * params[8:9, :])
    for index, total in enumerate(rows_out):
        sums[index : index + 1, :] = jnp.sum(total, axis=0, keepdims=True)


def unconvolve_kernel(grad_conv, halo, masks, params, out, ext):
    tokens, width = grad_conv.shape
    count = halo.shape[0]
    size = tokens // count

    def spread(chunk, carry):
        rows = chunk_rows(chunk, size)
        ext[0:size, :] = grad_conv[rows, :].astype(f32)
        ext[size : size + 8, :] = halo[chunk].astype(f32)
        total = params[0:1, :] * ext[0:size, :]
        for k in (1, 2, 3):
            total = total + params[k : k + 1, :] * ext[k : k + size, :] * masks[rows, 3 + k : 4 + k]
        out[rows, :] = total.astype(bf16)
        return carry

    lax.fori_loop(0, count, spread, 0)


def body(
    tokens,
    lengths,
    norm_one,
    gelu_weight,
    input_weight,
    conv_weight,
    conv_bias,
    gate_input,
    bias_input,
    gate_recur,
    bias_recur,
    decay_param,
    out_weight,
    norm_two,
    gate_weight,
    up_weight,
    down_weight,
    cotangent,
):
    row_count, size, model = tokens.shape
    local = row_count * size
    block, hidden = gelu_weight.shape
    inner = gate_weight.shape[1]
    head = gate_input.shape[1]
    channels, units = hidden // 8, inner // 8
    strip = gate_input.shape[0]
    width = -(-channels // 128) * 128
    spare = width - channels
    row_at, z_at, y_at, x_at = (lax.axis_index(name) for name in everywhere)
    plane_at = y_at * 4 + x_at
    chunks = 16
    total_tokens = chunks * size
    flat = tokens.reshape(local, model)

    row_total = jnp.sum(lengths, axis=1)
    own_slots = (z_at * 16 + plane_at) * size + jnp.arange(size)
    valid = (own_slots[None, :] < row_total[:, None]).astype(f32).reshape(local, 1)
    upstream = cotangent.reshape(local, model).astype(f32) * valid

    def halves(whole):
        whole = whole.reshape(2, 4 * local, -1)
        return [
            lax.dynamic_index_in_dim(whole, row_at ^ other, 0, keepdims=False) for other in (0, 1)
        ]

    tokens_own, tokens_other = halves(lax.all_gather(flat, team, axis=0, tiled=True))

    gains = jnp.stack([norm_one, norm_two], axis=1)
    gains = jnp.broadcast_to(
        jnp.pad(gains, ((0, 0), (0, spare - 2)))[:, None, :], (block, 8, spare)
    )
    third = jnp.concatenate(
        [
            gelu_weight.reshape(block, 8, channels),
            jnp.zeros_like(gains),
            gate_weight.reshape(block, 8, units),
            up_weight.reshape(block, 8, units),
        ],
        axis=2,
    ).transpose(1, 0, 2)
    lead = jnp.concatenate([input_weight.reshape(block, 8, channels), gains], axis=2)
    lead = lead.transpose(1, 0, 2)[:, None]
    lead = jnp.broadcast_to(lead, (8, 16, block, width)).reshape(model, width)
    input_full = lax.all_to_all(lead, everywhere, 0, 0, tiled=True)
    third = lax.all_to_all(after(third, input_full), team, 0, 0, tiled=True).reshape(8 * block, -1)
    first, third = third[:, :width], third[:, width:]
    small = jnp.stack([conv_bias, bias_input, bias_recur, decay_param], axis=1)
    rest = jnp.concatenate([gate_input, gate_recur, conv_weight, small], axis=1)
    rest = jnp.pad(rest, ((0, 32 - strip), (0, width - rest.shape[1])))
    rest = gather_plane(after(rest, first))

    def in_order(rows, count):
        rows = rows.reshape(16, count, block, rows.shape[-1])
        return rows.transpose(1, 0, 2, 3).reshape(count * 16 * block, rows.shape[-1])

    cuts = -(-model // width)
    out_pack = jnp.pad(out_weight, ((0, 32 - strip), (0, cuts * width - model)))
    out_pack = out_pack.reshape(32, cuts, width).transpose(1, 0, 2).reshape(cuts * 32, width)
    second = jnp.concatenate([first, out_pack], axis=0)
    second = lax.all_gather(second, plane, axis=0, tiled=False)
    gelu_full = in_order(second[:, : 8 * block], 8)
    out_rows = second[:, 8 * block :].reshape(16, cuts, 32, width)[:, :, :strip]
    out_rows = out_rows.transpose(0, 2, 1, 3).reshape(channels, cuts * width)[:, :model]
    out_rows = jnp.pad(out_rows, ((0, spare), (0, 0)))

    third = jnp.concatenate([third, fold_down(down_weight, 2 * units)], axis=0)
    third = lax.all_gather(third, plane, axis=0, tiled=False)
    down = unfold_down(third[:, 8 * block :], model).reshape(units, model)
    third = in_order(third[:, : 8 * block], 8)

    gain_one = input_full[:, channels].astype(f32)[None, :]
    gain_two = input_full[:, channels + 1].astype(f32)[None, :]
    def rms_unit(values):
        return lax.rsqrt(jnp.mean(values * values, axis=-1, keepdims=True) + epsilon)

    def norm_half(values):
        values = values.astype(f32)
        return (values * rms_unit(values) * gain_one).astype(bf16)

    own_head = (jnp.arange(width)[:, None] // head) == (jnp.arange(width)[None, :] // head)

    def spread_heads(part):
        return jnp.where(own_head, jnp.concatenate([part, part, part], axis=1)[:, :width], 0)

    own_tokens = flat.astype(f32)
    normed_own, normed_other = norm_half(tokens_own), norm_half(tokens_other)
    conv_in = joined(
        project_in(normed_own, input_full).astype(bf16),
        project_in(normed_other, input_full).astype(bf16),
    )
    by_chunk = (chunks, size, width)
    halo = hop(conv_in.reshape(by_chunk)[:, size - 8 :], plane, 1)
    rest = after(rest, halo)[:, :strip].reshape(channels, width)
    rest = jnp.pad(rest, ((0, spare), (0, 0)))
    w_in = spread_heads(rest[:, :head])
    w_rec = spread_heads(rest[:, head : 2 * head])
    rows_small = rest[:, 2 * head : 2 * head + 8].astype(f32).T
    decay_row = rows_small[7:8]
    params = jnp.concatenate(
        [
            rows_small[:7],
            -8.0 * jax.nn.softplus(decay_row),
            -8.0 * jax.nn.sigmoid(decay_row),
            jnp.zeros((7, width), f32),
        ],
        axis=0,
    )

    lens = jnp.stack([lengths, hop(lengths, "row", 1)], axis=0)
    starts = jnp.cumsum(lens, axis=2) - lens
    first_slot = jnp.arange(4) * (16 * size) + plane_at * size

    def position(slot):
        live = (lens > 0)[:, None, :, None, :] & (starts[:, None, :, None, :] <= slot[..., None])
        origin = jnp.max(jnp.where(live, starts[:, None, :, None, :], 0), axis=-1)
        return slot - origin

    slots = first_slot[None, :, None, None] + jnp.arange(size)[None, None, None, :]
    slots = jnp.broadcast_to(slots, (2, 4, row_count, size))
    here = position(slots)
    columns = [here != 0] + [here >= k for k in (1, 2, 3)]
    for k in (1, 2, 3):
        ahead = slots + k
        columns.append((position(ahead) >= k) & (ahead < 64 * size))
    columns.append(jnp.zeros_like(columns[0]))
    masks = jnp.stack(columns, axis=-1).astype(f32).reshape(total_tokens, 8)

    def turned(rim, shift):
        by_z = rim.reshape((2, 4, row_count) + rim.shape[1:])
        return jnp.roll(by_z, shift, axis=1).reshape(rim.shape)

    halo = jnp.where(plane_at == 0, turned(halo, 1), halo)
    wide = ((total_tokens, width), f32)
    narrow = ((total_tokens, width), bf16)
    paneled = ((width // 128, total_tokens, 128), f32)
    ends_shape = ((2, chunks, width), f32)
    extended = pltpu.VMEM((size + 8, width), f32)
    whole = pltpu.VMEM(*wide)
    folded = pltpu.VMEM(*paneled)
    conv_vals, factor, local_state, decay, ends = kernel_call(
        gates_kernel,
        60,
        [narrow, paneled, paneled, paneled, ends_shape],
        [extended, whole, whole, folded],
    )(conv_in, halo, masks, params, w_in, w_rec)


    def carried(pieces, backward):
        spot = plane_at.astype(jnp.int32).reshape(1)
        return pl.pallas_call(
            partial(carry_kernel, backward),
            cost_estimate=cost(1),
            out_shape=jax.ShapeDtypeStruct((chunks, 1, width), f32),
            in_specs=[pl.BlockSpec(memory_space=pltpu.SMEM), pl.BlockSpec(memory_space=pltpu.VMEM)],
            out_specs=pl.BlockSpec(memory_space=pltpu.VMEM),
        )(spot, pieces)

    pieces = gather_plane(ends)
    down_own, down_other = gather_team(after(upstream.astype(bf16), conv_in), pieces)
    entering = after(carried(pieces, False), down_own)
    gelu_own, gelu_other = project_in(normed_own, gelu_full), project_in(normed_other, gelu_full)
    half = total_tokens // 2

    def mix(which, gelu_pre):
        rows = pl.BlockSpec((half, width), lambda i: (0, 0))
        folds = pl.BlockSpec((width // 128, half, 128), lambda i: (0, which, 0))
        return pl.pallas_call(
            mix_kernel,
            cost_estimate=cost(5),
            out_shape=[
                jax.ShapeDtypeStruct((half, width), f32),
                jax.ShapeDtypeStruct((half, width), bf16),
                jax.ShapeDtypeStruct((half, model), bf16),
            ],
            grid=(1,),
            in_specs=[
                rows,
                folds,
                folds,
                pl.BlockSpec((chunks // 2, 1, width), lambda i: (which, 0, 0)),
                pl.BlockSpec((width, model), lambda i: (0, 0)),
            ],
            out_specs=[
                pl.BlockSpec((half, width), lambda i: (0, 0)),
                pl.BlockSpec((half, width), lambda i: (0, 0)),
                pl.BlockSpec((half, model), lambda i: (0, 0)),
            ],
            compiler_params=pltpu.CompilerParams(vmem_limit_bytes=vmem_limit),
        )(gelu_pre, local_state, decay, entering, out_rows)

    other_state, other_mixed, other_middle = mix(1, gelu_other)
    own_state, own_mixed, own_middle = mix(0, gelu_own)
    middle = own_tokens + reduce_team(other_middle, own_middle)[0]

    scale_two = rms_unit(middle)
    normed_two = (middle * scale_two * gain_two).astype(bf16)
    two_own, two_other = gather_team(normed_two)

    def feed(values, grad_inner):
        pre = project_in(values, third)
        act, slope = gelu_parts(pre[:, :units])
        up = pre[:, units:]
        grad = [(grad_inner * up * slope).astype(bf16), (grad_inner * act).astype(bf16)]
        return (act * up).astype(bf16), jnp.concatenate(grad, axis=1)

    inner_own, pre_own = feed(two_own, project_back(down_own, down))
    inner_other, pre_other = feed(two_other, project_back(down_other, down))
    terms_other = project_back(pre_other, third).astype(bf16)
    terms_own = project_back(pre_own, third).astype(bf16)
    grad_two, _ = reduce_team(terms_other, terms_own)
    def back_to_rows(grad):
        grad = grad.astype(bf16).reshape(8, block, -1)
        return lax.all_to_all(grad, team, 0, 0, tiled=True).astype(f32).transpose(1, 0, 2)

    def norm_back(values, scale, gain, grad):
        pulled = gain * grad
        mean = jnp.mean(pulled * values, axis=-1, keepdims=True)
        return scale * pulled - values * (scale * scale * scale * mean)

    def gain_grad(gain, pairs):
        total = sum(jnp.sum(weight.astype(f32) * grad, axis=1) for weight, grad in pairs)
        return total / gain.astype(f32)

    grad_middle = upstream + norm_back(middle, scale_two, gain_two, grad_two)
    fold = 8 * block
    tail = fold + units * model // (32 * units)
    share = tail + 48
    packed_down = outer_folded(
        (inner_own, inner_other), (down_own, down_other), (16, share, 2 * units), fold
    )
    grad_third = add_outer(packed_down, (two_own, two_other), (pre_own, pre_other))
    branch_own, branch_other = gather_team(
        after(grad_middle.astype(bf16), packed_down), grad_third
    )
    grad_third = add_strips(
        grad_third, (own_mixed, other_mixed), (branch_own, branch_other), strip, tail
    )
    grad_third = lax.psum_scatter(
        grad_third.reshape(16 * share, 2 * units), plane, scatter_dimension=0, tiled=True
    )
    grad_gelu, adjoint, reach, ends = kernel_call(
        unmix_kernel, 100, [narrow, paneled, paneled, ends_shape], [folded]
    )(
        project_back(branch_own, out_rows), project_back(branch_other, out_rows),
        gelu_own, gelu_other, own_state, other_state, factor,
    )
    normed = (normed_own, normed_other)
    grad_gelu_rows = jnp.zeros((16, 8 * block, width), bf16)
    grad_gelu_rows = add_outer(grad_gelu_rows, normed, (grad_gelu,))
    result_own = project_in(after(inner_own, ends), down).astype(bf16)
    result_other = project_in(after(inner_other, ends), down).astype(bf16)
    arriving = after(
        carried(gather_plane(ends), True), grad_gelu_rows, result_own, result_other
    )
    grad_gelu_rows = lax.all_to_all(after(grad_gelu_rows, arriving), plane, 0, 0, tiled=True)
    grad_in, grad_rec, grad_conv, sums = kernel_call(
        ungate_kernel, 100, [narrow, narrow, narrow, ((8, width), f32)], [extended, whole, whole]
    )(
        adjoint, reach, arriving, own_state, other_state, entering, conv_vals, conv_in, halo, masks,
        params, w_in, w_rec,
    )
    ahead = hop(grad_conv.reshape(by_chunk)[:, :8], plane, -1)
    ahead = after(ahead, grad_gelu_rows)
    ahead = jnp.where(plane_at == 15, turned(ahead, -1), ahead)
    (grad_conv_in,) = kernel_call(unconvolve_kernel, 1, [narrow], [extended])(
        grad_conv, ahead, masks, params
    )

    def own_heads(grad):
        grad = jnp.where(own_head, grad, 0)[:channels]
        return grad[:, :head] + grad[:, head:channels]

    grad_rest = jnp.concatenate(
        [
            own_heads(outer_sum(conv_vals, grad_in)),
            own_heads(outer_sum(conv_vals, grad_rec)),
            sums.T[:channels],
        ],
        axis=1,
    ).astype(bf16)
    grad_rest = grad_rest.reshape(16, strip, -1)
    grad_rest = jnp.pad(
        grad_rest, ((0, 0), (0, 32 - strip), (0, width - grad_rest.shape[2]))
    )
    grad_lead = jnp.pad(grad_rest, ((0, 0), (8 * block, 0), (0, 0)))
    grad_conv_in = after(grad_conv_in, grad_lead)
    grad_pair = jnp.concatenate([grad_conv_in, grad_gelu], axis=1)
    pair_weight = jnp.concatenate([input_full, gelu_full], axis=1)
    terms_other = project_back(grad_pair[half:], pair_weight).astype(bf16)
    terms_own = project_back(grad_pair[:half], pair_weight).astype(bf16)
    grad_normed, upward = reduce_team(
        jnp.concatenate([terms_other, result_other], axis=1),
        jnp.concatenate([terms_own, result_own], axis=1),
    )
    result = (middle + grad_normed[:, model:]) * valid
    output = result.reshape(row_count, size, model).astype(bf16)
    grad_normed = grad_normed[:, :model]
    grad_lead = add_outer(grad_lead, normed, (grad_conv_in,))
    grad_lead = lax.all_to_all(grad_lead, plane, 0, 0, tiled=True)
    cut = 8 * block
    grad_lead = total_of(after(grad_lead, upward))
    grad_rest = grad_lead[cut : cut + strip]
    grad_gelu_rows = total_of(after(grad_gelu_rows, upward)).astype(bf16)
    grad_gate_input = grad_rest[:, :head]
    grad_gate_recur = grad_rest[:, head : 2 * head]
    grad_small = grad_rest[:, 2 * head : 2 * head + 8]
    grad_third = after(grad_third, upward)
    grad_down_weight = unfold_down(grad_third[fold:tail], model).astype(f32)
    last = grad_third[tail + 32 :, : model // 2]
    last = joined(last[:, : model // 4], last[:, model // 4 :])
    grad_out_weight = jnp.concatenate(
        [grad_third[tail : tail + strip], last[:strip]], axis=1
    ).astype(f32)
    team_third = jnp.concatenate(
        [grad_third[:cut], grad_lead[:cut].astype(bf16), grad_gelu_rows], axis=1
    )
    team_third = back_to_rows(team_third)
    grad_input_weight = team_third[:, :, 2 * units : 2 * units + channels].reshape(block, hidden)
    grad_gelu_weight = team_third[:, :, 2 * units + width :][:, :, :channels].reshape(block, hidden)
    grad_gate_weight = team_third[:, :, :units].reshape(block, inner)
    grad_up_weight = team_third[:, :, units : 2 * units].reshape(block, inner)

    grad_norm_two = gain_grad(
        norm_two, [(gate_weight, grad_gate_weight), (up_weight, grad_up_weight)]
    )
    grad_norm_one = gain_grad(
        norm_one, [(gelu_weight, grad_gelu_weight), (input_weight, grad_input_weight)]
    )
    own_scale = rms_unit(own_tokens)
    grad_tokens = grad_middle + norm_back(own_tokens, own_scale, gain_one, grad_normed)
    return (
        output,
        grad_tokens.reshape(row_count, size, model),
        grad_norm_one,
        grad_gelu_weight,
        grad_input_weight,
        grad_small[:, :4],
        grad_small[:, 4],
        grad_gate_input,
        grad_small[:, 5],
        grad_gate_recur,
        grad_small[:, 6],
        grad_small[:, 7],
        grad_out_weight,
        grad_norm_two,
        grad_gate_weight,
        grad_up_weight,
        grad_down_weight,
    )


def solution(mesh):
    grid = Mesh(mesh.devices.reshape(2, 4, 4, 4), everywhere)
    slots = P("row", ("z", "y", "x"), None)
    line = P(everywhere)
    sheet = P(everywhere, None)
    return jax.shard_map(
        body,
        mesh=grid,
        in_specs=(
            slots, P("row", None), line, sheet, sheet, sheet, line, sheet, line, sheet, line, line,
            sheet, line, sheet, sheet, sheet, slots,
        ),
        out_specs=(
            slots, slots, line, sheet, sheet, sheet, line, sheet, line, sheet, line, line, sheet,
            line, sheet, sheet, sheet,
        ),
        check_vma=False,
    )
```

```python
from functools import partial

import jax
import jax.numpy as jnp
from jax import lax
from jax.experimental import pallas as pl
from jax.experimental.pallas import tpu as pltpu
from jax.sharding import Mesh
from jax.sharding import PartitionSpec as P

epsilon = 1e-06
beta_floor = 0.001
bf16 = jnp.bfloat16
f32 = jnp.float32
everywhere = ("row", "z", "y", "x")
team = ("row", "z")
plane = ("y", "x")
vmem_limit = 32 * 1024 * 1024


def hop(block, axis, distance):
    count = lax.axis_size(axis)
    return lax.ppermute(block, axis, [(i, (i + distance) % count) for i in range(count)])


def gather_plane(piece):
    return lax.all_to_all(jnp.broadcast_to(piece, (16,) + piece.shape), plane, 0, 0, tiled=True)


def outer_kernel(packed, left_own, left_other, right_own, right_other, out):
    total = outer_sum(left_own[...], right_own[...]) + outer_sum(left_other[...], right_other[...])
    count, rows, columns = out.shape
    total = total.astype(bf16).reshape(count, rows, total.shape[1])
    out[:, :, : total.shape[2]] = total
    if total.shape[2] < columns:
        out[:, :, total.shape[2] :] = jnp.zeros((count, rows, columns - total.shape[2]), bf16)


def add_outer(packed, left, right):
    half, model = left[0].shape
    if len(right) == 1:
        right, starts = right * 2, (0, 1)
    else:
        starts = (0, 0)
    columns = right[0].shape[1]
    block = model // 128
    return pl.pallas_call(
        outer_kernel,
        cost_estimate=cost(model * columns / 350000),
        grid=(8,),
        in_specs=[pl.BlockSpec(memory_space=pl.ANY)]
        + [pl.BlockSpec((half, 16 * block), lambda s: (0, s))] * 2
        + [pl.BlockSpec((half, columns), partial(lambda at, s: (at, 0), at)) for at in starts],
        out_specs=pl.BlockSpec((16, block, packed.shape[2]), lambda s: (0, s, 0)),
        out_shape=jax.ShapeDtypeStruct(packed.shape, packed.dtype),
        input_output_aliases={0: 0},
        compiler_params=pltpu.CompilerParams(vmem_limit_bytes=vmem_limit),
    )(packed, *left, *right)


def strips_kernel(strip, packed, left_own, left_other, right_own, right_other, out, total):
    step = pl.program_id(0)

    @pl.when(step % 2 == 0)
    def compute():
        total[...] = outer_sum(left_own[...], right_own[...]) + outer_sum(
            left_other[...], right_other[...]
        )

    for part in range(2):

        @pl.when(step % 2 == part)
        def store(part=part):
            for place in range(out.shape[0]):
                start = place * strip + part * 16
                out[place] = total[start : start + 16, :].astype(bf16)


def add_strips(packed, left, right, strip, first):
    half, width = left[0].shape
    columns = right[0].shape[1] // 4
    row = first // 16

    def spot(step):
        lower, strip_at = step % 2, step // 2
        last = strip_at == 3
        return (0, jnp.where(last, row + 2, row + lower), jnp.where(last, lower, strip_at))

    return pl.pallas_call(
        partial(strips_kernel, strip),
        cost_estimate=cost(4),
        grid=(8,),
        in_specs=[pl.BlockSpec(memory_space=pl.ANY)]
        + [pl.BlockSpec((half, width), lambda s: (0, 0))] * 2
        + [pl.BlockSpec((half, columns), lambda s: (0, s // 2))] * 2,
        out_specs=pl.BlockSpec((packed.shape[0], 16, columns), spot),
        out_shape=jax.ShapeDtypeStruct(packed.shape, packed.dtype),
        input_output_aliases={0: 0},
        scratch_shapes=[pltpu.VMEM((width, columns), f32)],
        compiler_params=pltpu.CompilerParams(vmem_limit_bytes=vmem_limit),
    )(packed, *left, *right)


def folded_kernel(left_own, left_other, right_own, right_other, out):
    _, rows, columns = out.shape
    total = outer_sum(left_own[...], right_own[...]) + outer_sum(left_other[...], right_other[...])
    total = total.astype(bf16).reshape(out.shape[0], -1, total.shape[1])
    tall = total.shape[1]
    out[:, :tall, :] = total[:, :, :columns]
    over = total.shape[2] - columns
    for at in range(columns // over):
        part = total[:, at * (rows - tall) : (at + 1) * (rows - tall), columns:]
        out[:, tall:, at * over : (at + 1) * over] = part


def outer_folded(left, right, shape, first):
    places, rows, columns = shape
    tokens, units = left[0].shape
    model = right[0].shape[1]
    high = units * model // (places * columns)
    return pl.pallas_call(
        folded_kernel,
        cost_estimate=cost(5),
        grid=(2,),
        in_specs=[pl.BlockSpec((tokens, units // 2), lambda s: (0, s))] * 2
        + [pl.BlockSpec((tokens, model), lambda s: (0, 0))] * 2,
        out_specs=pl.BlockSpec((places // 2, high, columns), lambda s: (s, first // high, 0)),
        out_shape=jax.ShapeDtypeStruct(shape, bf16),
        compiler_params=pltpu.CompilerParams(vmem_limit_bytes=vmem_limit),
    )(*left, *right)


def total_of(pieces):
    return jnp.sum(pieces.astype(f32), axis=0)


def after(value, *others):
    return lax.optimization_barrier((value,) + others)[0]


def joined(*parts):
    return jnp.concatenate(parts, axis=0)


def gather_team(block, *stage):
    z_at = lax.axis_index("z")
    half = block.shape[0] // 2
    below, above = hop(block, "z", 1), hop(block, "z", -1)
    if stage:
        below, above = after(below, *stage), after(above, *stage)
    across = joined(hop(below[:half], "z", 1), hop(above[half:], "z", -1))
    own = jnp.zeros((4,) + block.shape, block.dtype)
    for offset, part in ((0, block), (1, above), (3, below), (2, across)):
        own = lax.dynamic_update_index_in_dim(own, part, (z_at + offset) % 4, 0)
    own = own.reshape(4 * block.shape[0], -1)
    return own, hop(own, "row", 1)


def reduce_team(other, own):
    z_at = lax.axis_index("z")
    other = hop(other, "row", 1).reshape(4, -1, other.shape[-1])
    own = own.reshape(other.shape)

    def block(offset):
        at = (z_at + offset) % 4
        parts = [lax.dynamic_index_in_dim(whole, at, 0, keepdims=False) for whole in (own, other)]
        return parts[0].astype(f32) + parts[1].astype(f32)

    sums = {offset: block(offset) for offset in (2, 1, 3, 0)}
    half = own.shape[1] // 2
    from_below = hop(sums[2][:half].astype(bf16), "z", 1)
    from_above = hop(sums[2][half:].astype(bf16), "z", -1)
    up = joined(sums[1][:half] + from_below.astype(f32), sums[1][half:]).astype(bf16)
    down = joined(sums[3][:half], sums[3][half:] + from_above.astype(f32)).astype(bf16)
    up, down = hop(up, "z", 1), hop(down, "z", -1)
    return sums[0] + up.astype(f32) + down.astype(f32), up


def project_in(left, weight):
    return jnp.dot(left, weight, preferred_element_type=f32)


def project_back(grad, weight):
    return lax.dot_general(grad, weight, (((1,), (1,)), ((), ())), preferred_element_type=f32)


def outer_sum(left, grad):
    return lax.dot_general(left, grad, (((0,), (0,)), ((), ())), preferred_element_type=f32)


def fold_down(rows, width):
    over = rows.shape[-1] - width
    group = rows.shape[-2] * over // width
    tail = [rows[..., at : at + group, width:] for at in range(0, rows.shape[-2], group)]
    return jnp.concatenate([rows[..., :width], jnp.concatenate(tail, axis=-1)], axis=-2)


def unfold_down(rows, model):
    width = rows.shape[-1]
    over = model - width
    count = rows.shape[-2] * width // model
    tail = rows[..., count:, :]
    tail = [tail[..., at : at + over] for at in range(0, width, over)]
    return jnp.concatenate([rows[..., :count, :], jnp.concatenate(tail, axis=-2)], axis=-1)


def cost(micros):
    return pl.CostEstimate(flops=0, bytes_accessed=int(micros * 3.0e6), transcendentals=0)


def kernel_call(kernel, micros, outs, scratch=()):
    return pl.pallas_call(
        kernel,
        cost_estimate=cost(micros),
        out_shape=[jax.ShapeDtypeStruct(shape, dtype) for shape, dtype in outs],
        scratch_shapes=list(scratch),
        compiler_params=pltpu.CompilerParams(vmem_limit_bytes=vmem_limit),
    )


def chunk_rows(chunk, size):
    return pl.ds(pl.multiple_of(chunk * size, size), size)


def panels(ref, rows):
    return jnp.concatenate([ref[at, rows, :] for at in range(ref.shape[0])], axis=1)


def set_panels(ref, rows, value):
    for at in range(ref.shape[0]):
        ref[at, rows, :] = value[:, at * 128 : (at + 1) * 128]


def gate_parts(raw_in, raw_rec, params):
    gate_in = jax.nn.sigmoid(raw_in + params[5:6, :])
    gate_rec = jax.nn.sigmoid(raw_rec + params[6:7, :])
    log_decay = gate_rec * params[7:8, :]
    base = jnp.exp(log_decay)
    return gate_in, gate_rec, base, -jnp.tanh(log_decay) * (base * base + 1.0)


def gates_kernel(
    cin, halo, masks, params, w_in, w_rec,
    conv, factor, state, decay, ends, ext, raw_in, raw_rec, drive,
):
    tokens, width = cin.shape
    count = halo.shape[0]
    size = tokens // count
    tiles = width // 128

    def convolve(chunk, carry):
        rows = chunk_rows(chunk, size)
        ext[0:8, :] = halo[chunk].astype(f32)
        ext[8 : 8 + size, :] = cin[rows, :].astype(f32)
        total = params[4:5, :] + params[0:1, :] * ext[8 : 8 + size, :]
        for k in (1, 2, 3):
            total = total + params[k : k + 1, :] * ext[8 - k : 8 - k + size, :] * masks[rows, k : k + 1]
        conv[rows, :] = total.astype(bf16)
        return carry

    lax.fori_loop(0, count, convolve, 0)
    raw_in[...] = jnp.dot(conv[...], w_in[...], preferred_element_type=f32)
    raw_rec[...] = jnp.dot(conv[...], w_rec[...], preferred_element_type=f32)

    def gate(chunk, carry):
        rows = chunk_rows(chunk, size)
        gate_in, _, base, kept = gate_parts(raw_in[rows, :], raw_rec[rows, :], params)
        scale = jnp.sqrt(jnp.maximum(kept, beta_floor))
        set_panels(factor, rows, base * masks[rows, 0:1])
        set_panels(drive, rows, scale * gate_in * conv[rows, :].astype(f32))
        return carry

    lax.fori_loop(0, count, gate, 0)

    def scan(slot, carry):
        at = pl.ds(slot, count, stride=size)
        after = []
        for tile, (held, gone) in enumerate(carry):
            step = factor[tile, at, :]
            held = step * held + drive[tile, at, :]
            gone = step * gone
            state[tile, at, :] = held
            decay[tile, at, :] = gone
            after.append((held, gone))
        return tuple(after)

    first = pl.ds(0, count, stride=size)
    start = []
    for tile in range(tiles):
        zero = drive[tile, first, :] * 0.0
        start.append((zero, zero + 1.0))
    last = lax.fori_loop(0, size, scan, tuple(start))
    for tile, (held, gone) in enumerate(last):
        ends[0, :, tile * 128 : (tile + 1) * 128] = gone
        ends[1, :, tile * 128 : (tile + 1) * 128] = held


def carry_kernel(backward, spot, pieces, entering):
    mine = spot[0]
    places = pieces.shape[0]
    order = range(places - 1, -1, -1) if backward else range(places)
    decay, state = pieces[order[0], 0], pieces[order[0], 1]
    here = jnp.where(mine == order[0], 1.0, 0.0)
    own_decay, own_state = jnp.zeros_like(decay) + here, jnp.zeros_like(state)
    for place_at in order[1:]:
        here = jnp.where(mine == place_at, 1.0, 0.0)
        own_decay = own_decay + decay * here
        own_state = own_state + state * here
        step = pieces[place_at, 0]
        state = step * state + pieces[place_at, 1]
        decay = step * decay
    for row in range(2):
        held = jnp.zeros((2, decay.shape[1]), f32)
        for z in range(3, -1, -1) if backward else range(4):
            start = row * 8 + z * 2
            part = slice(start, start + 2)
            inside = own_decay[part] * held + own_state[part]
            held = decay[part] * held + state[part]
            for line in range(2):
                entering[start + line] = inside[line : line + 1]


def gelu_parts(value):
    slope = 0.7978845608028654
    square = value * value
    inner = jnp.tanh(slope * (value + 0.044715 * value * square))
    half = 0.5 * (1.0 + inner)
    act = value * half
    grad = half + 0.5 * value * (1.0 - inner * inner) * slope * (1.0 + 3 * 0.044715 * square)
    return act, grad


def mix_kernel(pre, state, decay, entering, out_rows, rec_state, mixed, partial_sum):
    count = entering.shape[0]
    tokens, width = rec_state.shape
    size = tokens // count

    def mix(chunk, carry):
        rows = chunk_rows(chunk, size)
        full = panels(state, rows) + panels(decay, rows) * entering[chunk]
        rec_state[rows, :] = full
        mixed[rows, :] = (gelu_parts(pre[rows, :])[0] * full).astype(bf16)
        return carry

    lax.fori_loop(0, count, mix, 0)
    partial_sum[...] = jnp.dot(
        mixed[...], out_rows[...], preferred_element_type=f32
    ).astype(bf16)


def unmix_kernel(
    mixed_own, mixed_other, pre_own, pre_other, rec_own, rec_other, factor,
    grad_gelu, adjoint, reach, ends, grad_state,
):
    half, width = rec_own.shape
    count = ends.shape[1]
    size = 2 * half // count
    tiles = width // 128

    def unmix(start, grad_mixed, pre, rec_state, chunk, carry):
        rows = chunk_rows(chunk, size)
        out = chunk_rows(chunk + start, size)
        act, slope = gelu_parts(pre[rows, :])
        grad = grad_mixed[rows, :]
        grad_gelu[out, :] = (grad * rec_state[rows, :] * slope).astype(bf16)
        set_panels(grad_state, out, grad * act)
        return carry

    lax.fori_loop(0, count // 2, partial(unmix, 0, mixed_own, pre_own, rec_own), 0)
    lax.fori_loop(0, count // 2, partial(unmix, count // 2, mixed_other, pre_other, rec_other), 0)

    def scan(step, carry):
        at = pl.ds(size - 1 - step, count, stride=size)
        after = []
        for tile, (held, gone, ahead) in enumerate(carry):
            held = ahead * held + grad_state[tile, at, :]
            gone = ahead * gone
            adjoint[tile, at, :] = held
            reach[tile, at, :] = gone
            after.append((held, gone, factor[tile, at, :]))
        return tuple(after)

    first = pl.ds(0, count, stride=size)
    start = []
    for tile in range(tiles):
        zero = factor[tile, first, :] * 0.0
        start.append((zero, zero + 1.0, zero + 1.0))
    last = lax.fori_loop(0, size, scan, tuple(start))
    for tile, (held, gone, ahead) in enumerate(last):
        ends[0, :, tile * 128 : (tile + 1) * 128] = ahead * gone
        ends[1, :, tile * 128 : (tile + 1) * 128] = ahead * held


def ungate_kernel(
    adjoint, reach, arriving, rec_own, rec_other, entering, conv, cin, halo, masks, params, w_in,
    w_rec, grad_in, grad_rec, grad_conv, sums, ext, direct, raw_rec,
):
    tokens, width = cin.shape
    count = halo.shape[0]
    size = tokens // count
    zero = params[0:8, :] * 0.0

    def fold(value):
        total = value[0:8]
        for at in range(8, size, 8):
            total = total + value[at : at + 8]
        return total

    def ungate(start, rec_state, chunk, carry):
        sum_in, sum_rec, sum_decay = carry
        ext[8 : 8 + size, :] = rec_state[chunk_rows(chunk, size), :]
        chunk = chunk + start
        rows = chunk_rows(chunk, size)
        ext[7:8, :] = entering[chunk]
        full = panels(adjoint, rows) + panels(reach, rows) * arriving[chunk]
        gate_in, gate_rec, base, square = gate_parts(direct[rows, :], raw_rec[rows, :], params)
        scale = jnp.sqrt(jnp.maximum(square, beta_floor))
        values = conv[rows, :].astype(f32)
        scaled = full * scale
        drive = full * gate_in * values
        slope = jnp.where(square > beta_floor, (1.0 - square) / scale, 0.0)
        grad_log = full * base * masks[rows, 0:1] * ext[7 : 7 + size, :] - slope * drive
        raw_in = scale * drive * (1.0 - gate_in)
        pulled = grad_log * gate_rec
        rec = pulled * params[7:8, :] * (1.0 - gate_rec)
        grad_in[rows, :] = raw_in.astype(bf16)
        grad_rec[rows, :] = rec.astype(bf16)
        direct[rows, :] = scaled * gate_in
        return (sum_in + fold(raw_in), sum_rec + fold(rec), sum_decay + fold(pulled))

    direct[...] = jnp.dot(conv[...], w_in[...], preferred_element_type=f32)
    raw_rec[...] = jnp.dot(conv[...], w_rec[...], preferred_element_type=f32)
    half = count // 2
    totals = lax.fori_loop(0, half, partial(ungate, 0, rec_own), (zero, zero, zero))
    sum_in, sum_rec, sum_decay = lax.fori_loop(0, half, partial(ungate, half, rec_other), totals)
    back = (((1,), (1,)), ((), ()))
    direct[...] += lax.dot_general(grad_in[...], w_in[...], back, preferred_element_type=f32)
    direct[...] += lax.dot_general(grad_rec[...], w_rec[...], back, preferred_element_type=f32)

    def taps(chunk, carry):
        sum_bias, sum_taps = carry
        rows = chunk_rows(chunk, size)
        grad = direct[rows, :].astype(bf16)
        grad_conv[rows, :] = grad
        grad = grad.astype(f32)
        ext[0:8, :] = halo[chunk].astype(f32)
        ext[8 : 8 + size, :] = cin[rows, :].astype(f32)
        new_taps = [sum_taps[0] + fold(grad * ext[8 : 8 + size, :])]
        for k in (1, 2, 3):
            moved = ext[8 - k : 8 - k + size, :] * masks[rows, k : k + 1]
            new_taps.append(sum_taps[k] + fold(grad * moved))
        return (sum_bias + fold(grad), tuple(new_taps))

    sum_bias, sum_taps = lax.fori_loop(0, count, taps, (zero, (zero,) * 4))
    rows_out = sum_taps + (sum_bias, sum_in, sum_rec, sum_decay * params[8:9, :])
    for index, total in enumerate(rows_out):
        sums[index : index + 1, :] = jnp.sum(total, axis=0, keepdims=True)


def unconvolve_kernel(grad_conv, halo, masks, params, out, ext):
    tokens, width = grad_conv.shape
    count = halo.shape[0]
    size = tokens // count

    def spread(chunk, carry):
        rows = chunk_rows(chunk, size)
        ext[0:size, :] = grad_conv[rows, :].astype(f32)
        ext[size : size + 8, :] = halo[chunk].astype(f32)
        total = params[0:1, :] * ext[0:size, :]
        for k in (1, 2, 3):
            total = total + params[k : k + 1, :] * ext[k : k + size, :] * masks[rows, 3 + k : 4 + k]
        out[rows, :] = total.astype(bf16)
        return carry

    lax.fori_loop(0, count, spread, 0)


def body(
    tokens,
    lengths,
    norm_one,
    gelu_weight,
    input_weight,
    conv_weight,
    conv_bias,
    gate_input,
    bias_input,
    gate_recur,
    bias_recur,
    decay_param,
    out_weight,
    norm_two,
    gate_weight,
    up_weight,
    down_weight,
    cotangent,
):
    row_count, size, model = tokens.shape
    local = row_count * size
    block, hidden = gelu_weight.shape
    inner = gate_weight.shape[1]
    head = gate_input.shape[1]
    channels, units = hidden // 8, inner // 8
    strip = gate_input.shape[0]
    width = -(-channels // 128) * 128
    spare = width - channels
    row_at, z_at, y_at, x_at = (lax.axis_index(name) for name in everywhere)
    plane_at = y_at * 4 + x_at
    chunks = 16
    total_tokens = chunks * size
    flat = tokens.reshape(local, model)

    row_total = jnp.sum(lengths, axis=1)
    own_slots = (z_at * 16 + plane_at) * size + jnp.arange(size)
    valid = (own_slots[None, :] < row_total[:, None]).astype(f32).reshape(local, 1)
    upstream = cotangent.reshape(local, model).astype(f32) * valid

    def halves(whole):
        whole = whole.reshape(2, 4 * local, -1)
        return [
            lax.dynamic_index_in_dim(whole, row_at ^ other, 0, keepdims=False) for other in (0, 1)
        ]

    tokens_own, tokens_other = halves(lax.all_gather(flat, team, axis=0, tiled=True))

    gains = jnp.stack([norm_one, norm_two], axis=1)
    gains = jnp.broadcast_to(
        jnp.pad(gains, ((0, 0), (0, spare - 2)))[:, None, :], (block, 8, spare)
    )
    third = jnp.concatenate(
        [
            gelu_weight.reshape(block, 8, channels),
            jnp.zeros_like(gains),
            gate_weight.reshape(block, 8, units),
            up_weight.reshape(block, 8, units),
        ],
        axis=2,
    ).transpose(1, 0, 2)
    lead = jnp.concatenate([input_weight.reshape(block, 8, channels), gains], axis=2)
    lead = lead.transpose(1, 0, 2)[:, None]
    lead = jnp.broadcast_to(lead, (8, 16, block, width)).reshape(model, width)
    input_full = lax.all_to_all(lead, everywhere, 0, 0, tiled=True)
    third = lax.all_to_all(after(third, input_full), team, 0, 0, tiled=True).reshape(8 * block, -1)
    first, third = third[:, :width], third[:, width:]
    small = jnp.stack([conv_bias, bias_input, bias_recur, decay_param], axis=1)
    rest = jnp.concatenate([gate_input, gate_recur, conv_weight, small], axis=1)
    rest = jnp.pad(rest, ((0, 32 - strip), (0, width - rest.shape[1])))
    rest = gather_plane(after(rest, first))

    def in_order(rows, count):
        rows = rows.reshape(16, count, block, rows.shape[-1])
        return rows.transpose(1, 0, 2, 3).reshape(count * 16 * block, rows.shape[-1])

    cuts = -(-model // width)
    out_pack = jnp.pad(out_weight, ((0, 32 - strip), (0, cuts * width - model)))
    out_pack = out_pack.reshape(32, cuts, width).transpose(1, 0, 2).reshape(cuts * 32, width)
    second = jnp.concatenate([first, out_pack], axis=0)
    second = lax.all_gather(second, plane, axis=0, tiled=False)
    gelu_full = in_order(second[:, : 8 * block], 8)
    out_rows = second[:, 8 * block :].reshape(16, cuts, 32, width)[:, :, :strip]
    out_rows = out_rows.transpose(0, 2, 1, 3).reshape(channels, cuts * width)[:, :model]
    out_rows = jnp.pad(out_rows, ((0, spare), (0, 0)))

    third = jnp.concatenate([third, fold_down(down_weight, 2 * units)], axis=0)
    third = lax.all_gather(third, plane, axis=0, tiled=False)
    down = unfold_down(third[:, 8 * block :], model).reshape(units, model)
    third = in_order(third[:, : 8 * block], 8)

    gain_one = input_full[:, channels].astype(f32)[None, :]
    gain_two = input_full[:, channels + 1].astype(f32)[None, :]
    def rms_unit(values):
        return lax.rsqrt(jnp.mean(values * values, axis=-1, keepdims=True) + epsilon)

    def norm_half(values):
        values = values.astype(f32)
        return (values * rms_unit(values) * gain_one).astype(bf16)

    own_head = (jnp.arange(width)[:, None] // head) == (jnp.arange(width)[None, :] // head)

    def spread_heads(part):
        return jnp.where(own_head, jnp.concatenate([part, part, part], axis=1)[:, :width], 0)

    own_tokens = flat.astype(f32)
    normed_own, normed_other = norm_half(tokens_own), norm_half(tokens_other)
    conv_in = joined(
        project_in(normed_own, input_full).astype(bf16),
        project_in(normed_other, input_full).astype(bf16),
    )
    by_chunk = (chunks, size, width)
    halo = hop(conv_in.reshape(by_chunk)[:, size - 8 :], plane, 1)
    rest = after(rest, halo)[:, :strip].reshape(channels, width)
    rest = jnp.pad(rest, ((0, spare), (0, 0)))
    w_in = spread_heads(rest[:, :head])
    w_rec = spread_heads(rest[:, head : 2 * head])
    rows_small = rest[:, 2 * head : 2 * head + 8].astype(f32).T
    decay_row = rows_small[7:8]
    params = jnp.concatenate(
        [
            rows_small[:7],
            -8.0 * jax.nn.softplus(decay_row),
            -8.0 * jax.nn.sigmoid(decay_row),
            jnp.zeros((7, width), f32),
        ],
        axis=0,
    )

    lens = jnp.stack([lengths, hop(lengths, "row", 1)], axis=0)
    starts = jnp.cumsum(lens, axis=2) - lens
    first_slot = jnp.arange(4) * (16 * size) + plane_at * size

    def position(slot):
        live = (lens > 0)[:, None, :, None, :] & (starts[:, None, :, None, :] <= slot[..., None])
        origin = jnp.max(jnp.where(live, starts[:, None, :, None, :], 0), axis=-1)
        return slot - origin

    slots = first_slot[None, :, None, None] + jnp.arange(size)[None, None, None, :]
    slots = jnp.broadcast_to(slots, (2, 4, row_count, size))
    here = position(slots)
    columns = [here != 0] + [here >= k for k in (1, 2, 3)]
    for k in (1, 2, 3):
        ahead = slots + k
        columns.append((position(ahead) >= k) & (ahead < 64 * size))
    columns.append(jnp.zeros_like(columns[0]))
    masks = jnp.stack(columns, axis=-1).astype(f32).reshape(total_tokens, 8)

    def turned(rim, shift):
        by_z = rim.reshape((2, 4, row_count) + rim.shape[1:])
        return jnp.roll(by_z, shift, axis=1).reshape(rim.shape)

    halo = jnp.where(plane_at == 0, turned(halo, 1), halo)
    wide = ((total_tokens, width), f32)
    narrow = ((total_tokens, width), bf16)
    paneled = ((width // 128, total_tokens, 128), f32)
    ends_shape = ((2, chunks, width), f32)
    extended = pltpu.VMEM((size + 8, width), f32)
    whole = pltpu.VMEM(*wide)
    folded = pltpu.VMEM(*paneled)
    conv_vals, factor, local_state, decay, ends = kernel_call(
        gates_kernel,
        60,
        [narrow, paneled, paneled, paneled, ends_shape],
        [extended, whole, whole, folded],
    )(conv_in, halo, masks, params, w_in, w_rec)


    def carried(pieces, backward):
        spot = plane_at.astype(jnp.int32).reshape(1)
        return pl.pallas_call(
            partial(carry_kernel, backward),
            cost_estimate=cost(1),
            out_shape=jax.ShapeDtypeStruct((chunks, 1, width), f32),
            in_specs=[pl.BlockSpec(memory_space=pltpu.SMEM), pl.BlockSpec(memory_space=pltpu.VMEM)],
            out_specs=pl.BlockSpec(memory_space=pltpu.VMEM),
        )(spot, pieces)

    pieces = gather_plane(ends)
    down_own, down_other = gather_team(after(upstream.astype(bf16), conv_in), pieces)
    entering = after(carried(pieces, False), down_own)
    gelu_own, gelu_other = project_in(normed_own, gelu_full), project_in(normed_other, gelu_full)
    half = total_tokens // 2

    def mix(which, gelu_pre):
        rows = pl.BlockSpec((half, width), lambda i: (0, 0))
        folds = pl.BlockSpec((width // 128, half, 128), lambda i: (0, which, 0))
        return pl.pallas_call(
            mix_kernel,
            cost_estimate=cost(5),
            out_shape=[
                jax.ShapeDtypeStruct((half, width), f32),
                jax.ShapeDtypeStruct((half, width), bf16),
                jax.ShapeDtypeStruct((half, model), bf16),
            ],
            grid=(1,),
            in_specs=[
                rows,
                folds,
                folds,
                pl.BlockSpec((chunks // 2, 1, width), lambda i: (which, 0, 0)),
                pl.BlockSpec((width, model), lambda i: (0, 0)),
            ],
            out_specs=[
                pl.BlockSpec((half, width), lambda i: (0, 0)),
                pl.BlockSpec((half, width), lambda i: (0, 0)),
                pl.BlockSpec((half, model), lambda i: (0, 0)),
            ],
            compiler_params=pltpu.CompilerParams(vmem_limit_bytes=vmem_limit),
        )(gelu_pre, local_state, decay, entering, out_rows)

    other_state, other_mixed, other_middle = mix(1, gelu_other)
    own_state, own_mixed, own_middle = mix(0, gelu_own)
    middle = own_tokens + reduce_team(other_middle, own_middle)[0]

    scale_two = rms_unit(middle)
    normed_two = (middle * scale_two * gain_two).astype(bf16)
    two_own, two_other = gather_team(normed_two)

    def feed(values, grad_inner):
        pre = project_in(values, third)
        act, slope = gelu_parts(pre[:, :units])
        up = pre[:, units:]
        grad = [(grad_inner * up * slope).astype(bf16), (grad_inner * act).astype(bf16)]
        return (act * up).astype(bf16), jnp.concatenate(grad, axis=1)

    inner_own, pre_own = feed(two_own, project_back(down_own, down))
    inner_other, pre_other = feed(two_other, project_back(down_other, down))
    terms_other = project_back(pre_other, third).astype(bf16)
    terms_own = project_back(pre_own, third).astype(bf16)
    grad_two, _ = reduce_team(terms_other, terms_own)
    def back_to_rows(grad):
        grad = grad.astype(bf16).reshape(8, block, -1)
        return lax.all_to_all(grad, team, 0, 0, tiled=True).astype(f32).transpose(1, 0, 2)

    def norm_back(values, scale, gain, grad):
        pulled = gain * grad
        mean = jnp.mean(pulled * values, axis=-1, keepdims=True)
        return scale * pulled - values * (scale * scale * scale * mean)

    def gain_grad(gain, pairs):
        total = sum(jnp.sum(weight.astype(f32) * grad, axis=1) for weight, grad in pairs)
        return total / gain.astype(f32)

    grad_middle = upstream + norm_back(middle, scale_two, gain_two, grad_two)
    fold = 8 * block
    tail = fold + units * model // (32 * units)
    share = tail + 48
    packed_down = outer_folded(
        (inner_own, inner_other), (down_own, down_other), (16, share, 2 * units), fold
    )
    grad_third = add_outer(packed_down, (two_own, two_other), (pre_own, pre_other))
    branch_own, branch_other = gather_team(
        after(grad_middle.astype(bf16), packed_down), grad_third
    )

    grad_gelu, adjoint, reach, ends = kernel_call(
        unmix_kernel, 100, [narrow, paneled, paneled, ends_shape], [folded]
    )(
        project_back(branch_own, out_rows), project_back(branch_other, out_rows),
        gelu_own, gelu_other, own_state, other_state, factor,
    )
    grad_third = add_strips(
        grad_third, (own_mixed, other_mixed), (branch_own, branch_other), strip, tail
    )
    joined_ends = gather_plane(ends)
    grad_third = after(grad_third, joined_ends)
    grad_third = lax.psum_scatter(
        grad_third.reshape(16 * share, 2 * units), plane, scatter_dimension=0, tiled=True
    )
    normed = (normed_own, norm_half(after(tokens_other, ends)))
    grad_gelu_rows = jnp.zeros((16, 8 * block, width), bf16)
    grad_gelu_rows = add_outer(grad_gelu_rows, normed, (grad_gelu,))
    result_own = project_in(after(inner_own, ends), down).astype(bf16)
    result_other = project_in(after(inner_other, ends), down).astype(bf16)
    arriving = after(
        carried(joined_ends, True), grad_gelu_rows, result_own, result_other
    )
    grad_gelu_rows = lax.all_to_all(after(grad_gelu_rows, arriving), plane, 0, 0, tiled=True)
    grad_in, grad_rec, grad_conv, sums = kernel_call(
        ungate_kernel, 100, [narrow, narrow, narrow, ((8, width), f32)], [extended, whole, whole]
    )(
        adjoint, reach, arriving, own_state, other_state, entering, conv_vals, conv_in, halo, masks,
        params, w_in, w_rec,
    )
    ahead = hop(grad_conv.reshape(by_chunk)[:, :8], plane, -1)
    ahead = after(ahead, grad_gelu_rows)
    ahead = jnp.where(plane_at == 15, turned(ahead, -1), ahead)
    (grad_conv_in,) = kernel_call(unconvolve_kernel, 1, [narrow], [extended])(
        grad_conv, ahead, masks, params
    )

    def own_heads(grad):
        grad = jnp.where(own_head, grad, 0)[:channels]
        return grad[:, :head] + grad[:, head:channels]

    grad_rest = jnp.concatenate(
        [
            own_heads(outer_sum(after(conv_vals, ahead), grad_in)),
            own_heads(outer_sum(after(conv_vals, ahead), grad_rec)),
            sums.T[:channels],
        ],
        axis=1,
    ).astype(bf16)
    grad_rest = grad_rest.reshape(16, strip, -1)
    grad_rest = jnp.pad(
        grad_rest, ((0, 0), (0, 32 - strip), (0, width - grad_rest.shape[2]))
    )
    grad_lead = jnp.pad(grad_rest, ((0, 0), (8 * block, 0), (0, 0)))
    grad_pair = jnp.concatenate([grad_conv_in, grad_gelu], axis=1)
    pair_weight = jnp.concatenate([input_full, gelu_full], axis=1)
    terms_other = project_back(grad_pair[half:], pair_weight).astype(bf16)
    terms_own = project_back(grad_pair[:half], pair_weight).astype(bf16)
    grad_normed, upward = reduce_team(
        jnp.concatenate([terms_other, result_other], axis=1),
        jnp.concatenate([terms_own, result_own], axis=1),
    )
    result = (middle + grad_normed[:, model:]) * valid
    output = result.reshape(row_count, size, model).astype(bf16)
    grad_normed = grad_normed[:, :model]
    grad_lead = add_outer(grad_lead, normed, (grad_conv_in,))
    grad_lead = lax.all_to_all(grad_lead, plane, 0, 0, tiled=True)
    cut = 8 * block
    grad_lead = total_of(after(grad_lead, upward))
    grad_rest = grad_lead[cut : cut + strip]
    grad_gelu_rows = total_of(after(grad_gelu_rows, upward)).astype(bf16)
    grad_gate_input = grad_rest[:, :head]
    grad_gate_recur = grad_rest[:, head : 2 * head]
    grad_small = grad_rest[:, 2 * head : 2 * head + 8]
    grad_third = after(grad_third, upward)
    grad_down_weight = unfold_down(grad_third[fold:tail], model).astype(f32)
    last = grad_third[tail + 32 :, : model // 2]
    last = joined(last[:, : model // 4], last[:, model // 4 :])
    grad_out_weight = jnp.concatenate(
        [grad_third[tail : tail + strip], last[:strip]], axis=1
    ).astype(f32)
    team_third = jnp.concatenate(
        [grad_third[:cut], grad_lead[:cut].astype(bf16), grad_gelu_rows], axis=1
    )
    team_third = back_to_rows(team_third)
    grad_input_weight = team_third[:, :, 2 * units : 2 * units + channels].reshape(block, hidden)
    grad_gelu_weight = team_third[:, :, 2 * units + width :][:, :, :channels].reshape(block, hidden)
    grad_gate_weight = team_third[:, :, :units].reshape(block, inner)
    grad_up_weight = team_third[:, :, units : 2 * units].reshape(block, inner)

    grad_norm_two = gain_grad(
        norm_two, [(gate_weight, grad_gate_weight), (up_weight, grad_up_weight)]
    )
    grad_norm_one = gain_grad(
        norm_one, [(gelu_weight, grad_gelu_weight), (input_weight, grad_input_weight)]
    )
    own_scale = rms_unit(own_tokens)
    grad_tokens = grad_middle + norm_back(own_tokens, own_scale, gain_one, grad_normed)
    return (
        output,
        grad_tokens.reshape(row_count, size, model),
        grad_norm_one,
        grad_gelu_weight,
        grad_input_weight,
        grad_small[:, :4],
        grad_small[:, 4],
        grad_gate_input,
        grad_small[:, 5],
        grad_gate_recur,
        grad_small[:, 6],
        grad_small[:, 7],
        grad_out_weight,
        grad_norm_two,
        grad_gate_weight,
        grad_up_weight,
        grad_down_weight,
    )


def solution(mesh):
    grid = Mesh(mesh.devices.reshape(2, 4, 4, 4), everywhere)
    slots = P("row", ("z", "y", "x"), None)
    line = P(everywhere)
    sheet = P(everywhere, None)
    return jax.shard_map(
        body,
        mesh=grid,
        in_specs=(
            slots, P("row", None), line, sheet, sheet, sheet, line, sheet, line, sheet, line, line,
            sheet, line, sheet, sheet, sheet, slots,
        ),
        out_specs=(
            slots, slots, line, sheet, sheet, sheet, line, sheet, line, sheet, line, line, sheet,
            line, sheet, sheet, sheet,
        ),
        check_vma=False,
    )
```

```python
from functools import partial

import jax
import jax.numpy as jnp
from jax import lax
from jax.experimental import pallas as pl
from jax.experimental.pallas import tpu as pltpu
from jax.sharding import Mesh
from jax.sharding import PartitionSpec as P

epsilon = 1e-06
beta_floor = 0.001
bf16 = jnp.bfloat16
f32 = jnp.float32
everywhere = ("row", "z", "y", "x")
team = ("row", "z")
plane = ("y", "x")
vmem_limit = 32 * 1024 * 1024


def hop(block, axis, distance):
    count = lax.axis_size(axis)
    return lax.ppermute(block, axis, [(i, (i + distance) % count) for i in range(count)])


def gather_plane(piece):
    return lax.all_to_all(jnp.broadcast_to(piece, (16,) + piece.shape), plane, 0, 0, tiled=True)


def outer_kernel(packed, left_own, left_other, right_own, right_other, out):
    total = outer_sum(left_own[...], right_own[...]) + outer_sum(left_other[...], right_other[...])
    count, rows, columns = out.shape
    total = total.astype(bf16).reshape(count, rows, total.shape[1])
    out[:, :, : total.shape[2]] = total
    if total.shape[2] < columns:
        out[:, :, total.shape[2] :] = jnp.zeros((count, rows, columns - total.shape[2]), bf16)


def add_outer(packed, left, right):
    half, model = left[0].shape
    if len(right) == 1:
        right, starts = right * 2, (0, 1)
    else:
        starts = (0, 0)
    columns = right[0].shape[1]
    block = model // 128
    return pl.pallas_call(
        outer_kernel,
        cost_estimate=cost(model * columns / 350000),
        grid=(8,),
        in_specs=[pl.BlockSpec(memory_space=pl.ANY)]
        + [pl.BlockSpec((half, 16 * block), lambda s: (0, s))] * 2
        + [pl.BlockSpec((half, columns), partial(lambda at, s: (at, 0), at)) for at in starts],
        out_specs=pl.BlockSpec((16, block, packed.shape[2]), lambda s: (0, s, 0)),
        out_shape=jax.ShapeDtypeStruct(packed.shape, packed.dtype),
        input_output_aliases={0: 0},
        compiler_params=pltpu.CompilerParams(vmem_limit_bytes=vmem_limit),
    )(packed, *left, *right)


def strips_kernel(strip, packed, left_own, left_other, right_own, right_other, out, total):
    step = pl.program_id(0)

    @pl.when(step % 2 == 0)
    def compute():
        total[...] = outer_sum(left_own[...], right_own[...]) + outer_sum(
            left_other[...], right_other[...]
        )

    for part in range(2):

        @pl.when(step % 2 == part)
        def store(part=part):
            for place in range(out.shape[0]):
                start = place * strip + part * 16
                out[place] = total[start : start + 16, :].astype(bf16)


def add_strips(packed, left, right, strip, first):
    half, width = left[0].shape
    columns = right[0].shape[1] // 4
    row = first // 16

    def spot(step):
        lower, strip_at = step % 2, step // 2
        last = strip_at == 3
        return (0, jnp.where(last, row + 2, row + lower), jnp.where(last, lower, strip_at))

    return pl.pallas_call(
        partial(strips_kernel, strip),
        cost_estimate=cost(4),
        grid=(8,),
        in_specs=[pl.BlockSpec(memory_space=pl.ANY)]
        + [pl.BlockSpec((half, width), lambda s: (0, 0))] * 2
        + [pl.BlockSpec((half, columns), lambda s: (0, s // 2))] * 2,
        out_specs=pl.BlockSpec((packed.shape[0], 16, columns), spot),
        out_shape=jax.ShapeDtypeStruct(packed.shape, packed.dtype),
        input_output_aliases={0: 0},
        scratch_shapes=[pltpu.VMEM((width, columns), f32)],
        compiler_params=pltpu.CompilerParams(vmem_limit_bytes=vmem_limit),
    )(packed, *left, *right)


def folded_kernel(left_own, left_other, right_own, right_other, out):
    _, rows, columns = out.shape
    total = outer_sum(left_own[...], right_own[...]) + outer_sum(left_other[...], right_other[...])
    total = total.astype(bf16).reshape(out.shape[0], -1, total.shape[1])
    tall = total.shape[1]
    out[:, :tall, :] = total[:, :, :columns]
    over = total.shape[2] - columns
    for at in range(columns // over):
        part = total[:, at * (rows - tall) : (at + 1) * (rows - tall), columns:]
        out[:, tall:, at * over : (at + 1) * over] = part


def outer_folded(left, right, shape, first):
    places, rows, columns = shape
    tokens, units = left[0].shape
    model = right[0].shape[1]
    high = units * model // (places * columns)
    return pl.pallas_call(
        folded_kernel,
        cost_estimate=cost(5),
        grid=(2,),
        in_specs=[pl.BlockSpec((tokens, units // 2), lambda s: (0, s))] * 2
        + [pl.BlockSpec((tokens, model), lambda s: (0, 0))] * 2,
        out_specs=pl.BlockSpec((places // 2, high, columns), lambda s: (s, first // high, 0)),
        out_shape=jax.ShapeDtypeStruct(shape, bf16),
        compiler_params=pltpu.CompilerParams(vmem_limit_bytes=vmem_limit),
    )(*left, *right)


def total_of(pieces):
    return jnp.sum(pieces.astype(f32), axis=0)


def after(value, *others):
    return lax.optimization_barrier((value,) + others)[0]


def joined(*parts):
    return jnp.concatenate(parts, axis=0)


def gather_team(block, *stage):
    z_at = lax.axis_index("z")
    half = block.shape[0] // 2
    below, above = hop(block, "z", 1), hop(block, "z", -1)
    if stage:
        below, above = after(below, *stage), after(above, *stage)
    across = joined(hop(below[:half], "z", 1), hop(above[half:], "z", -1))
    own = jnp.zeros((4,) + block.shape, block.dtype)
    for offset, part in ((0, block), (1, above), (3, below), (2, across)):
        own = lax.dynamic_update_index_in_dim(own, part, (z_at + offset) % 4, 0)
    own = own.reshape(4 * block.shape[0], -1)
    return own, hop(own, "row", 1)


def reduce_team(other, own):
    z_at = lax.axis_index("z")
    other = hop(other, "row", 1).reshape(4, -1, other.shape[-1])
    own = own.reshape(other.shape)

    def block(offset):
        at = (z_at + offset) % 4
        parts = [lax.dynamic_index_in_dim(whole, at, 0, keepdims=False) for whole in (own, other)]
        return parts[0].astype(f32) + parts[1].astype(f32)

    sums = {offset: block(offset) for offset in (2, 1, 3, 0)}
    half = own.shape[1] // 2
    from_below = hop(sums[2][:half].astype(bf16), "z", 1)
    from_above = hop(sums[2][half:].astype(bf16), "z", -1)
    up = joined(sums[1][:half] + from_below.astype(f32), sums[1][half:]).astype(bf16)
    down = joined(sums[3][:half], sums[3][half:] + from_above.astype(f32)).astype(bf16)
    up, down = hop(up, "z", 1), hop(down, "z", -1)
    return sums[0] + up.astype(f32) + down.astype(f32), up


def project_in(left, weight):
    return jnp.dot(left, weight, preferred_element_type=f32)


def project_back(grad, weight):
    return lax.dot_general(grad, weight, (((1,), (1,)), ((), ())), preferred_element_type=f32)


def outer_sum(left, grad):
    return lax.dot_general(left, grad, (((0,), (0,)), ((), ())), preferred_element_type=f32)


def fold_down(rows, width):
    over = rows.shape[-1] - width
    group = rows.shape[-2] * over // width
    tail = [rows[..., at : at + group, width:] for at in range(0, rows.shape[-2], group)]
    return jnp.concatenate([rows[..., :width], jnp.concatenate(tail, axis=-1)], axis=-2)


def unfold_down(rows, model):
    width = rows.shape[-1]
    over = model - width
    count = rows.shape[-2] * width // model
    tail = rows[..., count:, :]
    tail = [tail[..., at : at + over] for at in range(0, width, over)]
    return jnp.concatenate([rows[..., :count, :], jnp.concatenate(tail, axis=-2)], axis=-1)


def cost(micros):
    return pl.CostEstimate(flops=0, bytes_accessed=int(micros * 3.0e6), transcendentals=0)


def kernel_call(kernel, micros, outs, scratch=()):
    return pl.pallas_call(
        kernel,
        cost_estimate=cost(micros),
        out_shape=[jax.ShapeDtypeStruct(shape, dtype) for shape, dtype in outs],
        scratch_shapes=list(scratch),
        compiler_params=pltpu.CompilerParams(vmem_limit_bytes=vmem_limit),
    )


def chunk_rows(chunk, size):
    return pl.ds(pl.multiple_of(chunk * size, size), size)


def panels(ref, rows):
    return jnp.concatenate([ref[at, rows, :] for at in range(ref.shape[0])], axis=1)


def set_panels(ref, rows, value):
    for at in range(ref.shape[0]):
        ref[at, rows, :] = value[:, at * 128 : (at + 1) * 128]


def gate_parts(raw_in, raw_rec, params):
    gate_in = jax.nn.sigmoid(raw_in + params[5:6, :])
    gate_rec = jax.nn.sigmoid(raw_rec + params[6:7, :])
    log_decay = gate_rec * params[7:8, :]
    base = jnp.exp(log_decay)
    return gate_in, gate_rec, base, -jnp.tanh(log_decay) * (base * base + 1.0)


def gates_kernel(
    cin, halo, masks, params, w_in, w_rec,
    conv, factor, state, decay, ends, ext, raw_in, raw_rec, drive,
):
    tokens, width = cin.shape
    count = halo.shape[0]
    size = tokens // count
    tiles = width // 128

    def convolve(chunk, carry):
        rows = chunk_rows(chunk, size)
        ext[0:8, :] = halo[chunk].astype(f32)
        ext[8 : 8 + size, :] = cin[rows, :].astype(f32)
        total = params[4:5, :] + params[0:1, :] * ext[8 : 8 + size, :]
        for k in (1, 2, 3):
            total = total + params[k : k + 1, :] * ext[8 - k : 8 - k + size, :] * masks[rows, k : k + 1]
        conv[rows, :] = total.astype(bf16)
        return carry

    lax.fori_loop(0, count, convolve, 0)
    raw_in[...] = jnp.dot(conv[...], w_in[...], preferred_element_type=f32)
    raw_rec[...] = jnp.dot(conv[...], w_rec[...], preferred_element_type=f32)

    def gate(chunk, carry):
        rows = chunk_rows(chunk, size)
        gate_in, _, base, kept = gate_parts(raw_in[rows, :], raw_rec[rows, :], params)
        scale = jnp.sqrt(jnp.maximum(kept, beta_floor))
        set_panels(factor, rows, base * masks[rows, 0:1])
        set_panels(drive, rows, scale * gate_in * conv[rows, :].astype(f32))
        return carry

    lax.fori_loop(0, count, gate, 0)

    def scan(slot, carry):
        at = pl.ds(slot, count, stride=size)
        after = []
        for tile, (held, gone) in enumerate(carry):
            step = factor[tile, at, :]
            held = step * held + drive[tile, at, :]
            gone = step * gone
            state[tile, at, :] = held
            decay[tile, at, :] = gone
            after.append((held, gone))
        return tuple(after)

    first = pl.ds(0, count, stride=size)
    start = []
    for tile in range(tiles):
        zero = drive[tile, first, :] * 0.0
        start.append((zero, zero + 1.0))
    last = lax.fori_loop(0, size, scan, tuple(start))
    for tile, (held, gone) in enumerate(last):
        ends[0, :, tile * 128 : (tile + 1) * 128] = gone
        ends[1, :, tile * 128 : (tile + 1) * 128] = held


def carry_kernel(backward, spot, pieces, entering):
    mine = spot[0]
    places = pieces.shape[0]
    order = range(places - 1, -1, -1) if backward else range(places)
    decay, state = pieces[order[0], 0], pieces[order[0], 1]
    here = jnp.where(mine == order[0], 1.0, 0.0)
    own_decay, own_state = jnp.zeros_like(decay) + here, jnp.zeros_like(state)
    for place_at in order[1:]:
        here = jnp.where(mine == place_at, 1.0, 0.0)
        own_decay = own_decay + decay * here
        own_state = own_state + state * here
        step = pieces[place_at, 0]
        state = step * state + pieces[place_at, 1]
        decay = step * decay
    for row in range(2):
        held = jnp.zeros((2, decay.shape[1]), f32)
        for z in range(3, -1, -1) if backward else range(4):
            start = row * 8 + z * 2
            part = slice(start, start + 2)
            inside = own_decay[part] * held + own_state[part]
            held = decay[part] * held + state[part]
            for line in range(2):
                entering[start + line] = inside[line : line + 1]


def gelu_parts(value):
    slope = 0.7978845608028654
    square = value * value
    inner = jnp.tanh(slope * (value + 0.044715 * value * square))
    half = 0.5 * (1.0 + inner)
    act = value * half
    grad = half + 0.5 * value * (1.0 - inner * inner) * slope * (1.0 + 3 * 0.044715 * square)
    return act, grad


def mix_kernel(pre, state, decay, entering, out_rows, rec_state, mixed, partial_sum):
    count = entering.shape[0]
    tokens, width = rec_state.shape
    size = tokens // count

    def mix(chunk, carry):
        rows = chunk_rows(chunk, size)
        full = panels(state, rows) + panels(decay, rows) * entering[chunk]
        rec_state[rows, :] = full
        mixed[rows, :] = (gelu_parts(pre[rows, :])[0] * full).astype(bf16)
        return carry

    lax.fori_loop(0, count, mix, 0)
    partial_sum[...] = jnp.dot(
        mixed[...], out_rows[...], preferred_element_type=f32
    ).astype(bf16)


def unmix_kernel(
    mixed_own, mixed_other, pre_own, pre_other, rec_own, rec_other, factor,
    grad_gelu, adjoint, reach, ends, grad_state,
):
    half, width = rec_own.shape
    count = ends.shape[1]
    size = 2 * half // count
    tiles = width // 128

    def unmix(start, grad_mixed, pre, rec_state, chunk, carry):
        rows = chunk_rows(chunk, size)
        out = chunk_rows(chunk + start, size)
        act, slope = gelu_parts(pre[rows, :])
        grad = grad_mixed[rows, :]
        grad_gelu[out, :] = (grad * rec_state[rows, :] * slope).astype(bf16)
        set_panels(grad_state, out, grad * act)
        return carry

    lax.fori_loop(0, count // 2, partial(unmix, 0, mixed_own, pre_own, rec_own), 0)
    lax.fori_loop(0, count // 2, partial(unmix, count // 2, mixed_other, pre_other, rec_other), 0)

    def scan(step, carry):
        at = pl.ds(size - 1 - step, count, stride=size)
        after = []
        for tile, (held, gone, ahead) in enumerate(carry):
            held = ahead * held + grad_state[tile, at, :]
            gone = ahead * gone
            adjoint[tile, at, :] = held
            reach[tile, at, :] = gone
            after.append((held, gone, factor[tile, at, :]))
        return tuple(after)

    first = pl.ds(0, count, stride=size)
    start = []
    for tile in range(tiles):
        zero = factor[tile, first, :] * 0.0
        start.append((zero, zero + 1.0, zero + 1.0))
    last = lax.fori_loop(0, size, scan, tuple(start))
    for tile, (held, gone, ahead) in enumerate(last):
        ends[0, :, tile * 128 : (tile + 1) * 128] = ahead * gone
        ends[1, :, tile * 128 : (tile + 1) * 128] = ahead * held


def ungate_kernel(
    adjoint, reach, arriving, rec_own, rec_other, entering, conv, cin, halo, masks, params, w_in,
    w_rec, grad_in, grad_rec, grad_conv, sums, ext, direct, raw_rec,
):
    tokens, width = cin.shape
    count = halo.shape[0]
    size = tokens // count
    zero = params[0:8, :] * 0.0

    def fold(value):
        total = value[0:8]
        for at in range(8, size, 8):
            total = total + value[at : at + 8]
        return total

    def ungate(start, rec_state, chunk, carry):
        sum_in, sum_rec, sum_decay = carry
        ext[8 : 8 + size, :] = rec_state[chunk_rows(chunk, size), :]
        chunk = chunk + start
        rows = chunk_rows(chunk, size)
        ext[7:8, :] = entering[chunk]
        full = panels(adjoint, rows) + panels(reach, rows) * arriving[chunk]
        gate_in, gate_rec, base, square = gate_parts(direct[rows, :], raw_rec[rows, :], params)
        scale = jnp.sqrt(jnp.maximum(square, beta_floor))
        values = conv[rows, :].astype(f32)
        scaled = full * scale
        drive = full * gate_in * values
        slope = jnp.where(square > beta_floor, (1.0 - square) / scale, 0.0)
        grad_log = full * base * masks[rows, 0:1] * ext[7 : 7 + size, :] - slope * drive
        raw_in = scale * drive * (1.0 - gate_in)
        pulled = grad_log * gate_rec
        rec = pulled * params[7:8, :] * (1.0 - gate_rec)
        grad_in[rows, :] = raw_in.astype(bf16)
        grad_rec[rows, :] = rec.astype(bf16)
        direct[rows, :] = scaled * gate_in
        return (sum_in + fold(raw_in), sum_rec + fold(rec), sum_decay + fold(pulled))

    direct[...] = jnp.dot(conv[...], w_in[...], preferred_element_type=f32)
    raw_rec[...] = jnp.dot(conv[...], w_rec[...], preferred_element_type=f32)
    half = count // 2
    totals = lax.fori_loop(0, half, partial(ungate, 0, rec_own), (zero, zero, zero))
    sum_in, sum_rec, sum_decay = lax.fori_loop(0, half, partial(ungate, half, rec_other), totals)
    back = (((1,), (1,)), ((), ()))
    direct[...] += lax.dot_general(grad_in[...], w_in[...], back, preferred_element_type=f32)
    direct[...] += lax.dot_general(grad_rec[...], w_rec[...], back, preferred_element_type=f32)

    def taps(chunk, carry):
        sum_bias, sum_taps = carry
        rows = chunk_rows(chunk, size)
        grad = direct[rows, :].astype(bf16)
        grad_conv[rows, :] = grad
        grad = grad.astype(f32)
        ext[0:8, :] = halo[chunk].astype(f32)
        ext[8 : 8 + size, :] = cin[rows, :].astype(f32)
        new_taps = [sum_taps[0] + fold(grad * ext[8 : 8 + size, :])]
        for k in (1, 2, 3):
            moved = ext[8 - k : 8 - k + size, :] * masks[rows, k : k + 1]
            new_taps.append(sum_taps[k] + fold(grad * moved))
        return (sum_bias + fold(grad), tuple(new_taps))

    sum_bias, sum_taps = lax.fori_loop(0, count, taps, (zero, (zero,) * 4))
    rows_out = sum_taps + (sum_bias, sum_in, sum_rec, sum_decay * params[8:9, :])
    for index, total in enumerate(rows_out):
        sums[index : index + 1, :] = jnp.sum(total, axis=0, keepdims=True)


def unconvolve_kernel(grad_conv, halo, masks, params, out, ext):
    tokens, width = grad_conv.shape
    count = halo.shape[0]
    size = tokens // count

    def spread(chunk, carry):
        rows = chunk_rows(chunk, size)
        ext[0:size, :] = grad_conv[rows, :].astype(f32)
        ext[size : size + 8, :] = halo[chunk].astype(f32)
        total = params[0:1, :] * ext[0:size, :]
        for k in (1, 2, 3):
            total = total + params[k : k + 1, :] * ext[k : k + size, :] * masks[rows, 3 + k : 4 + k]
        out[rows, :] = total.astype(bf16)
        return carry

    lax.fori_loop(0, count, spread, 0)


def body(
    tokens,
    lengths,
    norm_one,
    gelu_weight,
    input_weight,
    conv_weight,
    conv_bias,
    gate_input,
    bias_input,
    gate_recur,
    bias_recur,
    decay_param,
    out_weight,
    norm_two,
    gate_weight,
    up_weight,
    down_weight,
    cotangent,
):
    row_count, size, model = tokens.shape
    local = row_count * size
    block, hidden = gelu_weight.shape
    inner = gate_weight.shape[1]
    head = gate_input.shape[1]
    channels, units = hidden // 8, inner // 8
    strip = gate_input.shape[0]
    width = -(-channels // 128) * 128
    spare = width - channels
    row_at, z_at, y_at, x_at = (lax.axis_index(name) for name in everywhere)
    plane_at = y_at * 4 + x_at
    chunks = 16
    total_tokens = chunks * size
    flat = tokens.reshape(local, model)

    row_total = jnp.sum(lengths, axis=1)
    own_slots = (z_at * 16 + plane_at) * size + jnp.arange(size)
    valid = (own_slots[None, :] < row_total[:, None]).astype(f32).reshape(local, 1)
    upstream = cotangent.reshape(local, model).astype(f32) * valid

    def halves(whole):
        whole = whole.reshape(2, 4 * local, -1)
        return [
            lax.dynamic_index_in_dim(whole, row_at ^ other, 0, keepdims=False) for other in (0, 1)
        ]

    tokens_own, tokens_other = halves(lax.all_gather(flat, team, axis=0, tiled=True))

    gains = jnp.stack([norm_one, norm_two], axis=1)
    gains = jnp.broadcast_to(
        jnp.pad(gains, ((0, 0), (0, spare - 2)))[:, None, :], (block, 8, spare)
    )
    third = jnp.concatenate(
        [
            gelu_weight.reshape(block, 8, channels),
            jnp.zeros_like(gains),
            gate_weight.reshape(block, 8, units),
            up_weight.reshape(block, 8, units),
        ],
        axis=2,
    ).transpose(1, 0, 2)
    lead = jnp.concatenate([input_weight.reshape(block, 8, channels), gains], axis=2)
    lead = lead.transpose(1, 0, 2)[:, None]
    lead = jnp.broadcast_to(lead, (8, 16, block, width)).reshape(model, width)
    input_full = lax.all_to_all(lead, everywhere, 0, 0, tiled=True)
    third = lax.all_to_all(after(third, input_full), team, 0, 0, tiled=True).reshape(8 * block, -1)
    first, third = third[:, :width], third[:, width:]
    small = jnp.stack([conv_bias, bias_input, bias_recur, decay_param], axis=1)
    rest = jnp.concatenate([gate_input, gate_recur, conv_weight, small], axis=1)
    rest = jnp.pad(rest, ((0, 32 - strip), (0, width - rest.shape[1])))
    rest = gather_plane(after(rest, first))

    def in_order(rows, count):
        rows = rows.reshape(16, count, block, rows.shape[-1])
        return rows.transpose(1, 0, 2, 3).reshape(count * 16 * block, rows.shape[-1])

    cuts = -(-model // width)
    out_pack = jnp.pad(out_weight, ((0, 32 - strip), (0, cuts * width - model)))
    out_pack = out_pack.reshape(32, cuts, width).transpose(1, 0, 2).reshape(cuts * 32, width)
    second = jnp.concatenate([first, out_pack], axis=0)
    second = lax.all_gather(second, plane, axis=0, tiled=False)
    gelu_full = in_order(second[:, : 8 * block], 8)
    out_rows = second[:, 8 * block :].reshape(16, cuts, 32, width)[:, :, :strip]
    out_rows = out_rows.transpose(0, 2, 1, 3).reshape(channels, cuts * width)[:, :model]
    out_rows = jnp.pad(out_rows, ((0, spare), (0, 0)))

    third = jnp.concatenate([third, fold_down(down_weight, 2 * units)], axis=0)
    third = lax.all_gather(third, plane, axis=0, tiled=False)
    down = unfold_down(third[:, 8 * block :], model).reshape(units, model)
    third = in_order(third[:, : 8 * block], 8)

    gain_one = input_full[:, channels].astype(f32)[None, :]
    gain_two = input_full[:, channels + 1].astype(f32)[None, :]
    def rms_unit(values):
        return lax.rsqrt(jnp.mean(values * values, axis=-1, keepdims=True) + epsilon)

    def norm_half(values):
        values = values.astype(f32)
        return (values * rms_unit(values) * gain_one).astype(bf16)

    own_head = (jnp.arange(width)[:, None] // head) == (jnp.arange(width)[None, :] // head)

    def spread_heads(part):
        return jnp.where(own_head, jnp.concatenate([part, part, part], axis=1)[:, :width], 0)

    own_tokens = flat.astype(f32)
    normed_own, normed_other = norm_half(tokens_own), norm_half(tokens_other)
    conv_in = joined(
        project_in(normed_own, input_full).astype(bf16),
        project_in(normed_other, input_full).astype(bf16),
    )
    by_chunk = (chunks, size, width)
    halo = hop(conv_in.reshape(by_chunk)[:, size - 8 :], plane, 1)
    rest = after(rest, halo)[:, :strip].reshape(channels, width)
    rest = jnp.pad(rest, ((0, spare), (0, 0)))
    w_in = spread_heads(rest[:, :head])
    w_rec = spread_heads(rest[:, head : 2 * head])
    rows_small = rest[:, 2 * head : 2 * head + 8].astype(f32).T
    decay_row = rows_small[7:8]
    params = jnp.concatenate(
        [
            rows_small[:7],
            -8.0 * jax.nn.softplus(decay_row),
            -8.0 * jax.nn.sigmoid(decay_row),
            jnp.zeros((7, width), f32),
        ],
        axis=0,
    )

    lens = jnp.stack([lengths, hop(lengths, "row", 1)], axis=0)
    starts = jnp.cumsum(lens, axis=2) - lens
    first_slot = jnp.arange(4) * (16 * size) + plane_at * size

    def position(slot):
        live = (lens > 0)[:, None, :, None, :] & (starts[:, None, :, None, :] <= slot[..., None])
        origin = jnp.max(jnp.where(live, starts[:, None, :, None, :], 0), axis=-1)
        return slot - origin

    slots = first_slot[None, :, None, None] + jnp.arange(size)[None, None, None, :]
    slots = jnp.broadcast_to(slots, (2, 4, row_count, size))
    here = position(slots)
    columns = [here != 0] + [here >= k for k in (1, 2, 3)]
    for k in (1, 2, 3):
        ahead = slots + k
        columns.append((position(ahead) >= k) & (ahead < 64 * size))
    columns.append(jnp.zeros_like(columns[0]))
    masks = jnp.stack(columns, axis=-1).astype(f32).reshape(total_tokens, 8)

    def turned(rim, shift):
        by_z = rim.reshape((2, 4, row_count) + rim.shape[1:])
        return jnp.roll(by_z, shift, axis=1).reshape(rim.shape)

    halo = jnp.where(plane_at == 0, turned(halo, 1), halo)
    wide = ((total_tokens, width), f32)
    narrow = ((total_tokens, width), bf16)
    paneled = ((width // 128, total_tokens, 128), f32)
    ends_shape = ((2, chunks, width), f32)
    extended = pltpu.VMEM((size + 8, width), f32)
    whole = pltpu.VMEM(*wide)
    folded = pltpu.VMEM(*paneled)
    conv_vals, factor, local_state, decay, ends = kernel_call(
        gates_kernel,
        60,
        [narrow, paneled, paneled, paneled, ends_shape],
        [extended, whole, whole, folded],
    )(conv_in, halo, masks, params, w_in, w_rec)


    def carried(pieces, backward):
        spot = plane_at.astype(jnp.int32).reshape(1)
        return pl.pallas_call(
            partial(carry_kernel, backward),
            cost_estimate=cost(1),
            out_shape=jax.ShapeDtypeStruct((chunks, 1, width), f32),
            in_specs=[pl.BlockSpec(memory_space=pltpu.SMEM), pl.BlockSpec(memory_space=pltpu.VMEM)],
            out_specs=pl.BlockSpec(memory_space=pltpu.VMEM),
        )(spot, pieces)

    pieces = gather_plane(ends)
    down_own, down_other = gather_team(after(upstream.astype(bf16), conv_in), pieces)
    entering = after(carried(pieces, False), down_own)
    gelu_own, gelu_other = project_in(normed_own, gelu_full), project_in(normed_other, gelu_full)
    half = total_tokens // 2

    def mix(which, gelu_pre):
        rows = pl.BlockSpec((half, width), lambda i: (0, 0))
        folds = pl.BlockSpec((width // 128, half, 128), lambda i: (0, which, 0))
        return pl.pallas_call(
            mix_kernel,
            cost_estimate=cost(5),
            out_shape=[
                jax.ShapeDtypeStruct((half, width), f32),
                jax.ShapeDtypeStruct((half, width), bf16),
                jax.ShapeDtypeStruct((half, model), bf16),
            ],
            grid=(1,),
            in_specs=[
                rows,
                folds,
                folds,
                pl.BlockSpec((chunks // 2, 1, width), lambda i: (which, 0, 0)),
                pl.BlockSpec((width, model), lambda i: (0, 0)),
            ],
            out_specs=[
                pl.BlockSpec((half, width), lambda i: (0, 0)),
                pl.BlockSpec((half, width), lambda i: (0, 0)),
                pl.BlockSpec((half, model), lambda i: (0, 0)),
            ],
            compiler_params=pltpu.CompilerParams(vmem_limit_bytes=vmem_limit),
        )(gelu_pre, local_state, decay, entering, out_rows)

    other_state, other_mixed, other_middle = mix(1, gelu_other)
    own_state, own_mixed, own_middle = mix(0, gelu_own)
    middle = own_tokens + reduce_team(other_middle, own_middle)[0]

    scale_two = rms_unit(middle)
    normed_two = (middle * scale_two * gain_two).astype(bf16)
    two_own, two_other = gather_team(normed_two)

    def feed(values, grad_inner):
        pre = project_in(values, third)
        act, slope = gelu_parts(pre[:, :units])
        up = pre[:, units:]
        grad = [(grad_inner * up * slope).astype(bf16), (grad_inner * act).astype(bf16)]
        return (act * up).astype(bf16), jnp.concatenate(grad, axis=1)

    inner_own, pre_own = feed(two_own, project_back(down_own, down))
    inner_other, pre_other = feed(two_other, project_back(down_other, down))
    terms_other = project_back(pre_other, third).astype(bf16)
    terms_own = project_back(pre_own, third).astype(bf16)
    grad_two, _ = reduce_team(terms_other, terms_own)
    def back_to_rows(grad):
        grad = grad.astype(bf16).reshape(8, block, -1)
        return lax.all_to_all(grad, team, 0, 0, tiled=True).astype(f32).transpose(1, 0, 2)

    def norm_back(values, scale, gain, grad):
        pulled = gain * grad
        mean = jnp.mean(pulled * values, axis=-1, keepdims=True)
        return scale * pulled - values * (scale * scale * scale * mean)

    def gain_grad(gain, pairs):
        total = sum(jnp.sum(weight.astype(f32) * grad, axis=1) for weight, grad in pairs)
        return total / gain.astype(f32)

    grad_middle = upstream + norm_back(middle, scale_two, gain_two, grad_two)
    fold = 8 * block
    tail = fold + units * model // (32 * units)
    share = tail + 48
    packed_down = outer_folded(
        (inner_own, inner_other), (down_own, down_other), (16, share, 2 * units), fold
    )
    grad_third = add_outer(packed_down, (two_own, two_other), (pre_own, pre_other))
    branch_own, branch_other = gather_team(
        after(grad_middle.astype(bf16), packed_down), grad_third
    )
    grad_third = add_strips(
        grad_third, (own_mixed, other_mixed), (branch_own, branch_other), strip, tail
    )
    grad_third = lax.psum_scatter(
        grad_third.reshape(16 * share, 2 * units), plane, scatter_dimension=0, tiled=True
    )
    grad_gelu, adjoint, reach, ends = kernel_call(
        unmix_kernel, 100, [narrow, paneled, paneled, ends_shape], [folded]
    )(
        project_back(branch_own, out_rows), project_back(branch_other, out_rows),
        gelu_own, gelu_other, own_state, other_state, factor,
    )
    normed = (normed_own, norm_half(after(tokens_other, ends)))
    grad_gelu_rows = jnp.zeros((16, 8 * block, width), bf16)
    grad_gelu_rows = add_outer(grad_gelu_rows, normed, (grad_gelu,))
    result_own = project_in(after(inner_own, ends), down).astype(bf16)
    result_other = project_in(after(inner_other, ends), down).astype(bf16)
    arriving = after(
        carried(gather_plane(ends), True), grad_gelu_rows, result_own, result_other
    )
    grad_gelu_rows = lax.all_to_all(after(grad_gelu_rows, arriving), plane, 0, 0, tiled=True)
    grad_in, grad_rec, grad_conv, sums = kernel_call(
        ungate_kernel, 100, [narrow, narrow, narrow, ((8, width), f32)], [extended, whole, whole]
    )(
        adjoint, reach, arriving, own_state, other_state, entering, conv_vals, conv_in, halo, masks,
        params, w_in, w_rec,
    )
    ahead = hop(grad_conv.reshape(by_chunk)[:, :8], plane, -1)
    ahead = after(ahead, grad_gelu_rows)
    ahead = jnp.where(plane_at == 15, turned(ahead, -1), ahead)
    (grad_conv_in,) = kernel_call(unconvolve_kernel, 1, [narrow], [extended])(
        grad_conv, ahead, masks, params
    )

    def own_heads(grad):
        grad = jnp.where(own_head, grad, 0)[:channels]
        return grad[:, :head] + grad[:, head:channels]

    grad_rest = jnp.concatenate(
        [
            own_heads(outer_sum(after(conv_vals, ahead), grad_in)),
            own_heads(outer_sum(after(conv_vals, ahead), grad_rec)),
            sums.T[:channels],
        ],
        axis=1,
    ).astype(bf16)
    grad_rest = grad_rest.reshape(16, strip, -1)
    grad_rest = jnp.pad(
        grad_rest, ((0, 0), (0, 32 - strip), (0, width - grad_rest.shape[2]))
    )
    grad_lead = jnp.pad(grad_rest, ((0, 0), (8 * block, 0), (0, 0)))
    grad_pair = jnp.concatenate([grad_conv_in, grad_gelu], axis=1)
    pair_weight = jnp.concatenate([input_full, gelu_full], axis=1)
    terms_other = project_back(grad_pair[half:], pair_weight).astype(bf16)
    terms_own = project_back(grad_pair[:half], pair_weight).astype(bf16)
    grad_normed, upward = reduce_team(
        jnp.concatenate([terms_other, result_other], axis=1),
        jnp.concatenate([terms_own, result_own], axis=1),
    )
    result = (middle + grad_normed[:, model:]) * valid
    output = result.reshape(row_count, size, model).astype(bf16)
    grad_normed = grad_normed[:, :model]
    grad_lead = add_outer(grad_lead, normed, (grad_conv_in,))
    grad_lead = lax.all_to_all(grad_lead, plane, 0, 0, tiled=True)
    cut = 8 * block
    grad_lead = total_of(after(grad_lead, upward))
    grad_rest = grad_lead[cut : cut + strip]
    grad_gelu_rows = total_of(after(grad_gelu_rows, upward)).astype(bf16)
    grad_gate_input = grad_rest[:, :head]
    grad_gate_recur = grad_rest[:, head : 2 * head]
    grad_small = grad_rest[:, 2 * head : 2 * head + 8]
    grad_third = after(grad_third, upward)
    grad_down_weight = unfold_down(grad_third[fold:tail], model).astype(f32)
    last = grad_third[tail + 32 :, : model // 2]
    last = joined(last[:, : model // 4], last[:, model // 4 :])
    grad_out_weight = jnp.concatenate(
        [grad_third[tail : tail + strip], last[:strip]], axis=1
    ).astype(f32)
    team_third = jnp.concatenate(
        [grad_third[:cut], grad_lead[:cut].astype(bf16), grad_gelu_rows], axis=1
    )
    team_third = back_to_rows(team_third)
    grad_input_weight = team_third[:, :, 2 * units : 2 * units + channels].reshape(block, hidden)
    grad_gelu_weight = team_third[:, :, 2 * units + width :][:, :, :channels].reshape(block, hidden)
    grad_gate_weight = team_third[:, :, :units].reshape(block, inner)
    grad_up_weight = team_third[:, :, units : 2 * units].reshape(block, inner)

    grad_norm_two = gain_grad(
        norm_two, [(gate_weight, grad_gate_weight), (up_weight, grad_up_weight)]
    )
    grad_norm_one = gain_grad(
        norm_one, [(gelu_weight, grad_gelu_weight), (input_weight, grad_input_weight)]
    )
    own_scale = rms_unit(own_tokens)
    grad_tokens = grad_middle + norm_back(own_tokens, own_scale, gain_one, grad_normed)
    return (
        output,
        grad_tokens.reshape(row_count, size, model),
        grad_norm_one,
        grad_gelu_weight,
        grad_input_weight,
        grad_small[:, :4],
        grad_small[:, 4],
        grad_gate_input,
        grad_small[:, 5],
        grad_gate_recur,
        grad_small[:, 6],
        grad_small[:, 7],
        grad_out_weight,
        grad_norm_two,
        grad_gate_weight,
        grad_up_weight,
        grad_down_weight,
    )


def solution(mesh):
    grid = Mesh(mesh.devices.reshape(2, 4, 4, 4), everywhere)
    slots = P("row", ("z", "y", "x"), None)
    line = P(everywhere)
    sheet = P(everywhere, None)
    return jax.shard_map(
        body,
        mesh=grid,
        in_specs=(
            slots, P("row", None), line, sheet, sheet, sheet, line, sheet, line, sheet, line, line,
            sheet, line, sheet, sheet, sheet, slots,
        ),
        out_specs=(
            slots, slots, line, sheet, sheet, sheet, line, sheet, line, sheet, line, line, sheet,
            line, sheet, sheet, sheet,
        ),
        check_vma=False,
    )
```
